32 devices in a mesh: dp: 8 (over z, x), section: 2 (over core), tensor: 2 (over y).
Axes of the slice: x: 2, y: 2, z: 4, core: 2. Of those that a mesh axis runs over, the one named last changes fastest.
Arguments:
- patches: bfloat16 [16, 1024, 384], P(('dp', 'section'), 'tensor'), may hold values from -6 to 6
- image_ids: int32 [16, 1024], P('dp'), may hold values from 0 to 7, never falling along the last dimension, each value on 1 to 256 neighbouring positions
- cotangent: bfloat16 [16, 1024, 384], P(('dp', 'section'), 'tensor'), may hold values from -6 to 6
- norm_gains: float32 [2, 2, 384], P('section'), may hold values from 0.5 to 1.5
- qkv_weight: bfloat16 [2, 384, 3, 384], P('section', None, None, 'tensor'), may hold values from -0.4375 to 0.4375
- out_weight: bfloat16 [2, 384, 384], P('section', 'tensor'), may hold values from -1.25 to 1.25
- mlp_in: bfloat16 [384, 1536], P(None, 'tensor'), may hold values from -0.3125 to 0.3125
- mlp_out: bfloat16 [1536, 384], P('tensor'), may hold values from -0.15625 to 0.15625
- router: bfloat16 [384, 2], P(None, 'tensor'), may hold values from -0.21875 to 0.21875
- expert_in: bfloat16 [2, 384, 1536], P('tensor'), may hold values from -2 to 2
- expert_out: bfloat16 [2, 1536, 384], P('tensor'), may hold values from -0.15625 to 0.15625
Outputs:
- activations: bfloat16 [16, 1024, 384], P(('dp', 'section'), 'tensor')
- patch_grad: bfloat16 [16, 1024, 384], P(('dp', 'section'), 'tensor')
- gains_grad: float32 [2, 2, 384], P('section')
- qkv_grad: float32 [2, 384, 3, 384], P('section', None, None, 'tensor')
- out_grad: float32 [2, 384, 384], P('section', 'tensor')
- mlp_in_grad: float32 [384, 1536], P(None, 'tensor')
- mlp_out_grad: float32 [1536, 384], P('tensor')
- router_grad: float32 [384, 2], P(None, 'tensor')
- expert_in_grad: float32 [2, 384, 1536], P('tensor')
- expert_out_grad: float32 [2, 1536, 384], P('tensor')
The draws below stay inside these ranges and needn't reach their ends.
Inputs may be any that keep to these rules, and one draw needn't show every extreme that they name: `image_ids`: in each row the ids never fall; all 8 images are present, each with 1 to 256 patches, and one has exactly 256.
All inputs are finite; a program needn't handle non-finite values.
Results may differ from the reference program's by a relative error of at most 0.028.
The reference program's roundings to bfloat16 on the way count: a program that leaves them out, or rounds other values in their place, can miss the bound.
Values may be sent and summed in bfloat16 or wider, within the bound.
A program may use at most 128 MiB of HBM per device.

```python
import math
import jax
import jax.numpy as jnp
import numpy as np
from jax import lax

D = 384
HEADS = 6
HD = 64
FF = 1536
EXPERTS = 2
SEQ = 1024
IMAGES = 8
MOST = 256
ROWS = 16
N_SECTION = 2


def level_of(key, shape, split, least, high):
    def one(axis_at, parts):
        draws = jax.random.uniform(jax.random.fold_in(jax.random.fold_in(key, 6), axis_at), (parts,), jnp.float32, least / len(split), high / len(split))
        return jnp.repeat(jnp.exp(draws), shape[axis_at] // parts).reshape((-1,) + (1,) * (len(shape) - axis_at - 1))

    level = one(*split[0])
    for cut in split[1:]:
        level = level * one(*cut)
    return level


def length_profile(number_of, total, bound, slope):
    weights = [(1 << 20) // math.isqrt(standing ** slope) + 1 for standing in range(2, number_of + 1)]
    spare, holding = total - bound - (number_of - 1), [1] * (number_of - 1)
    while spare > 0:
        free = [i for i in range(number_of - 1) if holding[i] < bound]
        mass, left = sum([weights[i] for i in free]), spare
        for i in free:
            addition = min(bound - holding[i], max(1, left * weights[i] // mass), spare)
            holding[i] = holding[i] + addition
            spare = spare - addition
    return np.array([bound] + holding)


def uneven(own_key, count, total, limit, slope):
    if count == 2:
        one = jax.random.randint(own_key, (), max(1, total - limit), min(limit, total - 1) + 1)
        return jnp.stack([one, total - one])
    tallies = jnp.asarray(length_profile(count, total, limit, slope), jnp.int32)
    twos = (count - 1) // 2
    source_of, taker = tallies[1:1 + 2 * twos:2], tallies[2:2 + 2 * twos:2]
    margin = jnp.minimum(source_of - 1, limit - taker)
    shifted = jax.random.randint(jax.random.fold_in(own_key, 1), (twos,), 0, 1 << 20) % (margin + 1)
    tallies = tallies.at[1:1 + 2 * twos:2].set(source_of - shifted).at[2:2 + 2 * twos:2].set(taker + shifted)
    return tallies[jax.random.permutation(jax.random.fold_in(own_key, 2), count)]


def bell_draw(rng, dims, width, limit, cuts=(), kind=jnp.bfloat16):
    loudness = level_of(rng, dims, cuts, -0.22, 0.18) if cuts else 1.0
    result = jax.random.normal(rng, dims, jnp.float32) * width * loudness
    return jnp.minimum(jnp.maximum(result, -limit), limit).astype(kind)


def setup_inputs(seed: int = 0) -> dict:
    streams_of = jax.random.split(jax.random.key(seed), 12)
    return {
        "patches": bell_draw(streams_of[0], (ROWS, SEQ, D), 1.0, 6.0, ((0, 16), (1, 2))),
        "image_ids": jax.vmap(lambda own: jnp.searchsorted(jnp.cumsum(uneven(own, IMAGES, SEQ, MOST, 0)), jnp.arange(SEQ), side="right"))(jax.random.split(streams_of[1], ROWS)).reshape((ROWS, SEQ)).astype(jnp.int32),
        "cotangent": bell_draw(streams_of[2], (ROWS, SEQ, D), 1.0, 6.0, ((0, 16), (1, 2))),
        "norm_gains": jnp.clip(1.0 + 0.1 * jax.random.normal(streams_of[3], (N_SECTION, 2, D), jnp.float32), 0.5, 1.5),
        "qkv_weight": bell_draw(streams_of[4], (N_SECTION, D, 3, HEADS * HD), (D // 2) ** -0.5, 0.4375, ((0, 2), (3, 2))),
        "out_weight": bell_draw(streams_of[5], (N_SECTION, HEADS * HD, D), (HEADS * HD // 16) ** -0.5, 1.25, ((0, 2), (1, 2))),
        "mlp_in": bell_draw(streams_of[6], (D, FF), D ** -0.5, 0.3125, ((1, 2),)),
        "mlp_out": bell_draw(streams_of[7], (FF, D), FF ** -0.5, 0.15625, ((0, 2),)),
        "router": bell_draw(streams_of[8], (D, EXPERTS), (2 * D) ** -0.5, 0.21875, ((1, 2),)),
        "expert_in": bell_draw(streams_of[9], (EXPERTS, D, FF), (D // 48) ** -0.5, 2.0, ((0, 2),)),
        "expert_out": bell_draw(streams_of[10], (EXPERTS, FF, D), FF ** -0.5, 0.15625, ((0, 2),)),
    }


@jax.custom_vjp
def low(v):
    return lax.optimization_barrier(v.astype(jnp.bfloat16)).astype(jnp.float32)

@jax.custom_vjp
def low_back(v):
    return v

def low_keep(v):
    return (low(v), None)

def low_pass(kept, grad):
    return (grad,)

def back_keep(v):
    return (v, None)

def back_low(kept, grad):
    return (low(grad),)
low.defvjp(low_keep, low_pass)
low_back.defvjp(back_keep, back_low)
epsilon = 1e-06
highest = lax.Precision.HIGHEST

def layer_norm(values, gain_row):
    average = lax.optimization_barrier(jnp.mean(values, axis=-1, keepdims=True))
    centred = values - average
    spread = lax.optimization_barrier(jnp.mean(centred * centred, axis=-1, keepdims=True))
    return centred * lax.rsqrt(spread + epsilon) * gain_row

def smooth_gate(values):
    return jax.nn.gelu(values, approximate=False)

def attention(values, gain_row, w_qkv, w_attn_out, same_image):
    seq_len = values.shape[0]
    head_count = w_qkv.shape[2] // HD
    normed = low(layer_norm(values, gain_row))
    projected = low(low_back(jnp.einsum('td,dcf->ctf', normed, w_qkv, precision=highest)))
    queries = projected[0].reshape(seq_len, head_count, HD)
    key_rows = projected[1].reshape(seq_len, head_count, HD)
    value_rows = projected[2].reshape(seq_len, head_count, HD)
    scores = low_back(jnp.einsum('qhd,khd->hqk', queries, key_rows, precision=highest) * HD ** (-0.5))
    scores = jnp.where(same_image[None], scores, -1e+30)
    maxima = lax.optimization_barrier(jnp.max(scores, axis=-1, keepdims=True))
    exp_scores = jnp.exp(scores - maxima)
    attn_probs = exp_scores / lax.optimization_barrier(jnp.sum(exp_scores, axis=-1, keepdims=True))
    mixed_rows = jnp.einsum('hqk,khd->qhd', low(attn_probs), value_rows, precision=highest)
    mixed_rows = low_back(low(mixed_rows.reshape(seq_len, head_count * HD)))
    return values + low_back(jnp.dot(mixed_rows, w_attn_out, precision=highest))

def feed_forward(values, gain_row, w_in, w_out):
    normed = low(layer_norm(values, gain_row))
    hidden = low(smooth_gate(low_back(jnp.dot(normed, w_in, precision=highest))))
    return values + low_back(jnp.dot(hidden, w_out, precision=highest))

def soft_experts(values, gain_row, router_cols, w_in, w_out, member):
    normed = low(layer_norm(values, gain_row))
    logits = low_back(jnp.dot(normed, router_cols, precision=highest))
    exp_logits = jnp.exp(logits)
    totals = jnp.dot(member.T, exp_logits, precision=highest)
    dispatch = low(exp_logits / jnp.dot(member, totals, precision=highest))
    slot_rows = jnp.einsum('tg,te,td->egd', member, dispatch, normed, precision=highest)
    slot_rows = low_back(low(slot_rows))
    pre_act = low_back(jnp.einsum('egd,edf->egf', slot_rows, w_in, precision=highest))
    hidden = low(smooth_gate(pre_act))
    outputs = low_back(low(jnp.einsum('egf,efd->egd', hidden, w_out, precision=highest)))
    combine = low(exp_logits / lax.optimization_barrier(jnp.sum(exp_logits, axis=-1, keepdims=True)))
    per_token = jnp.einsum('tg,egd->ted', member, outputs, precision=highest)
    return values + low_back(jnp.einsum('te,ted->td', combine, per_token, precision=highest))

def forward_row(params, values, ids_row):
    gain_all, w_qkv, w_attn_out, w_mlp_in, w_mlp_out, router_cols, w_exp_in, w_exp_out = params
    same_image = ids_row[:, None] == ids_row[None, :]
    member = (ids_row[:, None] == jnp.arange(IMAGES, dtype=jnp.int32)[None, :]).astype(jnp.float32)
    values = attention(values, gain_all[0, 0], w_qkv[0], w_attn_out[0], same_image)
    values = feed_forward(values, gain_all[0, 1], w_mlp_in, w_mlp_out)
    values = low_back(low(values))
    values = attention(values, gain_all[1, 0], w_qkv[1], w_attn_out[1], same_image)
    return soft_experts(values, gain_all[1, 1], router_cols, w_exp_in, w_exp_out, member)

def reference(patches, image_ids, cotangent, norm_gains, qkv_weight, out_weight, mlp_in, mlp_out, router, expert_in, expert_out):
    params = (norm_gains.astype(jnp.float32), qkv_weight.astype(jnp.float32), out_weight.astype(jnp.float32), mlp_in.astype(jnp.float32), mlp_out.astype(jnp.float32), router.astype(jnp.float32), expert_in.astype(jnp.float32), expert_out.astype(jnp.float32))
    inputs = patches.astype(jnp.float32)
    checked = jax.checkpoint(forward_row)

    def run_rows(param_set, input_rows):

        def one_row(carry_now, item_now):
            return (carry_now, checked(param_set, item_now[0], item_now[1]))
        return lax.scan(one_row, jnp.float32(0.0), (input_rows, image_ids))[1]
    outputs, pullback = jax.vjp(run_rows, params, inputs)
    param_grads, input_grad = pullback(cotangent.astype(jnp.float32))
    return (outputs.astype(jnp.bfloat16), input_grad.astype(jnp.bfloat16), param_grads[0], param_grads[1], param_grads[2], param_grads[3], param_grads[4], param_grads[5], param_grads[6], param_grads[7])
```

```python
import functools

import jax
import jax.numpy as jnp
from jax import lax
from jax.experimental import pallas as pl
from jax.experimental.pallas import tpu as pltpu
from jax.sharding import PartitionSpec as P

HD = 64
IMAGES = 8
MOST = 256
LANES = 128
SLOTS = 16
EPSILON = 1e-06
BF = jnp.bfloat16
F32 = jnp.float32


def dot(a, b):
    return jnp.dot(a, b, preferred_element_type=F32)


def dot_t(a, b):
    return lax.dot_general(a, b, (((1,), (1,)), ((), ())), preferred_element_type=F32)


def t_dot(a, b):
    return lax.dot_general(a, b, (((0,), (0,)), ((), ())), preferred_element_type=F32)


def normalise(x):
    centred = x - jnp.mean(x, axis=-1, keepdims=True)
    scale = lax.rsqrt(jnp.mean(centred * centred, axis=-1, keepdims=True) + EPSILON)
    return centred * scale, scale


def norm_back(x, gain, gz):
    unit, scale = normalise(x)
    scaled = gz * gain
    mean_plain = jnp.mean(scaled, axis=-1, keepdims=True)
    mean_unit = jnp.mean(scaled * unit, axis=-1, keepdims=True)
    return scale * (scaled - mean_plain - unit * mean_unit), jnp.sum(gz * unit, axis=0, keepdims=True)


def gelu_parts(u):
    cdf = 0.5 * (1.0 + lax.erf(u * 0.7071067811865476))
    return u * cdf, cdf + u * (0.3989422804014327 * jnp.exp(-0.5 * u * u))


def pair_up(tile):
    row = lax.broadcasted_iota(jnp.int32, tile.shape, 0)
    zero = jnp.zeros_like(tile)
    return jnp.concatenate([jnp.where(row < HD, tile, zero), jnp.where(row >= HD, tile, zero)], axis=1)


def pair_down(both):
    n = both.shape[1] // 2
    row = lax.broadcasted_iota(jnp.int32, (both.shape[0], n), 0)
    return jnp.where(row < HD, both[:, :n], both[:, n:])


def bands(window):
    reach = MOST // LANES
    found, at = [], 0
    for i in range(window // LANES):
        first = max(0, i - reach) * LANES
        count = min(window, (i + reach + 1) * LANES) - first
        found.append((i * LANES, first, count, at))
        at += count
    return found, at


def compute_kernel(
    xw, cw, ids, gains, wqkv, wo, mi, mo, routert, ei, eo,
    act, pg, grad_attn, grad_mi, grad_mot, packs, small,
    z, x1, sent, x3, qt, kt, vt, kr, vr, ot, pt, tok, hidden, slope, gx, low, got, gt, gtok, gk_sum, gv_sum,
    bias, own, mixing, eslope, eout,
):
    window, width = xw.shape
    half = window // 2
    pairs = width // LANES
    total = ids.shape[1]
    tensor = lax.axis_index("tensor")
    section = lax.axis_index("section")
    blocks, _ = bands(window)
    row_blocks = window // LANES

    def rows(i, n=LANES):
        return pl.ds(pl.multiple_of(i * n, n), n)

    def loop(n, body):
        def step(i, carry):
            body(i)
            return carry

        lax.fori_loop(0, n, step, 0)

    ids_row = ids[pl.ds(section, 1), :].astype(F32)
    image = lax.broadcasted_iota(jnp.int32, (SLOTS, total), 0).astype(F32)
    spread = jnp.broadcast_to(ids_row, (SLOTS, total))
    middle = jnp.sum((spread < image).astype(F32) + (spread <= image).astype(F32), axis=1, keepdims=True)
    first_half = (middle < total).astype(F32)
    mine = jnp.where(tensor == 0, first_half, 1.0 - first_half)
    start = pl.multiple_of(tensor * (total - window), LANES)
    window_ids = ids[pl.ds(section, 1), pl.ds(start, window)].astype(F32)
    member = (jnp.broadcast_to(window_ids, (SLOTS, window)) == image[:, :window]).astype(F32)
    own_row = jnp.sum(member * mine, axis=0, keepdims=True)
    own[...] = jnp.broadcast_to(own_row, (LANES, window)).T
    ids_col = jnp.broadcast_to(window_ids, (LANES, window)).T
    for q0, k0, count, at in blocks:
        same = ids_col[k0 : k0 + count] == jnp.broadcast_to(window_ids[:, q0 : q0 + LANES], (count, LANES))
        bias[at : at + count, :] = jnp.where(same, 0.0, -1e30)

    def attention(b, x_of, out_ref):
        def norm(i):
            unit, _ = normalise(x_of(rows(i)))
            z[2 * b, rows(i)] = (unit * gains[2 * b : 2 * b + 1, :]).astype(BF)

        loop(row_blocks, norm)
        zz = z[2 * b]
        for c, dest in enumerate((qt, kt, vt)):
            tall = dot_t(wqkv[b, c * width : (c + 1) * width], zz)
            tall = (tall.astype(BF) * jnp.asarray(HD**-0.5 if c == 0 else 1.0, BF)).reshape(pairs, LANES, window)
            dest[b] = tall
        for c, dest in ((1, kr), (2, vr)):
            flat = dot_t(zz, wqkv[b, c * width : (c + 1) * width]).astype(BF)
            for j in range(pairs):
                dest[b, j] = flat[:, j * LANES : (j + 1) * LANES]

        def pair(j):
            for q0, k0, count, at in blocks:
                scores = dot(kr[b, j, k0 : k0 + count, :], pair_up(qt[b, j, :, q0 : q0 + LANES]))
                veil = bias[at : at + count, :]
                scores = scores + jnp.concatenate([veil, veil], axis=1)
                powers = jnp.exp(scores - jnp.max(scores, axis=0, keepdims=True))
                probs = (powers * (1.0 / jnp.sum(powers, axis=0, keepdims=True))).astype(BF)
                pt[b, j, at : at + count, :] = probs
                ot[b, j, :, q0 : q0 + LANES] = pair_down(dot(vt[b, j, :, k0 : k0 + count], probs)).astype(BF)

        loop(pairs, pair)
        for j in range(pairs):
            tok[:, j * LANES : (j + 1) * LANES] = ot[b, j].T

        def out(i):
            out_ref[rows(i, half)] = x_of(rows(i, half)) + dot(tok[rows(i, half)], wo[b])

        loop(2, out)

    def attention_back(b, x_of):
        ga = low[...]
        got[...] = dot_t(wo[b], ga).astype(BF).reshape(pairs, LANES, window)
        for j in range(pairs):
            piece = dot(ot[b, j], ga).astype(BF)
            put_grad(b, 3, j, piece)

        def pair(j):
            gk_sum[...] = jnp.zeros_like(gk_sum)
            gv_sum[...] = jnp.zeros_like(gv_sum)
            for q0, k0, count, at in blocks:
                go_pair = pair_up(got[j, :, q0 : q0 + LANES])
                q_pair = pair_up(qt[b, j, :, q0 : q0 + LANES])
                low_probs = pt[b, j, at : at + count, :]
                probs = low_probs.astype(F32)
                weighted = dot(vr[b, j, k0 : k0 + count, :], go_pair) * probs
                inner = jnp.sum(weighted, axis=0, keepdims=True)
                gs = (weighted - probs * inner).astype(BF)
                gq = pair_down(dot(kt[b, j, :, k0 : k0 + count], gs)) * HD**-0.5
                gt[pl.ds(pl.multiple_of(j * LANES, LANES), LANES), q0 : q0 + LANES] = gq.astype(BF)
                gk_sum[k0 : k0 + count] += dot_t(gs, q_pair)
                gv_sum[k0 : k0 + count] += dot_t(low_probs, go_pair)
            for c, total_of in ((1, gk_sum), (2, gv_sum)):
                gtok[c * pairs + j] = total_of[...].astype(BF)

        loop(pairs, pair)
        for j in range(pairs):
            gtok[j] = gt[j * LANES : (j + 1) * LANES].T
        for c in (1, 2):
            for j in range(pairs):
                at = (c * pairs + j) * LANES
                gt[at : at + LANES] = gtok[c * pairs + j].T
        zz = z[2 * b]
        for c in range(3):
            for j in range(pairs):
                at = (c * pairs + j) * LANES
                put_grad(b, c, j, dot(gt[at : at + LANES], zz).astype(BF))
        gain = gains[2 * b : 2 * b + 1, :]
        gain_grad = jnp.zeros((1, width), F32)

        def back(i, gain_grad):
            wide = jnp.concatenate([gtok[c, rows(i, half)] for c in range(3 * pairs)], axis=1)
            step, part = norm_back(x_of(rows(i, half)), gain, dot(wide, wqkv[b]))
            gx[rows(i, half)] += step
            return gain_grad + part

        small[2 * b : 2 * b + 1, :] = lax.fori_loop(0, 2, back, gain_grad)

    def put_grad(b, c, j, piece):
        at = c * 3 * HD
        if j < 2:
            grad_attn[b, j, at : at + 2 * HD, :] = piece
        else:
            for t in range(2):
                grad_attn[b, t, at + 2 * HD : at + 3 * HD, :] = piece[t * HD : (t + 1) * HD]

    attention(0, lambda r: xw[r].astype(F32), x1)

    def norm_middle(source, which):
        def body(i):
            unit, _ = normalise(source[rows(i)])
            z[which, rows(i)] = (unit * gains[which : which + 1, :]).astype(BF)

        loop(row_blocks, body)

    norm_middle(x1, 1)
    chunk = 256
    chunks = mi.shape[2] // chunk

    def hidden_chunk(i):
        part, at = i // chunks, pl.multiple_of(i % chunks * chunk, chunk)
        value, grad = gelu_parts(dot(z[1], mi[part, :, pl.ds(at, chunk)]))
        hidden[i] = value.astype(BF)
        slope[i] = grad

    loop(2 * chunks, hidden_chunk)

    def dense_out(i):
        h = jnp.concatenate([hidden[c, rows(i, half)] for c in range(2 * chunks)], axis=1)
        sent[rows(i, half)] = (x1[rows(i, half)] + dot(h, mo[...])).astype(BF)

    loop(2, dense_out)

    attention(1, lambda r: sent[r].astype(F32), x3)
    norm_middle(x3, 3)
    z3 = z[3]
    logits = dot_t(routert[...], z3)
    powers = [jnp.exp(logits[e : e + 1, :]) for e in range(2)]
    dispatch, combine = [], []
    for e in range(2):
        totals = jnp.sum(member * powers[e], axis=1, keepdims=True)
        dispatch.append(powers[e] / jnp.sum(member * totals, axis=0, keepdims=True))
        combine.append(powers[e] / (powers[0] + powers[1]))
        d_low = (member * dispatch[e].astype(BF).astype(F32)).astype(BF)
        c_low = (member * combine[e].astype(BF).astype(F32)).astype(BF)
        mixing[0, e * SLOTS : (e + 1) * SLOTS] = d_low
        mixing[1, e * SLOTS : (e + 1) * SLOTS] = c_low
        packs[e, :SLOTS] = dot(d_low, z3).astype(BF)
    for e in range(2):
        value, grad = gelu_parts(dot(packs[e, :SLOTS], ei[e]))
        eslope[e] = grad
        eout[e * SLOTS : (e + 1) * SLOTS] = dot(value.astype(BF), eo[e]).astype(BF)

    def finish(i):
        mixed = t_dot(mixing[1, :, pl.ds(pl.multiple_of(i * LANES, LANES), LANES)], eout[...])
        act[rows(i)] = (x3[rows(i)] + mixed).astype(BF)
        wide = jnp.concatenate([own[rows(i)]] * pairs, axis=1)
        low[rows(i)] = jnp.where(wide > 0.0, cw[rows(i)].astype(F32), 0.0).astype(BF)

    loop(row_blocks, finish)

    gy = low[...]
    slot_grads, logit_grads = [], []
    per_token = []
    for e in range(2):
        part = slice(e * SLOTS, (e + 1) * SLOTS)
        per_token.append(jnp.sum(dot_t(eout[part], gy) * member, axis=0, keepdims=True))
        packs[e, SLOTS:] = dot(mixing[1, part], gy).astype(BF)
    inner = combine[0] * per_token[0] + combine[1] * per_token[1]
    for e in range(2):
        g_hidden = dot_t(packs[e, SLOTS:], eo[e])
        slot_grad = dot_t((g_hidden * eslope[e]).astype(BF), ei[e]).astype(BF)
        slot_grads.append(slot_grad)
        g_dispatch = jnp.sum(dot_t(slot_grad, z3) * member, axis=0, keepdims=True)
        weighted = dispatch[e] * g_dispatch
        sums = jnp.sum(member * weighted, axis=1, keepdims=True)
        from_dispatch = weighted - dispatch[e] * jnp.sum(member * sums, axis=0, keepdims=True)
        logit_grads.append(combine[e] * (per_token[e] - inner) + from_dispatch)
    which = lax.broadcasted_iota(jnp.int32, (SLOTS, window), 0)
    logit_grad = jnp.where(which == 0, logit_grads[0], jnp.where(which == 1, logit_grads[1], 0.0)).astype(BF)
    small[4:6, :] = dot(logit_grad, z3)[:2]
    small[6:8, :] = jnp.zeros((2, width), F32)
    mixing[1, :SLOTS] = logit_grad
    slots_and_router = jnp.concatenate(slot_grads + [routert[...]], axis=0)

    def experts_back(i, gain_grad):
        at = pl.ds(pl.multiple_of(i * LANES, LANES), LANES)
        parts = jnp.concatenate([mixing[0, :, at], mixing[1, :SLOTS, at]], axis=0)
        step, part = norm_back(x3[rows(i)], gains[3:4, :], t_dot(parts, slots_and_router))
        total_of = low[rows(i)].astype(F32) + step
        gx[rows(i)] = total_of
        low[rows(i)] = total_of.astype(BF)
        return gain_grad + part

    small[3:4, :] = lax.fori_loop(0, row_blocks, experts_back, jnp.zeros((1, width), F32))
    attention_back(1, lambda r: sent[r].astype(F32))

    low[...] = gx[...].astype(BF)
    gsent = low[...]
    gsent_t = gsent.T
    z2 = z[1]
    z2_t = z2.T

    def hidden_back(i):
        part, at = i // chunks, pl.multiple_of(i % chunks * chunk, chunk)
        lanes = pl.ds(pl.multiple_of(i * chunk, chunk), chunk)
        grad_mot[:, lanes] = dot(gsent_t, hidden[i]).astype(BF)
        g_hidden = dot_t(gsent, mo[pl.ds(pl.multiple_of(i * chunk, chunk), chunk), :])
        g_pre = (g_hidden * slope[i]).astype(BF)
        hidden[i] = g_pre
        grad_mi[:, lanes] = dot(z2_t, g_pre).astype(BF)

    loop(2 * chunks, hidden_back)

    def dense_back(i, gain_grad):
        gz = jnp.zeros((half, width), F32)
        for part in range(2):
            g = jnp.concatenate([hidden[part * chunks + c, rows(i, half)] for c in range(chunks)], axis=1)
            gz = gz + dot_t(g, mi[part])
        step, part = norm_back(x1[rows(i, half)], gains[1:2, :], gz)
        total_of = low[rows(i, half)].astype(F32) + step
        gx[rows(i, half)] = total_of
        low[rows(i, half)] = total_of.astype(BF)
        return gain_grad + part

    small[1:2, :] = lax.fori_loop(0, 2, dense_back, jnp.zeros((1, width), F32))
    attention_back(0, lambda r: xw[r].astype(F32))
    pg[...] = gx[...].astype(BF)


def compute(xw, cw, ids, gains, wqkv, wo, mi, mo, routert, ei, eo):
    window, width = xw.shape
    pairs = width // LANES
    ff = ei.shape[2]
    _, kept = bands(window)
    chunk_count = 2 * mi.shape[2] // 256
    vmem = pl.BlockSpec(memory_space=pltpu.VMEM)
    return pl.pallas_call(
        compute_kernel,
        out_shape=(
            jax.ShapeDtypeStruct((window, width), BF),
            jax.ShapeDtypeStruct((window, width), BF),
            jax.ShapeDtypeStruct((2, 2, 2 * width, width), BF),
            jax.ShapeDtypeStruct((width, ff), BF),
            jax.ShapeDtypeStruct((width, ff), BF),
            jax.ShapeDtypeStruct((2, 2 * SLOTS, width), BF),
            jax.ShapeDtypeStruct((8, width), F32),
        ),
        in_specs=[vmem] * 11,
        out_specs=[vmem] * 7,
        scratch_shapes=[
            pltpu.VMEM((4, window, width), BF),
            pltpu.VMEM((window, width), F32),
            pltpu.VMEM((window, width), BF),
            pltpu.VMEM((window, width), F32),
            pltpu.VMEM((2, pairs, LANES, window), BF),
            pltpu.VMEM((2, pairs, LANES, window), BF),
            pltpu.VMEM((2, pairs, LANES, window), BF),
            pltpu.VMEM((2, pairs, window, LANES), BF),
            pltpu.VMEM((2, pairs, window, LANES), BF),
            pltpu.VMEM((2, pairs, LANES, window), BF),
            pltpu.VMEM((2, pairs, kept, 2 * LANES), BF),
            pltpu.VMEM((window, width), BF),
            pltpu.VMEM((chunk_count, window, 256), BF),
            pltpu.VMEM((chunk_count, window, 256), F32),
            pltpu.VMEM((window, width), F32),
            pltpu.VMEM((window, width), BF),
            pltpu.VMEM((pairs, LANES, window), BF),
            pltpu.VMEM((3 * width, window), BF),
            pltpu.VMEM((3 * pairs, window, LANES), BF),
            pltpu.VMEM((window, LANES), F32),
            pltpu.VMEM((window, LANES), F32),
            pltpu.VMEM((kept, LANES), F32),
            pltpu.VMEM((window, LANES), F32),
            pltpu.VMEM((2, 2 * SLOTS, window), BF),
            pltpu.VMEM((2, SLOTS, ff), F32),
            pltpu.VMEM((2 * SLOTS, width), BF),
        ],
        compiler_params=pltpu.CompilerParams(vmem_limit_bytes=60 * 1024 * 1024),
    )(xw, cw, ids, gains, wqkv, wo, mi, mo, routert, ei, eo)


def per_device(
    patches, image_ids, cotangent, norm_gains, qkv_weight, out_weight, mlp_in, mlp_out, router, expert_in, expert_out
):
    row_count, width = patches.shape[1:]
    tensor = lax.axis_index("tensor")
    tensors = lax.axis_size("tensor")
    extra = MOST // 2

    def swap(a):
        return lax.ppermute(a, "tensor", [(i, i ^ 1) for i in range(tensors)])

    def edge(a):
        return jnp.where(tensor == 0, a[-extra:], a[:extra])

    def widen(a):
        other = swap(edge(a))
        return jnp.where(tensor == 0, jnp.concatenate([a, other]), jnp.concatenate([other, a]))

    xw, cw = widen(patches[0]), widen(cotangent[0])

    def gathered(a, axes):
        for axis in axes:
            a = lax.all_gather(a, axis)
        return a

    heads = qkv_weight.shape[3] // HD
    tall = jnp.transpose(qkv_weight[0], (1, 2, 0)).reshape(3, heads, HD, width)
    tall = gathered(tall, ("tensor", "section"))

    def by_pairs(a):
        n = a.shape[2]
        a0, a1 = a[:, 0], a[:, 1]
        order = [a0[:, :, 0], a0[:, :, 1], a1[:, :, 0], a1[:, :, 1], a0[:, :, 2], a1[:, :, 2]]
        return jnp.stack(order, axis=2).reshape(a.shape[0], n * 2 * heads * HD, width)

    wqkv = by_pairs(tall)
    wo = by_pairs(gathered(out_weight[0].reshape(1, heads, HD, width), ("tensor", "section")))
    mi = gathered(mlp_in, ("tensor",))
    mo = gathered(mlp_out, ("tensor",)).reshape(-1, width)
    routert = gathered(router.T, ("tensor",)).reshape(-1, width)
    routert = jnp.pad(routert, ((0, SLOTS - routert.shape[0]), (0, 0)))
    ei = gathered(expert_in[0], ("tensor",))
    eo = gathered(expert_out[0], ("tensor",))
    gains = gathered(norm_gains[0], ("section",)).reshape(-1, width)

    act, pg, grad_attn, grad_mi, grad_mot, packs, small = compute(
        xw, cw, image_ids, gains, wqkv, wo, mi, mo, routert, ei, eo
    )

    ids_row = lax.dynamic_index_in_dim(image_ids, lax.axis_index("section"), 0, keepdims=False)
    total = ids_row.shape[0]
    of_image = jnp.arange(IMAGES)
    middle = jnp.sum(ids_row[None] < of_image[:, None], axis=1) + jnp.sum(ids_row[None] <= of_image[:, None], axis=1)
    is_first = jnp.sum((ids_row[:, None] == of_image[None]) * (middle < total)[None], axis=1)
    mine = lax.dynamic_slice_in_dim(is_first == (1 - tensor), tensor * row_count, row_count, 0)

    def merge(a):
        sent_out = jnp.where(tensor == 0, a[-extra:], a[:extra])
        arrived = swap(sent_out)
        own = jnp.where(tensor == 0, a[:row_count], a[extra:])
        blank = jnp.zeros((row_count - extra, width), a.dtype)
        other = jnp.where(tensor == 0, jnp.concatenate([blank, arrived]), jnp.concatenate([arrived, blank]))
        return jnp.where(mine[:, None], own, other)[None]

    activations, patch_grad = merge(act), merge(pg)

    rest = tuple(n for n in ("dp", "section", "tensor"))
    small = lax.psum(small, rest)
    gains_grad = lax.dynamic_slice_in_dim(small, 2 * lax.axis_index("section"), 2, 0)[None]
    router_grad = lax.dynamic_slice_in_dim(small, 4 + tensor, 1, 0).T
    grad_attn = lax.psum(grad_attn.astype(F32), rest)
    attn = lax.dynamic_index_in_dim(grad_attn, lax.axis_index("section"), 0, keepdims=False)
    attn = lax.dynamic_index_in_dim(attn, tensor, 0, keepdims=False)
    rows = 3 * heads * HD
    qkv_grad = jnp.transpose(attn[:rows].reshape(3, heads * HD, width), (2, 0, 1))[None]
    out_grad = attn[rows:][None]
    grad_mi = lax.psum(grad_mi.astype(F32), rest)
    grad_mot = lax.psum(grad_mot.astype(F32), rest)
    part = mlp_in.shape[1]
    mlp_in_grad = lax.dynamic_slice_in_dim(grad_mi, tensor * part, part, 1)
    mlp_out_grad = lax.dynamic_slice_in_dim(grad_mot, tensor * part, part, 1).T
    packs = lax.all_gather(packs, rest)
    packs = lax.dynamic_index_in_dim(packs, tensor, 1, keepdims=False)
    slots = packs[:, :SLOTS].reshape(-1, width)
    geo = packs[:, SLOTS:].reshape(-1, width)
    value, slope = gelu_parts(dot(slots, expert_in[0]))
    g_pre = (dot_t(geo, expert_out[0]) * slope).astype(BF)
    expert_in_grad = t_dot(slots, g_pre)[None]
    expert_out_grad = t_dot(value.astype(BF), geo)[None]
    return (
        activations, patch_grad, gains_grad, qkv_grad, out_grad, mlp_in_grad, mlp_out_grad, router_grad,
        expert_in_grad, expert_out_grad,
    )


def solution(mesh):
    return jax.shard_map(
        per_device,
        mesh=mesh,
        in_specs=(
            P(("dp", "section"), "tensor", None),
            P("dp", None),
            P(("dp", "section"), "tensor", None),
            P("section", None, None),
            P("section", None, None, "tensor"),
            P("section", "tensor", None),
            P(None, "tensor"),
            P("tensor", None),
            P(None, "tensor"),
            P("tensor", None, None),
            P("tensor", None, None),
        ),
        out_specs=(
            P(("dp", "section"), "tensor", None),
            P(("dp", "section"), "tensor", None),
            P("section", None, None),
            P("section", None, None, "tensor"),
            P("section", "tensor", None),
            P(None, "tensor"),
            P("tensor", None),
            P(None, "tensor"),
            P("tensor", None, None),
            P("tensor", None, None),
        ),
        check_vma=False,
    )
```

```python
import functools

import jax
import jax.numpy as jnp
from jax import lax
from jax.experimental import pallas as pl
from jax.experimental.pallas import tpu as pltpu
from jax.sharding import PartitionSpec as P

HD = 64
IMAGES = 8
MOST = 256
LANES = 128
SLOTS = 16
EPSILON = 1e-06
BF = jnp.bfloat16
F32 = jnp.float32


def dot(a, b):
    return jnp.dot(a, b, preferred_element_type=F32)


def dot_t(a, b):
    return lax.dot_general(a, b, (((1,), (1,)), ((), ())), preferred_element_type=F32)


def t_dot(a, b):
    return lax.dot_general(a, b, (((0,), (0,)), ((), ())), preferred_element_type=F32)


def normalise(x):
    centred = x - jnp.mean(x, axis=-1, keepdims=True)
    scale = lax.rsqrt(jnp.mean(centred * centred, axis=-1, keepdims=True) + EPSILON)
    return centred * scale, scale


def norm_back(x, gain, gz):
    unit, scale = normalise(x)
    scaled = gz * gain
    mean_plain = jnp.mean(scaled, axis=-1, keepdims=True)
    mean_unit = jnp.mean(scaled * unit, axis=-1, keepdims=True)
    return scale * (scaled - mean_plain - unit * mean_unit), jnp.sum(gz * unit, axis=0, keepdims=True)


def gelu_parts(u):
    cdf = 0.5 * (1.0 + lax.erf(u * 0.7071067811865476))
    return u * cdf, cdf + u * (0.3989422804014327 * jnp.exp(-0.5 * u * u))


def pair_up(tile):
    row = lax.broadcasted_iota(jnp.int32, tile.shape, 0)
    zero = jnp.zeros_like(tile)
    return jnp.concatenate([jnp.where(row < HD, tile, zero), jnp.where(row >= HD, tile, zero)], axis=1)


def pair_down(both):
    n = both.shape[1] // 2
    row = lax.broadcasted_iota(jnp.int32, (both.shape[0], n), 0)
    return jnp.where(row < HD, both[:, :n], both[:, n:])


def bands(window):
    reach = MOST // LANES
    found, at = [], 0
    for i in range(window // LANES):
        first = max(0, i - reach) * LANES
        count = min(window, (i + reach + 1) * LANES) - first
        found.append((i * LANES, first, count, at))
        at += count
    return found, at


MESH = pl.DeviceIdType.MESH


def compute_kernel(
    x_own, c_own, ids, gains_own, w_own, mi_own, mo_own, router_own, ei, eo,
    act_out, pg_out, grad_attn, grad_mi, grad_mot, pack, small,
    xw, cw, gains, wy, wc, wqkv, wo, mi, mo, routert, act, edge_in, slots, geos, slot_in,
    z, x1, sent, x3, qt, kt, vt, kr, vr, ot, pt, tok, hidden, slope, gx, low, got, gt, gtok, gk_sum, gv_sum,
    bias, own, mixing, eslope, eout, gslot, send_sem, recv_sem,
):
    row_count, width = x_own.shape
    window = xw.shape[0]
    extra = window - row_count
    half = window // 2
    pairs = width // LANES
    total = ids.shape[1]
    dp = lax.axis_index("dp")
    section = lax.axis_index("section")
    tensor = lax.axis_index("tensor")
    core = (dp, 1 - section, tensor)
    beside = (dp, section, 1 - tensor)
    blocks, _ = bands(window)
    row_blocks = window // LANES

    def at(start, size, step=LANES):
        return pl.ds(pl.multiple_of(start, step), size)

    def rows(i, n=LANES):
        return pl.ds(pl.multiple_of(i * n, n), n)

    def loop(n, body):
        def step(i, carry):
            body(i)
            return carry

        lax.fori_loop(0, n, step, 0)

    sending = []

    def copy(key, source, dest, device):
        return pltpu.make_async_remote_copy(
            src_ref=source,
            dst_ref=dest,
            send_sem=send_sem.at[key],
            recv_sem=recv_sem.at[key],
            device_id=device,
            device_id_type=MESH,
        )

    def send(key, source, dest, device):
        copy(key, source, dest, device).start()
        sending.append((key, source, dest, device, None))

    def arrived(key, dest):
        copy(key, dest, dest, core).wait_recv()

    def on(which, body):
        pl.when(section == which)(body)

    barrier = pltpu.get_barrier_semaphore()
    for device in (core, beside):
        pl.semaphore_signal(barrier, inc=1, device_id=device, device_id_type=MESH)
    pl.semaphore_wait(barrier, 2)

    edge = x_own.at[at((1 - tensor) * (row_count - extra), extra)]
    send(0, edge, xw.at[at(tensor * row_count, extra)], beside)
    send(1, gains_own, gains.at[section], core)
    send(2, w_own, wc.at[0], core)

    @pl.when(section == 0)
    def _():
        copy(3, w_own, wy, beside).start()

    def local(dest, source):
        dest[...] = source[...]

    local(xw.at[at(tensor * extra, row_count)], x_own)
    local(cw.at[at(tensor * extra, row_count)], c_own)
    local(mi.at[tensor], mi_own)
    local(mo.at[tensor], mo_own)
    local(gains.at[section], gains_own)

    ids_row = ids[pl.ds(section, 1), :].astype(F32)
    image = lax.broadcasted_iota(jnp.int32, (SLOTS, total), 0).astype(F32)
    spread = jnp.broadcast_to(ids_row, (SLOTS, total))
    middle = jnp.sum((spread < image).astype(F32) + (spread <= image).astype(F32), axis=1, keepdims=True)
    first_half = (middle < total).astype(F32)
    mine = jnp.where(tensor == 0, first_half, 1.0 - first_half)
    window_ids = ids[pl.ds(section, 1), at(tensor * (total - window), window)].astype(F32)
    member = (jnp.broadcast_to(window_ids, (SLOTS, window)) == image[:, :window]).astype(F32)
    member_own = member * mine
    own_row = jnp.sum(member_own, axis=0, keepdims=True)
    own[...] = jnp.broadcast_to(own_row, (LANES, window)).T
    ids_col = jnp.broadcast_to(window_ids, (LANES, window)).T
    for q0, k0, count, kept in blocks:
        same = ids_col[k0 : k0 + count] == jnp.broadcast_to(window_ids[:, q0 : q0 + LANES], (count, LANES))
        bias[kept : kept + count, :] = jnp.where(same, 0.0, -1e30)

    def place(source, b, t):
        for c in range(4):
            dest, base = (wqkv, c * width) if c < 3 else (wo, 0)
            first = c * 3 * HD
            dest[b, at(base + t * LANES, 2 * HD)] = source[first : first + 2 * HD]
            dest[b, at(base + 2 * LANES + t * HD, HD, HD)] = source[first + 2 * HD : first + 3 * HD]

    arrived(0, xw.at[at((1 - tensor) * row_count, extra)])
    arrived(1, gains.at[1 - section])
    arrived(2, wc.at[0])
    place(w_own, section, tensor)
    place(wc.at[0], 1 - section, tensor)

    @pl.when(section == 0)
    def _():
        arrived(3, wy)
        copy(4, wy, wc.at[1], core).start()
        copy(5, mi_own, mi.at[tensor], beside).start()
        place(wy, 0, 1 - tensor)

    @pl.when(section == 1)
    def _():
        copy(5, mo_own, mo.at[tensor], beside).start()
        copy(3, w_own, wy, beside).start()
        arrived(4, wc.at[1])
        place(wc.at[1], 0, 1 - tensor)

    c_edge = c_own.at[at((1 - tensor) * (row_count - extra), extra)]
    send(7, c_edge, cw.at[at(tensor * row_count, extra)], beside)
    send(8, router_own, routert.at[tensor], beside)

    def attention(b, x_of, out_ref):
        def norm(i):
            unit, _ = normalise(x_of(rows(i)))
            z[2 * b, rows(i)] = (unit * gains[b, 0:1, :]).astype(BF)

        loop(row_blocks, norm)
        zz = z[2 * b]
        for c, dest in enumerate((qt, kt, vt)):
            tall = dot_t(wqkv[b, c * width : (c + 1) * width], zz)
            tall = (tall.astype(BF) * jnp.asarray(HD**-0.5 if c == 0 else 1.0, BF)).reshape(pairs, LANES, window)
            dest[b] = tall
        for c, dest in ((1, kr), (2, vr)):
            flat = dot_t(zz, wqkv[b, c * width : (c + 1) * width]).astype(BF)
            for j in range(pairs):
                dest[b, j] = flat[:, j * LANES : (j + 1) * LANES]

        def pair(j):
            for q0, k0, count, kept in blocks:
                scores = dot(kr[b, j, k0 : k0 + count, :], pair_up(qt[b, j, :, q0 : q0 + LANES]))
                veil = bias[kept : kept + count, :]
                scores = scores + jnp.concatenate([veil, veil], axis=1)
                powers = jnp.exp(scores - jnp.max(scores, axis=0, keepdims=True))
                probs = (powers * (1.0 / jnp.sum(powers, axis=0, keepdims=True))).astype(BF)
                pt[b, j, kept : kept + count, :] = probs
                ot[b, j, :, q0 : q0 + LANES] = pair_down(dot(vt[b, j, :, k0 : k0 + count], probs)).astype(BF)

        loop(pairs, pair)
        for j in range(pairs):
            tok[:, j * LANES : (j + 1) * LANES] = ot[b, j].T

        def out(i):
            out_ref[rows(i, half)] = x_of(rows(i, half)) + dot(tok[rows(i, half)], wo[b])

        loop(2, out)

    def attention_back(b, x_of):
        ga = low[...]
        got[...] = dot_t(wo[b], ga).astype(BF).reshape(pairs, LANES, window)
        for j in range(pairs):
            piece = dot(ot[b, j], ga).astype(BF)
            put_grad(b, 3, j, piece)

        def pair(j):
            gk_sum[...] = jnp.zeros_like(gk_sum)
            gv_sum[...] = jnp.zeros_like(gv_sum)
            for q0, k0, count, kept in blocks:
                go_pair = pair_up(got[j, :, q0 : q0 + LANES])
                q_pair = pair_up(qt[b, j, :, q0 : q0 + LANES])
                low_probs = pt[b, j, kept : kept + count, :]
                probs = low_probs.astype(F32)
                weighted = dot(vr[b, j, k0 : k0 + count, :], go_pair) * probs
                inner = jnp.sum(weighted, axis=0, keepdims=True)
                gs = (weighted - probs * inner).astype(BF)
                gq = pair_down(dot(kt[b, j, :, k0 : k0 + count], gs)) * HD**-0.5
                gt[pl.ds(pl.multiple_of(j * LANES, LANES), LANES), q0 : q0 + LANES] = gq.astype(BF)
                gk_sum[k0 : k0 + count] += dot_t(gs, q_pair)
                gv_sum[k0 : k0 + count] += dot_t(low_probs, go_pair)
            for c, total_of in ((1, gk_sum), (2, gv_sum)):
                gtok[c * pairs + j] = total_of[...].astype(BF)

        loop(pairs, pair)
        for j in range(pairs):
            gtok[j] = gt[j * LANES : (j + 1) * LANES].T
        for c in (1, 2):
            for j in range(pairs):
                first = (c * pairs + j) * LANES
                gt[first : first + LANES] = gtok[c * pairs + j].T
        zz = z[2 * b]
        for c in range(3):
            for j in range(pairs):
                first = (c * pairs + j) * LANES
                put_grad(b, c, j, dot(gt[first : first + LANES], zz).astype(BF))
        gain = gains[b, 0:1, :]
        gain_grad = jnp.zeros((1, width), F32)

        def back(i, gain_grad):
            wide = jnp.concatenate([gtok[c, rows(i, half)] for c in range(3 * pairs)], axis=1)
            step, part = norm_back(x_of(rows(i, half)), gain, dot(wide, wqkv[b]))
            gx[rows(i, half)] += step
            return gain_grad + part

        small[2 * b : 2 * b + 1, :] = lax.fori_loop(0, 2, back, gain_grad)

    def put_grad(b, c, j, piece):
        first = c * 3 * HD
        if j < 2:
            grad_attn[b, j, first : first + 2 * HD, :] = piece
        else:
            for t in range(2):
                grad_attn[b, t, first + 2 * HD : first + 3 * HD, :] = piece[t * HD : (t + 1) * HD]

    attention(0, lambda r: xw[r].astype(F32), x1)

    def norm_middle(source, which):
        def body(i):
            unit, _ = normalise(source[rows(i)])
            z[which, rows(i)] = (unit * gains[which // 2, 1:2, :]).astype(BF)

        loop(row_blocks, body)

    norm_middle(x1, 1)

    @pl.when(section == 0)
    def _():
        arrived(5, mi.at[1 - tensor])
        copy(6, mi.at[1 - tensor], mi.at[1 - tensor], core).start()
        arrived(6, mo.at[1 - tensor])

    @pl.when(section == 1)
    def _():
        arrived(5, mo.at[1 - tensor])
        copy(6, mo.at[1 - tensor], mo.at[1 - tensor], core).start()
        arrived(6, mi.at[1 - tensor])

    chunk = 256
    chunks = mi.shape[2] // chunk

    def hidden_chunk(i):
        part, first = i // chunks, pl.multiple_of(i % chunks * chunk, chunk)
        value, grad = gelu_parts(dot(z[1], mi[part, :, pl.ds(first, chunk)]))
        hidden[i] = value.astype(BF)
        slope[i] = grad

    loop(2 * chunks, hidden_chunk)

    def dense_out(i):
        h = jnp.concatenate([hidden[c, rows(i, half)] for c in range(2 * chunks)], axis=1)
        sent[rows(i, half)] = (x1[rows(i, half)] + dot(h, mo[...].reshape(-1, width))).astype(BF)

    loop(2, dense_out)

    @pl.when(section == 0)
    def _():
        arrived(4, wc.at[1])
        place(wc.at[1], 1, 1 - tensor)

    @pl.when(section == 1)
    def _():
        arrived(3, wy)
        copy(4, wy, wc.at[1], core).start()
        place(wy, 1, 1 - tensor)

    attention(1, lambda r: sent[r].astype(F32), x3)
    norm_middle(x3, 3)
    z3 = z[3]
    local(routert.at[tensor], router_own)
    arrived(8, routert.at[1 - tensor])
    powers = [jnp.exp(dot_t(routert[e], z3)[:1]) for e in range(2)]
    dispatch, combine = [], []
    for e in range(2):
        totals = jnp.sum(member * powers[e], axis=1, keepdims=True)
        dispatch.append(powers[e] / jnp.sum(member * totals, axis=0, keepdims=True))
        combine.append(powers[e] / (powers[0] + powers[1]))
        d_low = (member_own * dispatch[e].astype(BF).astype(F32)).astype(BF)
        c_low = (member * combine[e].astype(BF).astype(F32)).astype(BF)
        mixing[0, e * SLOTS : (e + 1) * SLOTS] = d_low
        mixing[1, e * SLOTS : (e + 1) * SLOTS] = c_low
        slots[e] = dot(d_low, z3).astype(BF)
    send(9, slots.at[1 - tensor], slot_in.at[0], beside)
    arrived(7, cw.at[at((1 - tensor) * row_count, extra)])

    def mask(i):
        wide = jnp.concatenate([own[rows(i)]] * pairs, axis=1)
        low[rows(i)] = jnp.where(wide > 0.0, cw[rows(i)].astype(F32), 0.0).astype(BF)

    loop(row_blocks, mask)
    gy = low[...]
    for e in range(2):
        geos[e] = dot(mixing[1, e * SLOTS : (e + 1) * SLOTS], gy).astype(BF)
    send(10, geos.at[1 - tensor], slot_in.at[1], beside)

    arrived(9, slot_in.at[0])
    pack[:SLOTS] = slots[tensor] + slot_in[0]
    value, grad = gelu_parts(dot(pack[:SLOTS], ei[...]))
    eslope[...] = grad
    eout[tensor] = dot(value.astype(BF), eo[...]).astype(BF)
    send(11, eout.at[tensor], eout.at[tensor], beside)
    arrived(10, slot_in.at[1])
    pack[SLOTS:] = geos[tensor] + slot_in[1]
    g_hidden = dot_t(pack[SLOTS:], eo[...])
    gslot[tensor] = dot_t((g_hidden * eslope[...]).astype(BF), ei[...]).astype(BF)
    send(12, gslot.at[tensor], gslot.at[tensor], beside)
    arrived(11, eout.at[1 - tensor])
    outputs = eout[...].reshape(2 * SLOTS, width)

    def finish(i):
        mixed = t_dot(mixing[1, :, rows(i)], outputs)
        act[rows(i)] = (x3[rows(i)] + mixed).astype(BF)

    loop(row_blocks, finish)
    send(13, act.at[at((1 - tensor) * row_count, extra)], edge_in.at[0], beside)

    per_token = [jnp.sum(dot_t(eout[e], gy) * member, axis=0, keepdims=True) for e in range(2)]
    inner = combine[0] * per_token[0] + combine[1] * per_token[1]
    arrived(12, gslot.at[1 - tensor])
    logit_grads = []
    for e in range(2):
        g_dispatch = jnp.sum(dot_t(gslot[e], z3) * member_own, axis=0, keepdims=True)
        weighted = dispatch[e] * g_dispatch
        sums = jnp.sum(member * weighted, axis=1, keepdims=True)
        from_dispatch = weighted - dispatch[e] * jnp.sum(member * sums, axis=0, keepdims=True)
        logit_grads.append(combine[e] * (per_token[e] - inner) + from_dispatch)
    which_row = lax.broadcasted_iota(jnp.int32, (SLOTS, width), 0)
    router_rows = jnp.where(
        which_row == 0,
        jnp.broadcast_to(routert[0].astype(F32)[:1], (SLOTS, width)),
        jnp.where(which_row == 1, jnp.broadcast_to(routert[1].astype(F32)[:1], (SLOTS, width)), 0.0),
    ).astype(BF)
    which = lax.broadcasted_iota(jnp.int32, (SLOTS, window), 0)
    logit_grad = jnp.where(which == 0, logit_grads[0], jnp.where(which == 1, logit_grads[1], 0.0)).astype(BF)
    small[4:6, :] = dot(logit_grad, z3)[:2]
    small[6:8, :] = jnp.zeros((2, width), F32)
    mixing[1, :SLOTS] = logit_grad
    slots_and_router = jnp.concatenate([gslot[0], gslot[1], router_rows], axis=0)

    def experts_back(i, gain_grad):
        at = pl.ds(pl.multiple_of(i * LANES, LANES), LANES)
        parts = jnp.concatenate([mixing[0, :, at], mixing[1, :SLOTS, at]], axis=0)
        step, part = norm_back(x3[rows(i)], gains[1, 1:2, :], t_dot(parts, slots_and_router))
        total_of = low[rows(i)].astype(F32) + step
        gx[rows(i)] = total_of
        low[rows(i)] = total_of.astype(BF)
        return gain_grad + part

    small[3:4, :] = lax.fori_loop(0, row_blocks, experts_back, jnp.zeros((1, width), F32))
    attention_back(1, lambda r: sent[r].astype(F32))

    low[...] = gx[...].astype(BF)
    gsent = low[...]
    gsent_t = gsent.T
    z2 = z[1]
    z2_t = z2.T

    def hidden_back(i):
        part, first = i // chunks, pl.multiple_of(i % chunks * chunk, chunk)
        lanes = pl.ds(pl.multiple_of(i * chunk, chunk), chunk)
        grad_mot[:, lanes] = dot(gsent_t, hidden[i]).astype(BF)
        g_hidden = dot_t(gsent, mo[part, pl.ds(first, chunk), :])
        g_pre = (g_hidden * slope[i]).astype(BF)
        hidden[i] = g_pre
        grad_mi[:, lanes] = dot(z2_t, g_pre).astype(BF)

    loop(2 * chunks, hidden_back)

    def dense_back(i, gain_grad):
        gz = jnp.zeros((half, width), F32)
        for part in range(2):
            g = jnp.concatenate([hidden[part * chunks + c, rows(i, half)] for c in range(chunks)], axis=1)
            gz = gz + dot_t(g, mi[part])
        step, part = norm_back(x1[rows(i, half)], gains[0, 1:2, :], gz)
        total_of = low[rows(i, half)].astype(F32) + step
        gx[rows(i, half)] = total_of
        low[rows(i, half)] = total_of.astype(BF)
        return gain_grad + part

    small[1:2, :] = lax.fori_loop(0, 2, dense_back, jnp.zeros((1, width), F32))
    attention_back(0, lambda r: xw[r].astype(F32))
    low[...] = gx[...].astype(BF)
    send(14, low.at[at((1 - tensor) * row_count, extra)], edge_in.at[1], beside)

    for n, (source, dest) in enumerate(((act, act_out), (low, pg_out))):
        dest[...] = source[at(tensor * extra, row_count)]
        arrived(13 + n, edge_in.at[n])
        near = at(row_count - extra - tensor * (row_count - 2 * extra), extra)
        wide = jnp.concatenate([own[near]] * pairs, axis=1)
        merged = jnp.where(wide > 0.0, source[near].astype(F32), edge_in[n].astype(F32)).astype(BF)
        dest[at((1 - tensor) * (row_count - extra), extra)] = merged

    for key, source, dest, device, _ in sending:
        copy(key, source, dest, device).wait_send()
    copy(3, w_own, wy, beside).wait_send()
    copy(4, wy, wc.at[1], core).wait_send()
    copy(5, mi_own, mi.at[tensor], beside).wait_send()
    copy(6, mi.at[1 - tensor], mi.at[1 - tensor], core).wait_send()


def compute(x_own, c_own, ids, gains, w_own, mi, mo, router, ei, eo):
    row_count, width = x_own.shape
    window = row_count + MOST // 2
    extra = window - row_count
    pairs = width // LANES
    ff = ei.shape[1]
    _, kept = bands(window)
    chunk_count = 2 * mi.shape[1] // 256
    vmem = pl.BlockSpec(memory_space=pltpu.VMEM)
    copies = 15
    return pl.pallas_call(
        compute_kernel,
        out_shape=(
            jax.ShapeDtypeStruct((row_count, width), BF),
            jax.ShapeDtypeStruct((row_count, width), BF),
            jax.ShapeDtypeStruct((2, 2, 2 * width, width), BF),
            jax.ShapeDtypeStruct((width, ff), BF),
            jax.ShapeDtypeStruct((width, ff), BF),
            jax.ShapeDtypeStruct((2 * SLOTS, width), BF),
            jax.ShapeDtypeStruct((8, width), F32),
        ),
        in_specs=[vmem] * 10,
        out_specs=[vmem] * 7,
        scratch_shapes=[
            pltpu.VMEM((window, width), BF),
            pltpu.VMEM((window, width), BF),
            pltpu.VMEM((2, 8, width), F32),
            pltpu.VMEM((2 * width, width), BF),
            pltpu.VMEM((2, 2 * width, width), BF),
            pltpu.VMEM((2, 3 * width, width), BF),
            pltpu.VMEM((2, width, width), BF),
            pltpu.VMEM((2, *mi.shape), BF),
            pltpu.VMEM((2, *mo.shape), BF),
            pltpu.VMEM((2, SLOTS, width), BF),
            pltpu.VMEM((window, width), BF),
            pltpu.VMEM((2, extra, width), BF),
            pltpu.VMEM((2, SLOTS, width), BF),
            pltpu.VMEM((2, SLOTS, width), BF),
            pltpu.VMEM((2, SLOTS, width), BF),
            pltpu.VMEM((4, window, width), BF),
            pltpu.VMEM((window, width), F32),
            pltpu.VMEM((window, width), BF),
            pltpu.VMEM((window, width), F32),
            pltpu.VMEM((2, pairs, LANES, window), BF),
            pltpu.VMEM((2, pairs, LANES, window), BF),
            pltpu.VMEM((2, pairs, LANES, window), BF),
            pltpu.VMEM((2, pairs, window, LANES), BF),
            pltpu.VMEM((2, pairs, window, LANES), BF),
            pltpu.VMEM((2, pairs, LANES, window), BF),
            pltpu.VMEM((2, pairs, kept, 2 * LANES), BF),
            pltpu.VMEM((window, width), BF),
            pltpu.VMEM((chunk_count, window, 256), BF),
            pltpu.VMEM((chunk_count, window, 256), F32),
            pltpu.VMEM((window, width), F32),
            pltpu.VMEM((window, width), BF),
            pltpu.VMEM((pairs, LANES, window), BF),
            pltpu.VMEM((3 * width, window), BF),
            pltpu.VMEM((3 * pairs, window, LANES), BF),
            pltpu.VMEM((window, LANES), F32),
            pltpu.VMEM((window, LANES), F32),
            pltpu.VMEM((kept, LANES), F32),
            pltpu.VMEM((window, LANES), F32),
            pltpu.VMEM((2, 2 * SLOTS, window), BF),
            pltpu.VMEM((SLOTS, ff), F32),
            pltpu.VMEM((2, SLOTS, width), BF),
            pltpu.VMEM((2, SLOTS, width), BF),
            pltpu.SemaphoreType.DMA((copies,)),
            pltpu.SemaphoreType.DMA((copies,)),
        ],
        compiler_params=pltpu.CompilerParams(
            vmem_limit_bytes=60 * 1024 * 1024, collective_id=0, has_side_effects=True
        ),
    )(x_own, c_own, ids, gains, w_own, mi, mo, router, ei, eo)


def per_device(
    patches, image_ids, cotangent, norm_gains, qkv_weight, out_weight, mlp_in, mlp_out, router, expert_in, expert_out
):
    width = patches.shape[2]
    tensor = lax.axis_index("tensor")
    heads = qkv_weight.shape[3] // HD
    w_own = jnp.concatenate([jnp.transpose(qkv_weight[0], (1, 2, 0)).reshape(-1, width), out_weight[0]], axis=0)
    gains = jnp.pad(norm_gains[0], ((0, 6), (0, 0)))
    router_own = jnp.pad(router.T, ((0, SLOTS - router.shape[1]), (0, 0)))
    activations, patch_grad, grad_attn, grad_mi, grad_mot, pack, small = compute(
        patches[0], cotangent[0], image_ids, gains, w_own, mlp_in, mlp_out, router_own, expert_in[0], expert_out[0]
    )
    activations, patch_grad = activations[None], patch_grad[None]

    rest = tuple(n for n in ("dp", "section", "tensor"))
    small = lax.psum(small, rest)
    gains_grad = lax.dynamic_slice_in_dim(small, 2 * lax.axis_index("section"), 2, 0)[None]
    router_grad = lax.dynamic_slice_in_dim(small, 4 + tensor, 1, 0).T
    grad_attn = lax.psum(grad_attn.astype(F32), rest)
    attn = lax.dynamic_index_in_dim(grad_attn, lax.axis_index("section"), 0, keepdims=False)
    attn = lax.dynamic_index_in_dim(attn, tensor, 0, keepdims=False)
    rows = 3 * heads * HD
    qkv_grad = jnp.transpose(attn[:rows].reshape(3, heads * HD, width), (2, 0, 1))[None]
    out_grad = attn[rows:][None]
    grad_mi = lax.psum(grad_mi.astype(F32), rest)
    grad_mot = lax.psum(grad_mot.astype(F32), rest)
    part = mlp_in.shape[1]
    mlp_in_grad = lax.dynamic_slice_in_dim(grad_mi, tensor * part, part, 1)
    mlp_out_grad = lax.dynamic_slice_in_dim(grad_mot, tensor * part, part, 1).T
    packs = lax.all_gather(pack, ("dp", "section"))
    slots = packs[:, :SLOTS].reshape(-1, width)
    geo = packs[:, SLOTS:].reshape(-1, width)
    value, slope = gelu_parts(dot(slots, expert_in[0]))
    g_pre = (dot_t(geo, expert_out[0]) * slope).astype(BF)
    expert_in_grad = t_dot(slots, g_pre)[None]
    expert_out_grad = t_dot(value.astype(BF), geo)[None]
    return (
        activations, patch_grad, gains_grad, qkv_grad, out_grad, mlp_in_grad, mlp_out_grad, router_grad,
        expert_in_grad, expert_out_grad,
    )


def solution(mesh):
    return jax.shard_map(
        per_device,
        mesh=mesh,
        in_specs=(
            P(("dp", "section"), "tensor", None),
            P("dp", None),
            P(("dp", "section"), "tensor", None),
            P("section", None, None),
            P("section", None, None, "tensor"),
            P("section", "tensor", None),
            P(None, "tensor"),
            P("tensor", None),
            P(None, "tensor"),
            P("tensor", None, None),
            P("tensor", None, None),
        ),
        out_specs=(
            P(("dp", "section"), "tensor", None),
            P(("dp", "section"), "tensor", None),
            P("section", None, None),
            P("section", None, None, "tensor"),
            P("section", "tensor", None),
            P(None, "tensor"),
            P("tensor", None),
            P(None, "tensor"),
            P("tensor", None, None),
            P("tensor", None, None),
        ),
        check_vma=False,
    )
```

```python
import functools

import jax
import jax.numpy as jnp
from jax import lax
from jax.experimental import pallas as pl
from jax.experimental.pallas import tpu as pltpu
from jax.sharding import PartitionSpec as P

HD = 64
IMAGES = 8
MOST = 256
LANES = 128
SLOTS = 16
EPSILON = 1e-06
BF = jnp.bfloat16
F32 = jnp.float32


def dot(a, b):
    return jnp.dot(a, b, preferred_element_type=F32)


def dot_t(a, b):
    return lax.dot_general(a, b, (((1,), (1,)), ((), ())), preferred_element_type=F32)


def t_dot(a, b):
    return lax.dot_general(a, b, (((0,), (0,)), ((), ())), preferred_element_type=F32)


def normalise(x):
    centred = x - jnp.mean(x, axis=-1, keepdims=True)
    scale = lax.rsqrt(jnp.mean(centred * centred, axis=-1, keepdims=True) + EPSILON)
    return centred * scale, scale


def norm_back(x, gain, gz):
    unit, scale = normalise(x)
    scaled = gz * gain
    mean_plain = jnp.mean(scaled, axis=-1, keepdims=True)
    mean_unit = jnp.mean(scaled * unit, axis=-1, keepdims=True)
    return scale * (scaled - mean_plain - unit * mean_unit), jnp.sum(gz * unit, axis=0, keepdims=True)


def gelu_parts(u):
    cdf = 0.5 * (1.0 + lax.erf(u * 0.7071067811865476))
    return u * cdf, cdf + u * (0.3989422804014327 * jnp.exp(-0.5 * u * u))


def pair_up(tile):
    row = lax.broadcasted_iota(jnp.int32, tile.shape, 0)
    zero = jnp.zeros_like(tile)
    return jnp.concatenate([jnp.where(row < HD, tile, zero), jnp.where(row >= HD, tile, zero)], axis=1)


def pair_down(both):
    n = both.shape[1] // 2
    row = lax.broadcasted_iota(jnp.int32, (both.shape[0], n), 0)
    return jnp.where(row < HD, both[:, :n], both[:, n:])


def bands(window):
    reach = MOST // LANES
    found, at = [], 0
    for i in range(window // LANES):
        first = max(0, i - reach) * LANES
        count = min(window, (i + reach + 1) * LANES) - first
        found.append((i * LANES, first, count, at))
        at += count
    return found, at


MESH = pl.DeviceIdType.MESH


def compute_kernel(
    x_own, c_own, ids, gains_own, w_own, mi_own, mo_own, router_own, ei, eo,
    act_out, pg_out, attn_out, mlp_out, expert_in_out, expert_out_out, small_out,
    xw, cw, gains, wy, wc, wqkv, wo, mi, mo, routert, act, edge_in, slots, geos, slot_in, pack,
    z, x1, sent, x3, qt, kt, vt, kr, vr, ot, pt, tok, hidden, slope, gx, low, got, gt, gtok, gk_sum, gv_sum,
    bias, own, mixing, eslope, eout, gslot,
    grad_attn, attn_parts, attn_across, attn_sum,
    grad_mlp, mlp_core, mlp_beside, mlp_parts, mlp_across, mlp_sum,
    small, small_in, small_parts, small_across, packs, small_pack, send_sem, recv_sem,
    *, team, teams,
):
    row_count, width = x_own.shape
    window = xw.shape[0]
    extra = window - row_count
    half = window // 2
    pairs = width // LANES
    total = ids.shape[1]
    dp = lax.axis_index("dp")
    section = lax.axis_index("section")
    tensor = lax.axis_index("tensor")
    core = (dp, 1 - section, tensor)
    beside = (dp, section, 1 - tensor)

    spot = lax.rem(dp, team)
    this_team = dp // team

    def mate(k):
        place, bit = spot, 1
        while bit < team:
            if k & bit:
                place = jnp.where(lax.rem(spot // bit, 2) == 0, place + bit, place - bit)
            bit *= 2
        return (dp - spot + place, section, tensor), place

    def partner(k):
        return (lax.rem(dp + k * team, team * teams), section, tensor)

    blocks, _ = bands(window)
    row_blocks = window // LANES

    def at(start, size, step=LANES):
        return pl.ds(pl.multiple_of(start, step), size)

    def rows(i, n=LANES):
        return pl.ds(pl.multiple_of(i * n, n), n)

    def loop(n, body):
        def step(i, carry):
            body(i)
            return carry

        lax.fori_loop(0, n, step, 0)

    sent_off = {}

    def copy(key, source, dest, device):
        return pltpu.make_async_remote_copy(
            src_ref=source,
            dst_ref=dest,
            send_sem=send_sem.at[key],
            recv_sem=recv_sem.at[key],
            device_id=device,
            device_id_type=MESH,
        )

    def send(key, source, dest, device, like=None):
        copy(key, source, dest, device).start()
        sent_off[key] = source if like is None else like

    def arrived(key, dest):
        copy(key, dest, dest, core).wait_recv()

    barrier = pltpu.get_barrier_semaphore()
    neighbours = [core, beside] + [mate(k)[0] for k in range(1, team)] + [partner(k) for k in range(1, teams)]
    for device in neighbours:
        pl.semaphore_signal(barrier, inc=1, device_id=device, device_id_type=MESH)
    pl.semaphore_wait(barrier, len(neighbours))

    edge = x_own.at[at((1 - tensor) * (row_count - extra), extra)]
    send(0, edge, xw.at[at(tensor * row_count, extra)], beside)
    send(1, gains_own, gains.at[section], core)
    send(2, w_own, wc.at[0], core)

    @pl.when(section == 0)
    def _():
        send(3, w_own, wy, beside)

    def local(dest, source):
        dest[...] = source[...]

    local(xw.at[at(tensor * extra, row_count)], x_own)
    local(cw.at[at(tensor * extra, row_count)], c_own)
    local(mi.at[tensor], mi_own)
    local(mo.at[tensor], mo_own)
    local(gains.at[section], gains_own)

    ids_row = ids[pl.ds(section, 1), :].astype(F32)
    image = lax.broadcasted_iota(jnp.int32, (SLOTS, total), 0).astype(F32)
    spread = jnp.broadcast_to(ids_row, (SLOTS, total))
    middle = jnp.sum((spread < image).astype(F32) + (spread <= image).astype(F32), axis=1, keepdims=True)
    first_half = (middle < total).astype(F32)
    mine = jnp.where(tensor == 0, first_half, 1.0 - first_half)
    window_ids = ids[pl.ds(section, 1), at(tensor * (total - window), window)].astype(F32)
    member = (jnp.broadcast_to(window_ids, (SLOTS, window)) == image[:, :window]).astype(F32)
    member_own = member * mine
    own_row = jnp.sum(member_own, axis=0, keepdims=True)
    own[...] = jnp.broadcast_to(own_row, (LANES, window)).T
    ids_col = jnp.broadcast_to(window_ids, (LANES, window)).T
    for q0, k0, count, kept in blocks:
        same = ids_col[k0 : k0 + count] == jnp.broadcast_to(window_ids[:, q0 : q0 + LANES], (count, LANES))
        bias[kept : kept + count, :] = jnp.where(same, 0.0, -1e30)

    def place(source, b, t):
        for c in range(4):
            dest, base = (wqkv, c * width) if c < 3 else (wo, 0)
            first = c * 3 * HD
            dest[b, at(base + t * LANES, 2 * HD)] = source[first : first + 2 * HD]
            dest[b, at(base + 2 * LANES + t * HD, HD, HD)] = source[first + 2 * HD : first + 3 * HD]

    arrived(0, xw.at[at((1 - tensor) * row_count, extra)])
    arrived(1, gains.at[1 - section])
    arrived(2, wc.at[0])
    place(w_own, section, tensor)
    place(wc.at[0], 1 - section, tensor)

    @pl.when(section == 0)
    def _():
        arrived(3, wy)
        send(4, wy, wc.at[1], core)
        send(5, mi_own, mi.at[tensor], beside)
        place(wy, 0, 1 - tensor)

    @pl.when(section == 1)
    def _():
        send(5, mo_own, mo.at[tensor], beside)
        send(3, w_own, wy, beside)
        arrived(4, wc.at[1])
        place(wc.at[1], 0, 1 - tensor)

    c_edge = c_own.at[at((1 - tensor) * (row_count - extra), extra)]
    send(7, c_edge, cw.at[at(tensor * row_count, extra)], beside)
    send(8, router_own, routert.at[tensor], beside)

    class Sum:
        def __init__(self, key, core_in, beside_in, parts, across, total):
            self.key, self.core_in, self.beside_in = key, core_in, beside_in
            self.parts, self.across, self.total = parts, across, total
            self.size = parts.shape[1]
            self.like = parts.at[0]

        def part(self, place):
            return at(place * self.size, self.size, 16)

        def to_core(self, source):
            send(self.key, source, self.core_in, core, self.core_in)

        def to_beside(self, far):
            arrived(self.key, self.core_in)
            far[...] = (far[...].astype(F32) + self.core_in[1 - tensor].astype(F32)).astype(BF)
            send(self.key + 1, far, self.beside_in, beside, self.beside_in)

        def to_team(self, near):
            arrived(self.key + 1, self.beside_in)
            both = near[...].astype(F32) + self.core_in[tensor].astype(F32)
            near[...] = (both + self.beside_in[...].astype(F32)).astype(BF)
            for k in range(1, team):
                device, place = mate(k)
                send(self.key + 1 + k, near.at[self.part(place)], self.parts.at[k], device, self.like)

        def add_parts(self, near):
            whole = near[self.part(spot)].astype(F32)
            for k in range(1, team):
                arrived(self.key + 1 + k, self.parts.at[k])
                whole = whole + self.parts[k].astype(F32)
            piece = self.total.at[self.part(spot)]
            piece[...] = whole.astype(BF)
            first = self.key + 2 * team
            for k in range(1, teams):
                copy(first + team + k, piece, self.across.at[k], partner(k)).start()
            for k in range(1, teams):
                arrived(first + team + k, self.across.at[k])
                copy(first + team + k, piece, self.across.at[k], partner(k)).wait_send()
                whole = whole + self.across[k].astype(F32)
            if teams > 1:
                piece[...] = whole.astype(BF)
            for k in range(1, team):
                send(first + k, piece, piece, mate(k)[0], self.like)

        def finish(self):
            for k in range(1, team):
                arrived(self.key + 2 * team + k, self.total.at[self.part(mate(k)[1])])

        keys = 3 * team + teams

    key = 15
    attn = Sum(key, wc, wy, attn_parts, attn_across, attn_sum)
    key += Sum.keys
    mlp = Sum(key, mlp_core, mlp_beside, mlp_parts, mlp_across, mlp_sum.at[section])
    key += Sum.keys
    mlp_far, mlp_near = grad_mlp.at[section, 1 - tensor], grad_mlp.at[section, tensor]
    mlp_key, pack_key, small_key = key, key + 1, key + 1 + team + teams

    def attention(b, x_of, out_ref):
        def norm(i):
            unit, _ = normalise(x_of(rows(i)))
            z[2 * b, rows(i)] = (unit * gains[b, 0:1, :]).astype(BF)

        loop(row_blocks, norm)
        zz = z[2 * b]
        for c, dest in enumerate((qt.at[b], kt.at[b], vt)):
            tall = dot_t(wqkv[b, c * width : (c + 1) * width], zz)
            tall = (tall.astype(BF) * jnp.asarray(HD**-0.5 if c == 0 else 1.0, BF)).reshape(pairs, LANES, window)
            dest[...] = tall
        for c, dest in ((1, kr), (2, vr)):
            flat = dot_t(zz, wqkv[b, c * width : (c + 1) * width]).astype(BF)
            for j in range(pairs):
                dest[b, j] = flat[:, j * LANES : (j + 1) * LANES]

        def pair(j):
            for q0, k0, count, kept in blocks:
                scores = dot(kr[b, j, k0 : k0 + count, :], pair_up(qt[b, j, :, q0 : q0 + LANES]))
                veil = bias[kept : kept + count, :]
                scores = scores + jnp.concatenate([veil, veil], axis=1)
                powers = jnp.exp(scores - jnp.max(scores, axis=0, keepdims=True))
                probs = (powers * (1.0 / jnp.sum(powers, axis=0, keepdims=True))).astype(BF)
                pt[b, j, kept : kept + count, :] = probs
                ot[b, j, :, q0 : q0 + LANES] = pair_down(dot(vt[j, :, k0 : k0 + count], probs)).astype(BF)

        loop(pairs, pair)
        for j in range(pairs):
            tok[:, j * LANES : (j + 1) * LANES] = ot[b, j].T

        def out(i):
            out_ref[rows(i, half)] = x_of(rows(i, half)) + dot(tok[rows(i, half)], wo[b])

        loop(2, out)

    def attention_back(b, x_of, beside_pairs, beside_rest):
        ga = low[...]
        got[...] = dot_t(wo[b], ga).astype(BF).reshape(pairs, LANES, window)
        for j in range(pairs):
            piece = dot(ot[b, j], ga).astype(BF)
            put_grad(b, 3, j, piece)

        def pair(j):
            for at_pair, body in enumerate(beside_pairs):
                pl.when(j == at_pair)(body)
            gk_sum[...] = jnp.zeros_like(gk_sum)
            gv_sum[...] = jnp.zeros_like(gv_sum)
            for q0, k0, count, kept in blocks:
                go_pair = pair_up(got[j, :, q0 : q0 + LANES])
                q_pair = pair_up(qt[b, j, :, q0 : q0 + LANES])
                low_probs = pt[b, j, kept : kept + count, :]
                probs = low_probs.astype(F32)
                weighted = dot(vr[b, j, k0 : k0 + count, :], go_pair) * probs
                inner = jnp.sum(weighted, axis=0, keepdims=True)
                gs = (weighted - probs * inner).astype(BF)
                gq = pair_down(dot(kt[b, j, :, k0 : k0 + count], gs)) * HD**-0.5
                gt[pl.ds(pl.multiple_of(j * LANES, LANES), LANES), q0 : q0 + LANES] = gq.astype(BF)
                gk_sum[k0 : k0 + count] += dot_t(gs, q_pair)
                gv_sum[k0 : k0 + count] += dot_t(low_probs, go_pair)
            for c, total_of in ((1, gk_sum), (2, gv_sum)):
                gtok[c * pairs + j] = total_of[...].astype(BF)

        loop(pairs, pair)
        for j in range(pairs):
            gtok[j] = gt[j * LANES : (j + 1) * LANES].T
        for c in (1, 2):
            for j in range(pairs):
                first = (c * pairs + j) * LANES
                gt[first : first + LANES] = gtok[c * pairs + j].T
        zz = z[2 * b]
        for c in range(3):
            for j in range(pairs):
                first = (c * pairs + j) * LANES
                put_grad(b, c, j, dot(gt[first : first + LANES], zz).astype(BF))
        beside_rest()
        gain = gains[b, 0:1, :]
        gain_grad = jnp.zeros((1, width), F32)

        def back(i, gain_grad):
            wide = jnp.concatenate([gtok[c, rows(i, half)] for c in range(3 * pairs)], axis=1)
            step, part = norm_back(x_of(rows(i, half)), gain, dot(wide, wqkv[b]))
            gx[rows(i, half)] += step
            return gain_grad + part

        small[2 * b : 2 * b + 1, :] = lax.fori_loop(0, 2, back, gain_grad)

    def put_grad(b, c, j, piece):
        first = c * 3 * HD
        if j < 2:
            grad_attn[b, j, first : first + 2 * HD, :] = piece
        else:
            for t in range(2):
                grad_attn[b, t, first + 2 * HD : first + 3 * HD, :] = piece[t * HD : (t + 1) * HD]

    attention(0, lambda r: xw[r].astype(F32), x1)

    def norm_middle(source, which):
        def body(i):
            unit, _ = normalise(source[rows(i)])
            z[which, rows(i)] = (unit * gains[which // 2, 1:2, :]).astype(BF)

        loop(row_blocks, body)

    norm_middle(x1, 1)

    @pl.when(section == 0)
    def _():
        arrived(5, mi.at[1 - tensor])
        send(6, mi.at[1 - tensor], mi.at[1 - tensor], core, mi_own)
        arrived(6, mo.at[1 - tensor])

    @pl.when(section == 1)
    def _():
        arrived(5, mo.at[1 - tensor])
        send(6, mo.at[1 - tensor], mo.at[1 - tensor], core, mo_own)
        arrived(6, mi.at[1 - tensor])

    chunk = 256
    chunks = mi.shape[2] // chunk

    def hidden_chunk(i):
        part, first = i // chunks, pl.multiple_of(i % chunks * chunk, chunk)
        value, grad = gelu_parts(dot(z[1], mi[part, :, pl.ds(first, chunk)]))
        hidden[i] = value.astype(BF)
        slope[i] = grad.astype(BF)

    loop(2 * chunks, hidden_chunk)

    def dense_out(i):
        h = jnp.concatenate([hidden[c, rows(i, half)] for c in range(2 * chunks)], axis=1)
        sent[rows(i, half)] = (x1[rows(i, half)] + dot(h, mo[...].reshape(-1, width))).astype(BF)

    loop(2, dense_out)

    @pl.when(section == 0)
    def _():
        arrived(4, wc.at[1])
        place(wc.at[1], 1, 1 - tensor)

    @pl.when(section == 1)
    def _():
        arrived(3, wy)
        send(4, wy, wc.at[1], core)
        place(wy, 1, 1 - tensor)

    attention(1, lambda r: sent[r].astype(F32), x3)
    norm_middle(x3, 3)
    z3 = z[3]
    local(routert.at[tensor], router_own)
    arrived(8, routert.at[1 - tensor])
    powers = [jnp.exp(dot_t(routert[e], z3)[:1]) for e in range(2)]
    dispatch, combine = [], []
    for e in range(2):
        totals = jnp.sum(member * powers[e], axis=1, keepdims=True)
        dispatch.append(powers[e] / jnp.sum(member * totals, axis=0, keepdims=True))
        combine.append(powers[e] / (powers[0] + powers[1]))
        d_low = (member_own * dispatch[e].astype(BF).astype(F32)).astype(BF)
        c_low = (member * combine[e].astype(BF).astype(F32)).astype(BF)
        mixing[0, e * SLOTS : (e + 1) * SLOTS] = d_low
        mixing[1, e * SLOTS : (e + 1) * SLOTS] = c_low
        slots[e] = dot(d_low, z3).astype(BF)
    copy(4, wy, wc.at[1], core).wait_send()
    sent_off.pop(4)

    send(9, slots.at[1 - tensor], slot_in.at[0], beside)
    arrived(7, cw.at[at((1 - tensor) * row_count, extra)])

    def mask(i):
        wide = jnp.concatenate([own[rows(i)]] * pairs, axis=1)
        low[rows(i)] = jnp.where(wide > 0.0, cw[rows(i)].astype(F32), 0.0).astype(BF)

    loop(row_blocks, mask)
    gy = low[...]
    for e in range(2):
        geos[e] = dot(mixing[1, e * SLOTS : (e + 1) * SLOTS], gy).astype(BF)
    send(10, geos.at[1 - tensor], slot_in.at[1], beside)

    arrived(9, slot_in.at[0])
    pack[0] = slots[tensor] + slot_in[0]
    value, grad = gelu_parts(dot(pack[0], ei[...]))
    eslope[...] = grad
    eout[tensor] = dot(value.astype(BF), eo[...]).astype(BF)
    send(11, eout.at[tensor], eout.at[tensor], beside)
    arrived(10, slot_in.at[1])
    pack[1] = geos[tensor] + slot_in[1]
    g_hidden = dot_t(pack[1], eo[...])
    gslot[tensor] = dot_t((g_hidden * eslope[...]).astype(BF), ei[...]).astype(BF)
    send(12, gslot.at[tensor], gslot.at[tensor], beside)
    arrived(11, eout.at[1 - tensor])
    outputs = eout[...].reshape(2 * SLOTS, width)

    def finish(i):
        mixed = t_dot(mixing[1, :, rows(i)], outputs)
        act[rows(i)] = (x3[rows(i)] + mixed).astype(BF)

    loop(row_blocks, finish)
    send(13, act.at[at((1 - tensor) * row_count, extra)], edge_in.at[0], beside)

    def nothing():
        pass

    all_packs, team_like = packs.at[0], packs.at[0, 0]

    def share_slots():
        halves = [pack[n].astype(F32)[:IMAGES] for n in range(2)]
        small_pack[...] = jnp.concatenate(halves, axis=0).astype(BF)
        for k in range(1, team):
            send(pack_key + k, small_pack, packs.at[0, this_team, spot], mate(k)[0], small_pack)

    def gather_slots():
        for k in range(1, team):
            arrived(pack_key + k, packs.at[0, this_team, mate(k)[1]])
        packs[0, this_team, spot] = small_pack[...]
        for k in range(1, teams):
            team_packs = packs.at[0, this_team]
            send(pack_key + team + k, team_packs, team_packs, partner(k), team_like)
        for k in range(1, teams):
            arrived(pack_key + team + k, packs.at[0, lax.rem(this_team + k, teams)])
        send(pack_key, packs.at[0], packs.at[1], core, all_packs)

    per_token = [jnp.sum(dot_t(eout[e], gy) * member, axis=0, keepdims=True) for e in range(2)]
    inner = combine[0] * per_token[0] + combine[1] * per_token[1]
    arrived(12, gslot.at[1 - tensor])
    logit_grads = []
    for e in range(2):
        g_dispatch = jnp.sum(dot_t(gslot[e], z3) * member_own, axis=0, keepdims=True)
        weighted = dispatch[e] * g_dispatch
        sums = jnp.sum(member * weighted, axis=1, keepdims=True)
        from_dispatch = weighted - dispatch[e] * jnp.sum(member * sums, axis=0, keepdims=True)
        logit_grads.append(combine[e] * (per_token[e] - inner) + from_dispatch)
    which_row = lax.broadcasted_iota(jnp.int32, (SLOTS, width), 0)
    router_rows = jnp.where(
        which_row == 0,
        jnp.broadcast_to(routert[0].astype(F32)[:1], (SLOTS, width)),
        jnp.where(which_row == 1, jnp.broadcast_to(routert[1].astype(F32)[:1], (SLOTS, width)), 0.0),
    ).astype(BF)
    which = lax.broadcasted_iota(jnp.int32, (SLOTS, window), 0)
    logit_grad = jnp.where(which == 0, logit_grads[0], jnp.where(which == 1, logit_grads[1], 0.0)).astype(BF)
    small[4:6, :] = dot(logit_grad, z3)[:2]
    small[6:8, :] = jnp.zeros((2, width), F32)
    mixing[1, :SLOTS] = logit_grad
    slots_and_router = jnp.concatenate([gslot[0], gslot[1], router_rows], axis=0)

    def experts_back(i, gain_grad):
        at = pl.ds(pl.multiple_of(i * LANES, LANES), LANES)
        parts = jnp.concatenate([mixing[0, :, at], mixing[1, :SLOTS, at]], axis=0)
        step, part = norm_back(x3[rows(i)], gains[1, 1:2, :], t_dot(parts, slots_and_router))
        total_of = low[rows(i)].astype(F32) + step
        gx[rows(i)] = total_of
        low[rows(i)] = total_of.astype(BF)
        return gain_grad + part

    small[3:4, :] = lax.fori_loop(0, row_blocks, experts_back, jnp.zeros((1, width), F32))

    def share_second():
        @pl.when(section == 0)
        def _():
            attn.to_core(grad_attn.at[1])

    share_pack = [share_slots, gather_slots, nothing]
    attention_back(1, lambda r: sent[r].astype(F32), share_pack, share_second)

    low[...] = gx[...].astype(BF)
    gsent = low[...]
    gsent_t = gsent.T
    z2 = z[1]
    z2_t = z2.T

    def hidden_back(i):
        part, first = i // chunks, pl.multiple_of(i % chunks * chunk, chunk)
        lanes = pl.ds(first, chunk)
        grad_mlp[1, part, :, lanes] = dot(gsent_t, hidden[i]).astype(BF)
        g_hidden = dot_t(gsent, mo[part, pl.ds(first, chunk), :])
        g_pre = (g_hidden * slope[i].astype(F32)).astype(BF)
        hidden[i] = g_pre
        grad_mlp[0, part, :, lanes] = dot(z2_t, g_pre).astype(BF)

    @pl.when(section == 1)
    def _():
        attn.to_beside(grad_attn.at[1, 1 - tensor])

    loop(2 * chunks, hidden_back)
    mlp.to_core(grad_mlp.at[1 - section])

    @pl.when(section == 1)
    def _():
        attn.to_team(grad_attn.at[1, tensor])


    def dense_back(i, gain_grad):
        gz = jnp.zeros((half, width), F32)
        for part in range(2):
            g = jnp.concatenate([hidden[part * chunks + c, rows(i, half)] for c in range(chunks)], axis=1)
            gz = gz + dot_t(g, mi[part])
        step, part = norm_back(x1[rows(i, half)], gains[0, 1:2, :], gz)
        total_of = low[rows(i, half)].astype(F32) + step
        gx[rows(i, half)] = total_of
        low[rows(i, half)] = total_of.astype(BF)
        return gain_grad + part

    small[1:2, :] = lax.fori_loop(0, 2, dense_back, jnp.zeros((1, width), F32))

    def share_dense():
        mlp.to_beside(mlp_far)

    def reduce_second():
        @pl.when(section == 1)
        def _():
            attn.add_parts(grad_attn.at[1, tensor])

    def reduce_dense():
        mlp.to_team(mlp_near)

    def share_first():
        @pl.when(section == 1)
        def _():
            attn.to_core(grad_attn.at[0])

    attention_back(0, lambda r: xw[r].astype(F32), [share_dense, reduce_second, reduce_dense], share_first)
    low[...] = gx[...].astype(BF)
    send(14, low.at[at((1 - tensor) * row_count, extra)], edge_in.at[1], beside)
    send(small_key, small, small_in.at[0], core)

    @pl.when(section == 0)
    def _():
        attn.to_beside(grad_attn.at[0, 1 - tensor])

    arrived(small_key, small_in.at[0])
    small_in[1] = small[...] + small_in[0]
    send(small_key + 1, small_in.at[1], small_in.at[2], beside)
    mlp.add_parts(mlp_near)

    arrived(pack_key, packs.at[1])
    split_packs = packs[...].astype(F32).reshape(-1, 2, IMAGES, width)
    every_slot, every_grad = (split_packs[:, n].reshape(-1, width).astype(BF) for n in range(2))
    every_slot_t = every_slot.T

    few = chunk if teams == 1 else LANES

    def expert_grads(i):
        lanes = pl.ds(pl.multiple_of(i * few, few), few)
        value, grad = gelu_parts(dot(every_slot, ei[:, lanes]))
        g_pre = (dot_t(every_grad, eo[lanes, :]) * grad).astype(BF)
        expert_in_out[:, lanes] = dot(every_slot_t, g_pre).astype(BF)
        expert_out_out[lanes, :] = dot(value.astype(BF).T, every_grad).astype(BF)

    loop(2 * chunks * chunk // few, expert_grads)

    arrived(small_key + 1, small_in.at[2])
    small_parts[0] = small_in[1] + small_in[2]
    for k in range(1, team):
        send(small_key + 1 + k, small_parts.at[0], small_parts.at[k], mate(k)[0])

    @pl.when(section == 0)
    def _():
        attn.to_team(grad_attn.at[0, tensor])

    for n, (source, dest) in enumerate(((act, act_out), (low, pg_out))):
        dest[...] = source[at(tensor * extra, row_count)]
        arrived(13 + n, edge_in.at[n])
        near = at(row_count - extra - tensor * (row_count - 2 * extra), extra)
        wide = jnp.concatenate([own[near]] * pairs, axis=1)
        merged = jnp.where(wide > 0.0, source[near].astype(F32), edge_in[n].astype(F32)).astype(BF)
        dest[at((1 - tensor) * (row_count - extra), extra)] = merged

    @pl.when(section == 1)
    def _():
        attn.finish()

    mlp.finish()
    send(mlp_key, mlp_sum.at[section], mlp_sum.at[section], core, mlp_sum.at[0])

    for k in range(1, team):
        arrived(small_key + 1 + k, small_parts.at[k])
    small_across[0] = sum([small_parts[k] for k in range(1, team)], start=small_parts[0])
    for k in range(1, teams):
        send(small_key + 1 + team + k, small_across.at[0], small_across.at[k], partner(k))
    for k in range(1, teams):
        arrived(small_key + 1 + team + k, small_across.at[k])
    small_out[...] = sum([small_across[k] for k in range(1, teams)], start=small_across[0])

    @pl.when(section == 0)
    def _():
        attn.add_parts(grad_attn.at[0, tensor])
        attn.finish()

    arrived(mlp_key, mlp_sum.at[1 - section])
    attn_out[...] = attn_sum[...]
    mlp_out[...] = mlp_sum[...]

    for key, like in sent_off.items():
        copy(key, like, like, core).wait_send()


def compute(x_own, c_own, ids, gains, w_own, mi, mo, router, ei, eo):
    row_count, width = x_own.shape
    window = row_count + MOST // 2
    extra = window - row_count
    pairs = width // LANES
    ff = ei.shape[1]
    _, kept = bands(window)
    chunk_count = 2 * mi.shape[1] // 256
    vmem = pl.BlockSpec(memory_space=pltpu.VMEM)
    ranks = lax.axis_size("dp")
    team = min(8, ranks & -ranks)
    teams = ranks // team
    copies = 15 + 2 * (3 * team + teams) + 1 + team + teams + 1 + team + teams
    return pl.pallas_call(
        functools.partial(compute_kernel, team=team, teams=teams),
        out_shape=(
            jax.ShapeDtypeStruct((row_count, width), BF),
            jax.ShapeDtypeStruct((row_count, width), BF),
            jax.ShapeDtypeStruct((2 * width, width), BF),
            jax.ShapeDtypeStruct((2, width, ff // 2), BF),
            jax.ShapeDtypeStruct((width, ff), BF),
            jax.ShapeDtypeStruct((ff, width), BF),
            jax.ShapeDtypeStruct((8, width), F32),
        ),
        in_specs=[vmem] * 10,
        out_specs=[vmem] * 7,
        scratch_shapes=[
            pltpu.VMEM((window, width), BF),
            pltpu.VMEM((window, width), BF),
            pltpu.VMEM((2, 8, width), F32),
            pltpu.VMEM((2 * width, width), BF),
            pltpu.VMEM((2, 2 * width, width), BF),
            pltpu.VMEM((2, 3 * width, width), BF),
            pltpu.VMEM((2, width, width), BF),
            pltpu.VMEM((2, *mi.shape), BF),
            pltpu.VMEM((2, *mo.shape), BF),
            pltpu.VMEM((2, SLOTS, width), BF),
            pltpu.VMEM((window, width), BF),
            pltpu.VMEM((2, extra, width), BF),
            pltpu.VMEM((2, SLOTS, width), BF),
            pltpu.VMEM((2, SLOTS, width), BF),
            pltpu.VMEM((2, SLOTS, width), BF),
            pltpu.VMEM((2, SLOTS, width), BF),
            pltpu.VMEM((4, window, width), BF),
            pltpu.VMEM((window, width), F32),
            pltpu.VMEM((window, width), BF),
            pltpu.VMEM((window, width), F32),
            pltpu.VMEM((2, pairs, LANES, window), BF),
            pltpu.VMEM((2, pairs, LANES, window), BF),
            pltpu.VMEM((pairs, LANES, window), BF),
            pltpu.VMEM((2, pairs, window, LANES), BF),
            pltpu.VMEM((2, pairs, window, LANES), BF),
            pltpu.VMEM((2, pairs, LANES, window), BF),
            pltpu.VMEM((2, pairs, kept, 2 * LANES), BF),
            pltpu.VMEM((window, width), BF),
            pltpu.VMEM((chunk_count, window, 256), BF),
            pltpu.VMEM((chunk_count, window, 256), BF),
            pltpu.VMEM((window, width), F32),
            pltpu.VMEM((window, width), BF),
            pltpu.VMEM((pairs, LANES, window), BF),
            pltpu.VMEM((3 * width, window), BF),
            pltpu.VMEM((3 * pairs, window, LANES), BF),
            pltpu.VMEM((window, LANES), F32),
            pltpu.VMEM((window, LANES), F32),
            pltpu.VMEM((kept, LANES), F32),
            pltpu.VMEM((window, LANES), F32),
            pltpu.VMEM((2, 2 * SLOTS, window), BF),
            pltpu.VMEM((SLOTS, ff), F32),
            pltpu.VMEM((2, SLOTS, width), BF),
            pltpu.VMEM((2, SLOTS, width), BF),
            pltpu.VMEM((2, 2, 2 * width, width), BF),
            pltpu.VMEM((team, 2 * width // team, width), BF),
            pltpu.VMEM((teams, 2 * width // team, width), BF),
            pltpu.VMEM((2 * width, width), BF),
            pltpu.VMEM((2, 2, width, ff // 2), BF),
            pltpu.VMEM((2, width, ff // 2), BF),
            pltpu.VMEM((width, ff // 2), BF),
            pltpu.VMEM((team, width // team, ff // 2), BF),
            pltpu.VMEM((teams, width // team, ff // 2), BF),
            pltpu.VMEM((2, width, ff // 2), BF),
            pltpu.VMEM((8, width), F32),
            pltpu.VMEM((3, 8, width), F32),
            pltpu.VMEM((team, 8, width), F32),
            pltpu.VMEM((teams, 8, width), F32),
            pltpu.VMEM((2, teams, team, 2 * IMAGES, width), BF),
            pltpu.VMEM((2 * IMAGES, width), BF),
            pltpu.SemaphoreType.DMA((copies,)),
            pltpu.SemaphoreType.DMA((copies,)),
        ],
        compiler_params=pltpu.CompilerParams(
            vmem_limit_bytes=60 * 1024 * 1024, collective_id=0, has_side_effects=True
        ),
    )(x_own, c_own, ids, gains, w_own, mi, mo, router, ei, eo)


def per_device(
    patches, image_ids, cotangent, norm_gains, qkv_weight, out_weight, mlp_in, mlp_out, router, expert_in, expert_out
):
    width = patches.shape[2]
    tensor = lax.axis_index("tensor")
    heads = qkv_weight.shape[3] // HD
    w_own = jnp.concatenate([jnp.transpose(qkv_weight[0], (1, 2, 0)).reshape(-1, width), out_weight[0]], axis=0)
    gains = jnp.pad(norm_gains[0], ((0, 6), (0, 0)))
    router_own = jnp.pad(router.T, ((0, SLOTS - router.shape[1]), (0, 0)))
    activations, patch_grad, attn, mlp, expert_in_grad, expert_out_grad, small = compute(
        patches[0], cotangent[0], image_ids, gains, w_own, mlp_in, mlp_out, router_own, expert_in[0], expert_out[0]
    )
    rows = 3 * heads * HD
    qkv_grad = jnp.transpose(attn[:rows].astype(F32).reshape(3, heads * HD, width), (2, 0, 1))
    gains_grad = lax.dynamic_slice_in_dim(small, 2 * lax.axis_index("section"), 2, 0)
    router_grad = lax.dynamic_slice_in_dim(small, 4 + tensor, 1, 0).T
    return (
        activations[None],
        patch_grad[None],
        gains_grad[None],
        qkv_grad[None],
        attn[rows:].astype(F32)[None],
        mlp[0].astype(F32),
        mlp[1].astype(F32).T,
        router_grad,
        expert_in_grad.astype(F32)[None],
        expert_out_grad.astype(F32)[None],
    )


def solution(mesh):
    return jax.shard_map(
        per_device,
        mesh=mesh,
        in_specs=(
            P(("dp", "section"), "tensor", None),
            P("dp", None),
            P(("dp", "section"), "tensor", None),
            P("section", None, None),
            P("section", None, None, "tensor"),
            P("section", "tensor", None),
            P(None, "tensor"),
            P("tensor", None),
            P(None, "tensor"),
            P("tensor", None, None),
            P("tensor", None, None),
        ),
        out_specs=(
            P(("dp", "section"), "tensor", None),
            P(("dp", "section"), "tensor", None),
            P("section", None, None),
            P("section", None, None, "tensor"),
            P("section", "tensor", None),
            P(None, "tensor"),
            P("tensor", None),
            P(None, "tensor"),
            P("tensor", None, None),
            P("tensor", None, None),
        ),
        check_vma=False,
    )
```

```python
import functools

import jax
import jax.numpy as jnp
from jax import lax
from jax.experimental import pallas as pl
from jax.experimental.pallas import tpu as pltpu
from jax.sharding import PartitionSpec as P

HD = 64
IMAGES = 8
MOST = 256
LANES = 128
SLOTS = 16
EPSILON = 1e-06
BF = jnp.bfloat16
F32 = jnp.float32


def dot(a, b):
    return jnp.dot(a, b, preferred_element_type=F32)


def dot_t(a, b):
    return lax.dot_general(a, b, (((1,), (1,)), ((), ())), preferred_element_type=F32)


def t_dot(a, b):
    return lax.dot_general(a, b, (((0,), (0,)), ((), ())), preferred_element_type=F32)


def normalise(x):
    centred = x - jnp.mean(x, axis=-1, keepdims=True)
    scale = lax.rsqrt(jnp.mean(centred * centred, axis=-1, keepdims=True) + EPSILON)
    return centred * scale, scale


def norm_back(x, gain, gz):
    unit, scale = normalise(x)
    scaled = gz * gain
    mean_plain = jnp.mean(scaled, axis=-1, keepdims=True)
    mean_unit = jnp.mean(scaled * unit, axis=-1, keepdims=True)
    return scale * (scaled - mean_plain - unit * mean_unit), jnp.sum(gz * unit, axis=0, keepdims=True)


def gelu_parts(u):
    cdf = 0.5 * (1.0 + lax.erf(u * 0.7071067811865476))
    return u * cdf, cdf + u * (0.3989422804014327 * jnp.exp(-0.5 * u * u))


def pair_up(tile):
    row = lax.broadcasted_iota(jnp.int32, tile.shape, 0)
    zero = jnp.zeros_like(tile)
    return jnp.concatenate([jnp.where(row < HD, tile, zero), jnp.where(row >= HD, tile, zero)], axis=1)


def pair_down(both):
    n = both.shape[1] // 2
    row = lax.broadcasted_iota(jnp.int32, (both.shape[0], n), 0)
    return jnp.where(row < HD, both[:, :n], both[:, n:])


def bands(window):
    reach = MOST // LANES
    found, at = [], 0
    for i in range(window // LANES):
        first = max(0, i - reach) * LANES
        count = min(window, (i + reach + 1) * LANES) - first
        found.append((i * LANES, first, count, at))
        at += count
    return found, at


MESH = pl.DeviceIdType.MESH


def compute_kernel(
    x_own, c_own, ids, gains_own, qkv_own, out_own, mi_own, mo_own, router_own, ei, eo,
    act_out, pg_out, qkv_out, attn_out, mi_out, mot_out, expert_in_out, expert_out_out, small_out,
    xw, cw, gains, wy, wc, w_own, wqkv, wo, mi, mo, routert, act, edge_in, slots, geos, slot_in, pack,
    z, x1, sent, x3, qt, kt, vt, kr, vr, ot, pt, tok, hidden, slope, gx, low, got, gt, gtok, gk_sum, gv_sum,
    bias, own, mixing, eslope, eout, gslot, grad_attn, attn_sum, grad_mlp, mlp_core, mlp_sum,
    small, small_in, small_parts, small_across, packs, small_pack, send_sem, recv_sem,
    *boxes, team, teams, mlp_orders, attn_orders,
):
    row_count, width = x_own.shape
    window = xw.shape[0]
    extra = window - row_count
    half = window // 2
    pairs = width // LANES
    total = ids.shape[1]
    dp = lax.axis_index("dp")
    section = lax.axis_index("section")
    tensor = lax.axis_index("tensor")
    core = (dp, 1 - section, tensor)
    beside = (dp, section, 1 - tensor)

    spot = lax.rem(dp, team)
    this_team = dp // team

    def mate(k):
        place, bit = spot, 1
        while bit < team:
            if k & bit:
                place = jnp.where(lax.rem(spot // bit, 2) == 0, place + bit, place - bit)
            bit *= 2
        return (dp - spot + place, section, tensor), place

    def partner(k):
        return (lax.rem(dp + k * team, team * teams), section, tensor)

    blocks, _ = bands(window)
    row_blocks = window // LANES

    def at(start, size, step=LANES):
        return pl.ds(pl.multiple_of(start, step), size)

    def rows(i, n=LANES):
        return pl.ds(pl.multiple_of(i * n, n), n)

    def loop(n, body):
        def step(i, carry):
            body(i)
            return carry

        lax.fori_loop(0, n, step, 0)

    sent_off = {}

    def copy(key, source, dest, device):
        return pltpu.make_async_remote_copy(
            src_ref=source,
            dst_ref=dest,
            send_sem=send_sem.at[key],
            recv_sem=recv_sem.at[key],
            device_id=device,
            device_id_type=MESH,
        )

    def send(key, source, dest, device, like=None):
        copy(key, source, dest, device).start()
        sent_off[key] = source if like is None else like

    def arrived(key, dest):
        copy(key, dest, dest, core).wait_recv()

    def only(which):
        return pl.when(section == which)

    barrier = pltpu.get_barrier_semaphore()
    neighbours = [core, beside] + [mate(k)[0] for k in range(1, team)] + [partner(k) for k in range(1, teams)]
    for device in neighbours:
        pl.semaphore_signal(barrier, inc=1, device_id=device, device_id_type=MESH)
    pl.semaphore_wait(barrier, len(neighbours))

    edge = x_own.at[at((1 - tensor) * (row_count - extra), extra)]
    send(0, edge, xw.at[at(tensor * row_count, extra)], beside)
    gains[section, :2] = gains_own[...]
    send(1, gains.at[section], gains.at[section], core)
    w_own[: qkv_own.shape[0]] = qkv_own[...]
    w_own[qkv_own.shape[0] :] = out_own[...]
    send(2, w_own, wc.at[0], core)

    @only(0)
    def _():
        send(3, w_own, wy, beside)

    def local(dest, source):
        dest[...] = source[...]

    local(xw.at[at(tensor * extra, row_count)], x_own)
    local(cw.at[at(tensor * extra, row_count)], c_own)
    local(mi.at[tensor], mi_own)
    local(mo.at[tensor], mo_own)
    first_row = lax.broadcasted_iota(jnp.int32, (SLOTS, width), 0) == 0
    router_rows = jnp.broadcast_to(router_own[...].astype(F32), (SLOTS, width))
    routert[tensor] = jnp.where(first_row, router_rows, 0.0).astype(BF)

    ids_row = ids[pl.ds(section, 1), :].astype(F32)
    image = lax.broadcasted_iota(jnp.int32, (SLOTS, total), 0).astype(F32)
    spread = jnp.broadcast_to(ids_row, (SLOTS, total))
    middle = jnp.sum((spread < image).astype(F32) + (spread <= image).astype(F32), axis=1, keepdims=True)
    first_half = (middle < total).astype(F32)
    mine = jnp.where(tensor == 0, first_half, 1.0 - first_half)
    window_ids = ids[pl.ds(section, 1), at(tensor * (total - window), window)].astype(F32)
    member = (jnp.broadcast_to(window_ids, (SLOTS, window)) == image[:, :window]).astype(F32)
    member_own = member * mine
    own_row = jnp.sum(member_own, axis=0, keepdims=True)
    own[...] = jnp.broadcast_to(own_row, (LANES, window)).T
    ids_col = jnp.broadcast_to(window_ids, (LANES, window)).T
    for q0, k0, count, kept in blocks:
        same = ids_col[k0 : k0 + count] == jnp.broadcast_to(window_ids[:, q0 : q0 + LANES], (count, LANES))
        bias[kept : kept + count, :] = jnp.where(same, 0.0, -1e30)

    def place(source, b, t):
        for c in range(4):
            dest, base = (wqkv, c * width) if c < 3 else (wo, 0)
            first = c * 3 * HD
            dest[b, at(base + t * LANES, 2 * HD)] = source[first : first + 2 * HD]
            dest[b, at(base + 2 * LANES + t * HD, HD, HD)] = source[first + 2 * HD : first + 3 * HD]

    arrived(0, xw.at[at((1 - tensor) * row_count, extra)])
    arrived(1, gains.at[1 - section])
    arrived(2, wc.at[0])
    place(w_own, section, tensor)
    place(wc.at[0], 1 - section, tensor)

    @only(0)
    def _():
        arrived(3, wy)
        send(4, wy, wc.at[1], core)
        send(5, mi_own, mi.at[tensor], beside)
        place(wy, 0, 1 - tensor)

    @only(1)
    def _():
        send(5, mo_own, mo.at[tensor], beside)
        send(3, w_own, wy, beside)
        arrived(4, wc.at[1])
        place(wc.at[1], 0, 1 - tensor)

    c_edge = c_own.at[at((1 - tensor) * (row_count - extra), extra)]
    send(7, c_edge, cw.at[at(tensor * row_count, extra)], beside)
    send(8, routert.at[tensor], routert.at[tensor], beside)

    class Cube:
        def __init__(self, key, pick, core_in, total, order, boxes):
            self.key, self.pick, self.core_in, self.total, self.order = key, pick, core_in, total, order
            self.boxes, self.across = boxes[:-1], boxes[-1]
            start, size, self.plan = 0, total.shape[0], []
            for dim in order:
                if dim == "tensor":
                    self.plan.append((dim, start, size, start))
                else:
                    size //= 2
                    bit = lax.rem(spot // dim, 2)
                    self.plan.append((dim, start + bit * size, size, start + (1 - bit) * size))
                    start = start + bit * size
            self.back = [(i, *step) for i, step in enumerate(self.plan) if step[0] != "tensor"][::-1]
            self.like = {size: total.at[:size] for _, _, _, size, _ in self.back}
            self.along = order.index("tensor")

        def to_core(self, source):
            send(self.key, source, self.core_in, core, self.core_in)

        def add(self, parts, start, size, box):
            for n, part in enumerate(parts):
                kept = self.pick(part, at(start, size, 16))
                kept[...] = (kept[...].astype(F32) + box[n].astype(F32)).astype(BF)

        def stage(self, k):
            steps, rounds = len(self.plan), len(self.back)
            both = (0, 1)
            if k == 0:
                arrived(self.key, self.core_in)
                self.add(both, 0, self.total.shape[0], self.core_in)
            elif k <= steps:
                _, start, size, _ = self.plan[k - 1]
                arrived(self.key + k, self.boxes[k - 1])
                self.add((tensor,) if self.along < k else both, start, size, self.boxes[k - 1])
            else:
                _, _, _, size, start = self.back[k - steps - 1]
                arrived(self.key + k, self.total.at[at(start, size, 16)])
            if k < steps:
                dim, _, size, start = self.plan[k]
                if dim == "tensor":
                    device = beside
                    source = self.pick(pl.ds(1 - tensor, 1), at(start, size, 16))
                else:
                    device = mate(dim)[0]
                    parts = pl.ds(tensor, 1) if self.along < k else slice(None)
                    source = self.pick(parts, at(start, size, 16))
                send(self.key + k + 1, source, self.boxes[k], device, self.boxes[k])
            elif k == steps:
                _, start, size, _ = self.plan[-1]
                piece = self.total.at[at(start, size, 16)]
                piece[...] = self.pick(tensor, at(start, size, 16))[...]
                self.exchange_across(piece)
            if steps <= k < steps + rounds:
                _, dim, start, size, _ = self.back[k - steps]
                region = self.total.at[at(start, size, 16)]
                send(self.key + k + 1, region, region, mate(dim)[0], self.like[size])

        def exchange_across(self, piece):
            if teams == 1:
                return
            first = self.key + Cube.stages
            for k in range(1, teams):
                copy(first + k, piece, self.across.at[k], partner(k)).start()
            whole = piece[...].astype(F32)
            for k in range(1, teams):
                arrived(first + k, self.across.at[k])
                copy(first + k, piece, self.across.at[k], partner(k)).wait_send()
                whole = whole + self.across[k].astype(F32)
            piece[...] = whole.astype(BF)

        stages = len(attn_orders[0]) * 2
        keys = stages + teams

    chunks = len(mlp_orders)
    key, taken = 15, 0

    def boxes_of(order):
        nonlocal taken
        found = boxes[taken : taken + len(order) + 1]
        taken += len(order) + 1
        return found

    def mlp_pick(q):
        return lambda parts, where: grad_mlp.at[section, parts, q, where]

    def attn_pick(n):
        return lambda parts, where: grad_attn.at[section, parts, n, where]

    dense, attn = [], []
    for q in range(chunks):
        total_of = mlp_sum.at[section, q]
        dense.append(Cube(key, mlp_pick(q), mlp_core.at[q], total_of, mlp_orders[q], boxes_of(mlp_orders[q])))
        key += Cube.keys
    for n in range(2):
        heard = wc.at[:, n * width : (n + 1) * width]
        attn.append(Cube(key, attn_pick(n), heard, attn_sum.at[n], attn_orders[n], boxes_of(attn_orders[n])))
        key += Cube.keys
    mlp_key, pack_key, small_key = key, key + 1, key + 1 + team + teams
    mlp_like = mlp_sum.at[0]

    def give_attn(b, n):
        @only(1 - b)
        def _():
            attn[n].to_core(grad_attn.at[b, :, n])

    def attn_stage(b, n, k):
        @only(b)
        def _():
            attn[n].stage(k)

    def give_dense(q):
        dense[q].to_core(grad_mlp.at[1 - section, :, q])

    def attention(b, x_of, out_ref):
        def norm(i):
            unit, _ = normalise(x_of(rows(i)))
            z[2 * b, rows(i)] = (unit * gains[b, 0:1, :]).astype(BF)

        loop(row_blocks, norm)
        zz = z[2 * b]
        for c, dest in enumerate((qt.at[b], kt.at[b], vt)):
            tall = dot_t(wqkv[b, c * width : (c + 1) * width], zz)
            tall = (tall.astype(BF) * jnp.asarray(HD**-0.5 if c == 0 else 1.0, BF)).reshape(pairs, LANES, window)
            dest[...] = tall
        for c, dest in ((1, kr), (2, vr)):
            flat = dot_t(zz, wqkv[b, c * width : (c + 1) * width]).astype(BF)
            for j in range(pairs):
                dest[b, j] = flat[:, j * LANES : (j + 1) * LANES]

        def pair(j):
            for q0, k0, count, kept in blocks:
                scores = dot(kr[b, j, k0 : k0 + count, :], pair_up(qt[b, j, :, q0 : q0 + LANES]))
                veil = bias[kept : kept + count, :]
                scores = scores + jnp.concatenate([veil, veil], axis=1)
                powers = jnp.exp(scores - jnp.max(scores, axis=0, keepdims=True))
                probs = (powers * (1.0 / jnp.sum(powers, axis=0, keepdims=True))).astype(BF)
                pt[b, j, kept : kept + count, :] = probs
                ot[b, j, :, q0 : q0 + LANES] = pair_down(dot(vt[j, :, k0 : k0 + count], probs)).astype(BF)

        loop(pairs, pair)
        for j in range(pairs):
            tok[:, j * LANES : (j + 1) * LANES] = ot[b, j].T

        def out(i):
            out_ref[rows(i, half)] = x_of(rows(i, half)) + dot(tok[rows(i, half)], wo[b])

        loop(2, out)

    def attention_back(b, x_of, beside_pairs, after_pairs):
        ga = low[...]
        got[...] = dot_t(wo[b], ga).astype(BF).reshape(pairs, LANES, window)
        for j in range(pairs):
            piece = dot(ot[b, j], ga).astype(BF)
            if j < 2:
                grad_attn[b, j, 1, 3 * HD : 5 * HD, :] = piece
            else:
                for t in range(2):
                    grad_attn[b, t, 1, 5 * HD : 6 * HD, :] = piece[t * HD : (t + 1) * HD]
        zz = z[2 * b]

        def pair(j):
            for at_pair, body in enumerate(beside_pairs):
                pl.when(j == at_pair)(body)
            gk_sum[...] = jnp.zeros_like(gk_sum)
            gv_sum[...] = jnp.zeros_like(gv_sum)
            for q0, k0, count, kept in blocks:
                go_pair = pair_up(got[j, :, q0 : q0 + LANES])
                q_pair = pair_up(qt[b, j, :, q0 : q0 + LANES])
                low_probs = pt[b, j, kept : kept + count, :]
                probs = low_probs.astype(F32)
                weighted = dot(vr[b, j, k0 : k0 + count, :], go_pair) * probs
                inner = jnp.sum(weighted, axis=0, keepdims=True)
                gs = (weighted - probs * inner).astype(BF)
                gq = pair_down(dot(kt[b, j, :, k0 : k0 + count], gs)) * HD**-0.5
                gt[:LANES, q0 : q0 + LANES] = gq.astype(BF)
                gk_sum[k0 : k0 + count] += dot_t(gs, q_pair)
                gv_sum[k0 : k0 + count] += dot_t(low_probs, go_pair)
            gtok[j] = gt[:LANES].T
            for c, total_of in ((1, gk_sum), (2, gv_sum)):
                low_sum = total_of[...].astype(BF)
                gtok[c * pairs + j] = low_sum
                gt[c * LANES : (c + 1) * LANES] = low_sum.T
            pieces = [dot(gt[c * LANES : (c + 1) * LANES], zz).astype(BF) for c in range(3)]

            @pl.when(j < 2)
            def _():
                for c in range(3):
                    grad_attn[b, j, 0, c * LANES : (c + 1) * LANES, :] = pieces[c]

            @pl.when(j == 2)
            def _():
                for c in range(3):
                    for t in range(2):
                        grad_attn[b, t, 1, c * HD : (c + 1) * HD, :] = pieces[c][t * HD : (t + 1) * HD]

        loop(pairs, pair)
        after_pairs()
        gain = gains[b, 0:1, :]

        def back(i, gain_grad):
            wide = jnp.concatenate([gtok[c, rows(i, half)] for c in range(3 * pairs)], axis=1)
            step, part = norm_back(x_of(rows(i, half)), gain, dot(wide, wqkv[b]))
            gx[rows(i, half)] += step
            return gain_grad + part

        small[2 * b : 2 * b + 1, :] = lax.fori_loop(0, 2, back, jnp.zeros((1, width), F32))

    attention(0, lambda r: xw[r].astype(F32), x1)

    def norm_middle(source, which):
        def body(i):
            unit, _ = normalise(source[rows(i)])
            z[which, rows(i)] = (unit * gains[which // 2, 1:2, :]).astype(BF)

        loop(row_blocks, body)

    norm_middle(x1, 1)

    @only(0)
    def _():
        arrived(5, mi.at[1 - tensor])
        send(6, mi.at[1 - tensor], mi.at[1 - tensor], core, mi_own)
        arrived(6, mo.at[1 - tensor])

    @only(1)
    def _():
        arrived(5, mo.at[1 - tensor])
        send(6, mo.at[1 - tensor], mo.at[1 - tensor], core, mo_own)
        arrived(6, mi.at[1 - tensor])

    chunk = 256

    def hidden_chunk(i):
        part, first = i // chunks, pl.multiple_of(i % chunks * chunk, chunk)
        value, grad = gelu_parts(dot(z[1], mi[part, :, pl.ds(first, chunk)]))
        hidden[i] = value.astype(BF)
        slope[i] = grad.astype(BF)

    loop(2 * chunks, hidden_chunk)

    def dense_out(i):
        h = jnp.concatenate([hidden[c, rows(i, half)] for c in range(2 * chunks)], axis=1)
        sent[rows(i, half)] = (x1[rows(i, half)] + dot(h, mo[...].reshape(-1, width))).astype(BF)

    loop(2, dense_out)

    @only(0)
    def _():
        arrived(4, wc.at[1])
        place(wc.at[1], 1, 1 - tensor)

    @only(1)
    def _():
        arrived(3, wy)
        send(4, wy, wc.at[1], core)
        place(wy, 1, 1 - tensor)

    attention(1, lambda r: sent[r].astype(F32), x3)
    norm_middle(x3, 3)
    z3 = z[3]
    arrived(8, routert.at[1 - tensor])
    powers = [jnp.exp(dot_t(routert[e], z3)[:1]) for e in range(2)]
    dispatch, combine = [], []
    for e in range(2):
        totals = jnp.sum(member * powers[e], axis=1, keepdims=True)
        dispatch.append(powers[e] / jnp.sum(member * totals, axis=0, keepdims=True))
        combine.append(powers[e] / (powers[0] + powers[1]))
        d_low = (member_own * dispatch[e].astype(BF).astype(F32)).astype(BF)
        c_low = (member * combine[e].astype(BF).astype(F32)).astype(BF)
        mixing[0, e * SLOTS : (e + 1) * SLOTS] = d_low
        mixing[1, e * SLOTS : (e + 1) * SLOTS] = c_low
        slots[e] = dot(d_low, z3).astype(BF)
    send(9, slots.at[1 - tensor], slot_in.at[0], beside)
    arrived(7, cw.at[at((1 - tensor) * row_count, extra)])

    def mask(i):
        wide = jnp.concatenate([own[rows(i)]] * pairs, axis=1)
        low[rows(i)] = jnp.where(wide > 0.0, cw[rows(i)].astype(F32), 0.0).astype(BF)

    loop(row_blocks, mask)
    gy = low[...]
    for e in range(2):
        geos[e] = dot(mixing[1, e * SLOTS : (e + 1) * SLOTS], gy).astype(BF)
    send(10, geos.at[1 - tensor], slot_in.at[1], beside)

    arrived(9, slot_in.at[0])
    pack[0] = slots[tensor] + slot_in[0]
    value, grad = gelu_parts(dot(pack[0], ei[...]))
    eslope[...] = grad
    eout[tensor] = dot(value.astype(BF), eo[...]).astype(BF)
    send(11, eout.at[tensor], eout.at[tensor], beside)
    arrived(10, slot_in.at[1])
    pack[1] = geos[tensor] + slot_in[1]
    g_hidden = dot_t(pack[1], eo[...])
    gslot[tensor] = dot_t((g_hidden * eslope[...]).astype(BF), ei[...]).astype(BF)
    send(12, gslot.at[tensor], gslot.at[tensor], beside)
    arrived(11, eout.at[1 - tensor])
    outputs = eout[...].reshape(2 * SLOTS, width)

    def finish(i):
        mixed = t_dot(mixing[1, :, rows(i)], outputs)
        act[rows(i)] = (x3[rows(i)] + mixed).astype(BF)

    loop(row_blocks, finish)
    send(13, act.at[at((1 - tensor) * row_count, extra)], edge_in.at[0], beside)

    def nothing():
        pass

    all_packs, team_like = packs.at[0], packs.at[0, 0]

    def share_slots():
        halves = [pack[n].astype(F32)[:IMAGES] for n in range(2)]
        small_pack[...] = jnp.concatenate(halves, axis=0).astype(BF)
        for k in range(1, team):
            send(pack_key + k, small_pack, packs.at[0, this_team, spot], mate(k)[0], small_pack)

    def gather_slots():
        for k in range(1, team):
            arrived(pack_key + k, packs.at[0, this_team, mate(k)[1]])
        packs[0, this_team, spot] = small_pack[...]
        for k in range(1, teams):
            team_packs = packs.at[0, this_team]
            send(pack_key + team + k, team_packs, team_packs, partner(k), team_like)
        for k in range(1, teams):
            arrived(pack_key + team + k, packs.at[0, lax.rem(this_team + k, teams)])
        send(pack_key, packs.at[0], packs.at[1], core, all_packs)

    per_token = [jnp.sum(dot_t(eout[e], gy) * member, axis=0, keepdims=True) for e in range(2)]
    inner = combine[0] * per_token[0] + combine[1] * per_token[1]
    arrived(12, gslot.at[1 - tensor])
    logit_grads = []
    for e in range(2):
        g_dispatch = jnp.sum(dot_t(gslot[e], z3) * member_own, axis=0, keepdims=True)
        weighted = dispatch[e] * g_dispatch
        sums = jnp.sum(member * weighted, axis=1, keepdims=True)
        from_dispatch = weighted - dispatch[e] * jnp.sum(member * sums, axis=0, keepdims=True)
        logit_grads.append(combine[e] * (per_token[e] - inner) + from_dispatch)
    which_row = lax.broadcasted_iota(jnp.int32, (SLOTS, width), 0)
    router_rows = jnp.where(
        which_row == 0,
        jnp.broadcast_to(routert[0].astype(F32)[:1], (SLOTS, width)),
        jnp.where(which_row == 1, jnp.broadcast_to(routert[1].astype(F32)[:1], (SLOTS, width)), 0.0),
    ).astype(BF)
    which = lax.broadcasted_iota(jnp.int32, (SLOTS, window), 0)
    logit_grad = jnp.where(which == 0, logit_grads[0], jnp.where(which == 1, logit_grads[1], 0.0)).astype(BF)
    small[4:6, :] = dot(logit_grad, z3)[:2]
    small[6:8, :] = jnp.zeros((2, width), F32)
    mixing[1, :SLOTS] = logit_grad
    slots_and_router = jnp.concatenate([gslot[0], gslot[1], router_rows], axis=0)

    def experts_back(i, gain_grad):
        at = pl.ds(pl.multiple_of(i * LANES, LANES), LANES)
        parts = jnp.concatenate([mixing[0, :, at], mixing[1, :SLOTS, at]], axis=0)
        step, part = norm_back(x3[rows(i)], gains[1, 1:2, :], t_dot(parts, slots_and_router))
        total_of = low[rows(i)].astype(F32) + step
        gx[rows(i)] = total_of
        low[rows(i)] = total_of.astype(BF)
        return gain_grad + part

    small[3:4, :] = lax.fori_loop(0, row_blocks, experts_back, jnp.zeros((1, width), F32))

    def shares_second():
        gather_slots()
        give_attn(1, 0)

    share_slots()
    attention_back(1, lambda r: sent[r].astype(F32), [nothing, nothing, shares_second], lambda: give_attn(1, 1))

    low[...] = gx[...].astype(BF)
    gsent = low[...]
    gsent_t = gsent.T
    z2 = z[1]
    z2_t = z2.T

    def hidden_back(n):
        for ahead, body in ((2, dense_first), (4, dense_second)):
            pl.when(n == ahead)(body)
        q, part = n // 2, lax.rem(n, 2)
        i, first = part * chunks + q, pl.multiple_of(q * chunk, chunk)
        grad_mlp[1, part, q] = dot(gsent_t, hidden[i]).astype(BF)
        g_hidden = dot_t(gsent, mo[part, pl.ds(first, chunk), :])
        g_pre = (g_hidden * slope[i].astype(F32)).astype(BF)
        hidden[i] = g_pre
        grad_mlp[0, part, q] = dot(z2_t, g_pre).astype(BF)

    def dense_first():
        give_dense(0)
        attn_stage(1, 0, 0)

    def dense_second():
        give_dense(1)
        attn_stage(1, 1, 0)
        dense[0].stage(0)

    loop(2 * chunks, hidden_back)
    give_dense(2)
    dense[1].stage(0)

    def dense_back(i, gain_grad):
        gz = jnp.zeros((half, width), F32)
        for part in range(2):
            g = jnp.concatenate([hidden[part * chunks + c, rows(i, half)] for c in range(chunks)], axis=1)
            gz = gz + dot_t(g, mi[part])
        step, part = norm_back(x1[rows(i, half)], gains[0, 1:2, :], gz)
        total_of = low[rows(i, half)].astype(F32) + step
        gx[rows(i, half)] = total_of
        low[rows(i, half)] = total_of.astype(BF)
        return gain_grad + part

    small[1:2, :] = lax.fori_loop(0, 2, dense_back, jnp.zeros((1, width), F32))

    def beside_first():
        dense[2].stage(0)
        dense[0].stage(1)
        attn_stage(1, 0, 1)

    def beside_second():
        dense[1].stage(1)
        dense[0].stage(2)
        attn_stage(1, 1, 1)

    def beside_third():
        dense[2].stage(1)
        dense[1].stage(2)
        attn_stage(1, 0, 2)
        give_attn(0, 0)

    def beside_rest():
        dense[0].stage(3)
        dense[2].stage(2)
        attn_stage(1, 1, 2)
        give_attn(0, 1)

    attention_back(0, lambda r: xw[r].astype(F32), [beside_first, beside_second, beside_third], beside_rest)
    low[...] = gx[...].astype(BF)
    send(14, low.at[at((1 - tensor) * row_count, extra)], edge_in.at[1], beside)
    send(small_key, small, small_in.at[0], core)
    attn_stage(0, 0, 0)
    dense[1].stage(3)
    attn_stage(1, 0, 3)
    dense[0].stage(4)
    attn_stage(0, 1, 0)
    arrived(small_key, small_in.at[0])
    small_in[1] = small[...] + small_in[0]
    send(small_key + 1, small_in.at[1], small_in.at[2], beside)
    dense[2].stage(3)
    attn_stage(1, 1, 3)

    arrived(pack_key, packs.at[1])
    split_packs = packs[...].astype(F32).reshape(-1, 2, IMAGES, width)
    every_slot, every_grad = (split_packs[:, n].reshape(-1, width).astype(BF) for n in range(2))
    every_slot_t = every_slot.T
    few = chunk if teams == 1 else LANES
    expert_steps = 2 * chunks * chunk // few

    def expert_grads(i):
        for part, body in ((1, beside_experts_first), (2, beside_experts_second)):
            pl.when(i == part * expert_steps // 3)(body)
        lanes = pl.ds(pl.multiple_of(i * few, few), few)
        value, grad = gelu_parts(dot(every_slot, ei[:, lanes]))
        g_pre = (dot_t(every_grad, eo[lanes, :]) * grad).astype(BF)
        expert_in_out[:, lanes] = dot(every_slot_t, g_pre).astype(BF)
        expert_out_out[lanes, :] = dot(value.astype(BF).T, every_grad).astype(BF)

    def beside_experts_first():
        attn_stage(0, 0, 1)
        attn_stage(1, 0, 4)
        dense[1].stage(4)
        dense[0].stage(5)

    def beside_experts_second():
        attn_stage(0, 1, 1)
        attn_stage(1, 1, 4)
        dense[2].stage(4)

    loop(expert_steps, expert_grads)

    attn_stage(0, 0, 2)
    attn_stage(0, 1, 2)
    attn_stage(1, 0, 5)
    attn_stage(1, 1, 5)
    arrived(small_key + 1, small_in.at[2])
    small_parts[0] = small_in[1] + small_in[2]
    for k in range(1, team):
        send(small_key + 1 + k, small_parts.at[0], small_parts.at[k], mate(k)[0])
    dense[0].stage(6)
    dense[1].stage(5)
    dense[2].stage(5)
    attn_stage(0, 0, 3)
    attn_stage(0, 1, 3)

    for n, (source, dest) in enumerate(((act, act_out), (low, pg_out))):
        dest[...] = source[at(tensor * extra, row_count)]
        arrived(13 + n, edge_in.at[n])
        near = at(row_count - extra - tensor * (row_count - 2 * extra), extra)
        wide = jnp.concatenate([own[near]] * pairs, axis=1)
        merged = jnp.where(wide > 0.0, source[near].astype(F32), edge_in[n].astype(F32)).astype(BF)
        dest[at((1 - tensor) * (row_count - extra), extra)] = merged

    attn_stage(1, 0, 6)
    attn_stage(1, 1, 6)
    dense[0].stage(7)
    dense[1].stage(6)
    dense[2].stage(6)
    attn_stage(0, 0, 4)
    attn_stage(0, 1, 4)
    attn_stage(1, 0, 7)
    attn_stage(1, 1, 7)
    dense[1].stage(7)
    dense[2].stage(7)
    send(mlp_key, mlp_sum.at[section], mlp_sum.at[section], core, mlp_like)
    attn_stage(0, 0, 5)
    attn_stage(0, 1, 5)
    for k in range(1, team):
        arrived(small_key + 1 + k, small_parts.at[k])
    small_across[0] = sum([small_parts[k] for k in range(1, team)], start=small_parts[0])
    for k in range(1, teams):
        send(small_key + 1 + team + k, small_across.at[0], small_across.at[k], partner(k))
    for k in range(1, teams):
        arrived(small_key + 1 + team + k, small_across.at[k])
    small_out[...] = sum([small_across[k] for k in range(1, teams)], start=small_across[0])
    attn_stage(0, 0, 6)
    attn_stage(0, 1, 6)
    arrived(mlp_key, mlp_sum.at[1 - section])
    for q in range(chunks):
        for n, dest in enumerate((mi_out, mot_out)):
            dest[:, q * chunk : (q + 1) * chunk] = mlp_sum[n, q]
    attn_stage(0, 0, 7)
    attn_stage(0, 1, 7)
    for c in range(3):
        first = c * 3 * HD
        qkv_out[first : first + 2 * HD] = attn_sum[0, c * LANES : (c + 1) * LANES]
        qkv_out[first + 2 * HD : first + 3 * HD] = attn_sum[1, c * HD : (c + 1) * HD]
    attn_out[...] = attn_sum[1, 3 * HD :]

    for key, like in sent_off.items():
        copy(key, like, like, core).wait_send()


def compute(x_own, c_own, ids, gains, qkv, out, mi, mo, router, ei, eo):
    row_count, width = x_own.shape
    window = row_count + MOST // 2
    extra = window - row_count
    pairs = width // LANES
    ff = ei.shape[1]
    _, kept = bands(window)
    chunk_count = ff // 256
    chunks = chunk_count // 2
    vmem = pl.BlockSpec(memory_space=pltpu.VMEM)
    ranks = lax.axis_size("dp")
    team = min(8, ranks & -ranks)
    teams = ranks // team
    bits = [1 << n for n in range(team.bit_length() - 1)]
    spread = [bits[:1] + ["tensor"] + bits[1:], ["tensor"] + bits, bits[1::-1] + ["tensor"] + bits[2:]]
    mlp_orders = [spread[q % 3] for q in range(chunks)]
    attn_orders = [spread[2], spread[1]]
    boxes = []
    for order, lanes in [(order, 256) for order in mlp_orders] + [(order, width) for order in attn_orders]:
        size = width
        for n, dim in enumerate(order):
            size = size if dim == "tensor" else size // 2
            boxes.append(pltpu.VMEM((2 if "tensor" in order[n + 1 :] else 1, size, lanes), BF))
        boxes.append(pltpu.VMEM((teams, size, lanes), BF))
    stages = 2 * len(attn_orders[0])
    copies = 15 + (chunks + 2) * (stages + teams) + 1 + 2 * (team + teams + 1)
    return pl.pallas_call(
        functools.partial(
            compute_kernel, team=team, teams=teams, mlp_orders=mlp_orders, attn_orders=attn_orders
        ),
        out_shape=(
            jax.ShapeDtypeStruct((row_count, width), BF),
            jax.ShapeDtypeStruct((row_count, width), BF),
            jax.ShapeDtypeStruct(qkv.shape, BF),
            jax.ShapeDtypeStruct(out.shape, BF),
            jax.ShapeDtypeStruct((width, ff // 2), BF),
            jax.ShapeDtypeStruct((width, ff // 2), BF),
            jax.ShapeDtypeStruct((width, ff), BF),
            jax.ShapeDtypeStruct((ff, width), BF),
            jax.ShapeDtypeStruct((8, width), F32),
        ),
        in_specs=[vmem] * 11,
        out_specs=[vmem] * 9,
        scratch_shapes=[
            pltpu.VMEM((window, width), BF),
            pltpu.VMEM((window, width), BF),
            pltpu.VMEM((2, 8, width), F32),
            pltpu.VMEM((2 * width, width), BF),
            pltpu.VMEM((2, 2 * width, width), BF),
            pltpu.VMEM((2 * width, width), BF),
            pltpu.VMEM((2, 3 * width, width), BF),
            pltpu.VMEM((2, width, width), BF),
            pltpu.VMEM((2, *mi.shape), BF),
            pltpu.VMEM((2, *mo.shape), BF),
            pltpu.VMEM((2, SLOTS, width), BF),
            pltpu.VMEM((window, width), BF),
            pltpu.VMEM((2, extra, width), BF),
            pltpu.VMEM((2, SLOTS, width), BF),
            pltpu.VMEM((2, SLOTS, width), BF),
            pltpu.VMEM((2, SLOTS, width), BF),
            pltpu.VMEM((2, SLOTS, width), BF),
            pltpu.VMEM((4, window, width), BF),
            pltpu.VMEM((window, width), F32),
            pltpu.VMEM((window, width), BF),
            pltpu.VMEM((window, width), F32),
            pltpu.VMEM((2, pairs, LANES, window), BF),
            pltpu.VMEM((2, pairs, LANES, window), BF),
            pltpu.VMEM((pairs, LANES, window), BF),
            pltpu.VMEM((2, pairs, window, LANES), BF),
            pltpu.VMEM((2, pairs, window, LANES), BF),
            pltpu.VMEM((2, pairs, LANES, window), BF),
            pltpu.VMEM((2, pairs, kept, 2 * LANES), BF),
            pltpu.VMEM((window, width), BF),
            pltpu.VMEM((chunk_count, window, 256), BF),
            pltpu.VMEM((chunk_count, window, 256), BF),
            pltpu.VMEM((window, width), F32),
            pltpu.VMEM((window, width), BF),
            pltpu.VMEM((pairs, LANES, window), BF),
            pltpu.VMEM((3 * LANES, window), BF),
            pltpu.VMEM((3 * pairs, window, LANES), BF),
            pltpu.VMEM((window, LANES), F32),
            pltpu.VMEM((window, LANES), F32),
            pltpu.VMEM((kept, LANES), F32),
            pltpu.VMEM((window, LANES), F32),
            pltpu.VMEM((2, 2 * SLOTS, window), BF),
            pltpu.VMEM((SLOTS, ff), F32),
            pltpu.VMEM((2, SLOTS, width), BF),
            pltpu.VMEM((2, SLOTS, width), BF),
            pltpu.VMEM((2, 2, 2, width, width), BF),
            pltpu.VMEM((2, width, width), BF),
            pltpu.VMEM((2, 2, chunks, width, 256), BF),
            pltpu.VMEM((chunks, 2, width, 256), BF),
            pltpu.VMEM((2, chunks, width, 256), BF),
            pltpu.VMEM((8, width), F32),
            pltpu.VMEM((3, 8, width), F32),
            pltpu.VMEM((team, 8, width), F32),
            pltpu.VMEM((teams, 8, width), F32),
            pltpu.VMEM((2, teams, team, 2 * IMAGES, width), BF),
            pltpu.VMEM((2 * IMAGES, width), BF),
            pltpu.SemaphoreType.DMA((copies,)),
            pltpu.SemaphoreType.DMA((copies,)),
            *boxes,
        ],
        compiler_params=pltpu.CompilerParams(
            vmem_limit_bytes=62 * 1024 * 1024, collective_id=0, has_side_effects=True
        ),
    )(x_own, c_own, ids, gains, qkv, out, mi, mo, router, ei, eo)


def finish_kernel(
    act, pg, qkv, attn, mi, mot, expert_in, expert_out, small,
    act_out, pg_out, gains_out, qkv_out, attn_out, mi_out, mo_out, router_out, expert_in_out, expert_out_out,
):
    section, tensor = lax.axis_index("section"), lax.axis_index("tensor")
    act_out[...] = act[...]
    pg_out[...] = pg[...]
    gains_out[...] = jnp.where(section == 0, small[0:2], small[2:4])
    router_out[...] = jnp.where(tensor == 0, small[4:5], small[5:6])
    pairs = ((qkv, qkv_out), (attn, attn_out), (mi, mi_out), (expert_in, expert_in_out), (expert_out, expert_out_out))
    for source, dest in pairs:
        dest[...] = source[...].astype(F32)
    mo_out[...] = mot[...].astype(F32).T


def finish(act, pg, qkv, attn, mi, mot, expert_in, expert_out, small):
    steps = 3

    def by_rows(a):
        return pl.BlockSpec((a.shape[0] // steps, a.shape[1]), lambda i: (i, 0))

    def whole(a):
        return pl.BlockSpec(a.shape, lambda i: (0, 0))

    def like(a):
        return jax.ShapeDtypeStruct(a.shape, F32)

    gains = jax.ShapeDtypeStruct((2, act.shape[1]), F32)
    router = jax.ShapeDtypeStruct((1, act.shape[1]), F32)
    mo = jax.ShapeDtypeStruct(mot.shape[::-1], F32)
    mot_spec = pl.BlockSpec((mot.shape[0], mot.shape[1] // steps), lambda i: (0, i))
    return pl.pallas_call(
        finish_kernel,
        grid=(steps,),
        out_shape=(
            act, pg, gains, like(qkv), like(attn), like(mi), mo, router, like(expert_in), like(expert_out)
        ),
        in_specs=[
            whole(act), whole(pg), by_rows(qkv), by_rows(attn), by_rows(mi), mot_spec, by_rows(expert_in),
            by_rows(expert_out), whole(small),
        ],
        out_specs=[
            whole(act), whole(pg), whole(gains), by_rows(qkv), by_rows(attn), by_rows(mi), by_rows(mo), whole(router),
            by_rows(expert_in), by_rows(expert_out),
        ],
        compiler_params=pltpu.CompilerParams(vmem_limit_bytes=60 * 1024 * 1024),
    )(act, pg, qkv, attn, mi, mot, expert_in, expert_out, small)


def per_device(
    patches, image_ids, cotangent, norm_gains, qkv_weight, out_weight, mlp_in, mlp_out, router, expert_in, expert_out
):
    width = patches.shape[2]
    part = qkv_weight.shape[3]
    qkv = jnp.transpose(qkv_weight[0], (1, 2, 0)).reshape(-1, width)
    results = compute(
        patches[0], cotangent[0], image_ids, norm_gains[0], qkv, out_weight[0], mlp_in, mlp_out, router.T,
        expert_in[0], expert_out[0],
    )
    act, pg, gains, qkv_grad, out_grad, mi_grad, mo_grad, router_grad, ei_grad, eo_grad = finish(*results)
    qkv_grad = jnp.transpose(qkv_grad.reshape(3, part, width), (2, 0, 1))
    return (
        act[None], pg[None], gains[None], qkv_grad[None], out_grad[None], mi_grad, mo_grad, router_grad.T,
        ei_grad[None], eo_grad[None],
    )


def solution(mesh):
    return jax.shard_map(
        per_device,
        mesh=mesh,
        in_specs=(
            P(("dp", "section"), "tensor", None),
            P("dp", None),
            P(("dp", "section"), "tensor", None),
            P("section", None, None),
            P("section", None, None, "tensor"),
            P("section", "tensor", None),
            P(None, "tensor"),
            P("tensor", None),
            P(None, "tensor"),
            P("tensor", None, None),
            P("tensor", None, None),
        ),
        out_specs=(
            P(("dp", "section"), "tensor", None),
            P(("dp", "section"), "tensor", None),
            P("section", None, None),
            P("section", None, None, "tensor"),
            P("section", "tensor", None),
            P(None, "tensor"),
            P("tensor", None),
            P(None, "tensor"),
            P("tensor", None, None),
            P("tensor", None, None),
        ),
        check_vma=False,
    )
```

```python
import functools

import jax
import jax.numpy as jnp
from jax import lax
from jax.experimental import pallas as pl
from jax.experimental.pallas import tpu as pltpu
from jax.sharding import PartitionSpec as P

HD = 64
IMAGES = 8
MOST = 256
LANES = 128
SLOTS = 16
EPSILON = 1e-06
BF = jnp.bfloat16
F32 = jnp.float32


def dot(a, b):
    return jnp.dot(a, b, preferred_element_type=F32)


def dot_t(a, b):
    return lax.dot_general(a, b, (((1,), (1,)), ((), ())), preferred_element_type=F32)


def t_dot(a, b):
    return lax.dot_general(a, b, (((0,), (0,)), ((), ())), preferred_element_type=F32)


def normalise(x):
    centred = x - jnp.mean(x, axis=-1, keepdims=True)
    scale = lax.rsqrt(jnp.mean(centred * centred, axis=-1, keepdims=True) + EPSILON)
    return centred * scale, scale


def norm_back(x, gain, gz):
    unit, scale = normalise(x)
    scaled = gz * gain
    mean_plain = jnp.mean(scaled, axis=-1, keepdims=True)
    mean_unit = jnp.mean(scaled * unit, axis=-1, keepdims=True)
    return scale * (scaled - mean_plain - unit * mean_unit), jnp.sum(gz * unit, axis=0, keepdims=True)


def gelu_parts(u):
    cdf = 0.5 * (1.0 + lax.erf(u * 0.7071067811865476))
    return u * cdf, cdf + u * (0.3989422804014327 * jnp.exp(-0.5 * u * u))


def pair_up(tile):
    row = lax.broadcasted_iota(jnp.int32, tile.shape, 0)
    zero = jnp.zeros_like(tile)
    return jnp.concatenate([jnp.where(row < HD, tile, zero), jnp.where(row >= HD, tile, zero)], axis=1)


def pair_down(both):
    n = both.shape[1] // 2
    row = lax.broadcasted_iota(jnp.int32, (both.shape[0], n), 0)
    return jnp.where(row < HD, both[:, :n], both[:, n:])


def bands(window):
    reach = MOST // LANES
    found, at = [], 0
    for i in range(window // LANES):
        first = max(0, i - reach) * LANES
        count = min(window, (i + reach + 1) * LANES) - first
        found.append((i * LANES, first, count, at))
        at += count
    return found, at


MESH = pl.DeviceIdType.MESH


def compute_kernel(
    x_own, c_own, ids, gains_own, qkv_own, out_own, mi_own, mo_own, router_own, ei_own, eo_own,
    act_out, pg_out, qkv_out, attn_out, mi_out, mot_out, expert_in_out, expert_out_out, small_out,
    xw, cw, gains, wy, wc, w_own, wqkv, wo, mi, mo, ei, eo, expert_in_sum, expert_out_sum, routert, act, edge_in, slots, geos, slot_in, pack,
    z, x1, sent, x3, qt, kt, vt, kr, vr, ot, pt, tok, hidden, slope, gx, low, got, gt, gtok, gk_sum, gv_sum,
    bias, own, mixing, eslope, eout, gslot, grad_attn, attn_sum, grad_mlp, mlp_core, mlp_sum,
    small, small_in, small_parts, small_across, packs, small_pack, send_sem, recv_sem, here_sem,
    *boxes, team, teams, mlp_orders,
):
    row_count, width = x_own.shape
    window = xw.shape[0]
    extra = window - row_count
    half = window // 2
    pairs = width // LANES
    total = ids.shape[1]
    dp = lax.axis_index("dp")
    section = lax.axis_index("section")
    tensor = lax.axis_index("tensor")
    core = (dp, 1 - section, tensor)
    beside = (dp, section, 1 - tensor)

    spot = lax.rem(dp, team)
    this_team = dp // team

    def mate(k):
        place, bit = spot, 1
        while bit < team:
            if k & bit:
                place = jnp.where(lax.rem(spot // bit, 2) == 0, place + bit, place - bit)
            bit *= 2
        return (dp - spot + place, section, tensor), place

    def partner(k):
        return (lax.rem(dp + k * team, team * teams), section, tensor)

    blocks, _ = bands(window)
    row_blocks = window // LANES

    def at(start, size, step=LANES):
        return pl.ds(pl.multiple_of(start, step), size)

    def rows(i, n=LANES):
        return pl.ds(pl.multiple_of(i * n, n), n)

    def loop(n, body):
        def step(i, carry):
            body(i)
            return carry

        lax.fori_loop(0, n, step, 0)

    sent_off = {}

    def copy(key, source, dest, device):
        return pltpu.make_async_remote_copy(
            src_ref=source,
            dst_ref=dest,
            send_sem=send_sem.at[key],
            recv_sem=recv_sem.at[key],
            device_id=device,
            device_id_type=MESH,
        )

    def send(key, source, dest, device, like=None):
        copy(key, source, dest, device).start()
        sent_off[key] = source if like is None else like

    def arrived(key, dest):
        copy(key, dest, dest, core).wait_recv()

    def only(which):
        return pl.when(section == which)

    barrier = pltpu.get_barrier_semaphore()
    neighbours = [core, beside] + [mate(k)[0] for k in range(1, team)] + [partner(k) for k in range(1, teams)]
    for device in neighbours:
        pl.semaphore_signal(barrier, inc=1, device_id=device, device_id_type=MESH)

    def local(key, source, dest):
        found = pltpu.make_async_copy(source, dest, here_sem.at[key])
        found.start()
        return found

    qkv_rows = qkv_own.shape[0]
    own_rows = at(tensor * extra, row_count)
    near_copies = [
        local(0, x_own, xw.at[own_rows]),
        local(1, qkv_own, w_own.at[:qkv_rows]),
        local(2, out_own, w_own.at[qkv_rows:]),
    ]
    later_copies = [
        local(3, mi_own, mi.at[tensor]),
        local(4, mo_own, mo.at[tensor]),
        local(5, c_own, cw.at[own_rows]),
        local(6, ei_own, ei),
        local(7, eo_own, eo),
    ]
    gains[section, :2] = gains_own[...]
    first_row = lax.broadcasted_iota(jnp.int32, (SLOTS, width), 0) == 0
    router_rows = jnp.broadcast_to(router_own[...].astype(F32), (SLOTS, width))
    routert[tensor] = jnp.where(first_row, router_rows, 0.0).astype(BF)
    pl.semaphore_wait(barrier, len(neighbours))

    qkv_here, out_here = wy.at[:qkv_rows], wy.at[qkv_rows:]
    qkv_near, out_near = wc.at[0, :qkv_rows], wc.at[0, qkv_rows:]
    qkv_far, out_far = wc.at[1, :qkv_rows], wc.at[1, qkv_rows:]

    @only(0)
    def _():
        send(3, qkv_own, qkv_here, beside)
        send(15, out_own, out_here, beside)

    edge = x_own.at[at((1 - tensor) * (row_count - extra), extra)]
    send(0, edge, xw.at[at(tensor * row_count, extra)], beside)
    send(1, gains.at[section], gains.at[section], core)
    send(2, qkv_own, qkv_near, core)
    send(16, out_own, out_near, core)

    ids_row = ids[pl.ds(section, 1), :].astype(F32)
    image = lax.broadcasted_iota(jnp.int32, (SLOTS, total), 0).astype(F32)
    spread = jnp.broadcast_to(ids_row, (SLOTS, total))
    middle = jnp.sum((spread < image).astype(F32) + (spread <= image).astype(F32), axis=1, keepdims=True)
    first_half = (middle < total).astype(F32)
    mine = jnp.where(tensor == 0, first_half, 1.0 - first_half)
    window_ids = ids[pl.ds(section, 1), at(tensor * (total - window), window)].astype(F32)
    member = (jnp.broadcast_to(window_ids, (SLOTS, window)) == image[:, :window]).astype(F32)
    member_own = member * mine
    own_row = jnp.sum(member_own, axis=0, keepdims=True)
    own[...] = jnp.broadcast_to(own_row, (LANES, window)).T
    ids_col = jnp.broadcast_to(window_ids, (LANES, window)).T
    for q0, k0, count, kept in blocks:
        same = ids_col[k0 : k0 + count] == jnp.broadcast_to(window_ids[:, q0 : q0 + LANES], (count, LANES))
        bias[kept : kept + count, :] = jnp.where(same, 0.0, -1e30)

    def place(source, b, t, kinds=(0, 1, 2, 3)):
        for c in kinds:
            dest, base = (wqkv, c * width) if c < 3 else (wo, 0)
            first = c * 3 * HD
            dest[b, at(base + t * LANES, 2 * HD)] = source[first : first + 2 * HD]
            dest[b, at(base + 2 * LANES + t * HD, HD, HD)] = source[first + 2 * HD : first + 3 * HD]

    for found in near_copies:
        found.wait()
    place(w_own, section, tensor)
    arrived(1, gains.at[1 - section])
    arrived(2, qkv_near)
    arrived(16, out_near)
    place(wc.at[0], 1 - section, tensor)
    arrived(0, xw.at[at((1 - tensor) * row_count, extra)])

    @only(0)
    def _():
        arrived(3, qkv_here)
        send(4, qkv_here, qkv_far, core)
        send(5, mi_own, mi.at[tensor], beside)
        place(wy, 0, 1 - tensor, (0, 1, 2))

    @only(1)
    def _():
        arrived(4, qkv_far)
        send(5, mo_own, mo.at[tensor], beside)
        place(wc.at[1], 0, 1 - tensor, (0, 1, 2))

    def first_out():
        @only(0)
        def _():
            arrived(15, out_here)
            send(17, out_here, out_far, core)
            place(wy, 0, 1 - tensor, (3,))

        @only(1)
        def _():
            arrived(17, out_far)
            send(3, qkv_own, qkv_here, beside)
            send(15, out_own, out_here, beside)
            place(wc.at[1], 0, 1 - tensor, (3,))

    def second_out():
        @only(0)
        def _():
            arrived(17, out_far)
            place(wc.at[1], 1, 1 - tensor, (3,))

        @only(1)
        def _():
            arrived(15, out_here)
            send(17, out_here, out_far, core)
            place(wy, 1, 1 - tensor, (3,))

    def add_across(first, piece, heard):
        if teams == 1:
            return
        for k in range(1, teams):
            copy(first + k, piece, heard.at[k], partner(k)).start()
        whole = piece[...].astype(F32)
        for k in range(1, teams):
            arrived(first + k, heard.at[k])
            copy(first + k, piece, heard.at[k], partner(k)).wait_send()
            whole = whole + heard[k].astype(F32)
        piece[...] = whole.astype(BF)

    class Cube:
        def __init__(self, key, pick, core_in, total, order, boxes):
            self.key, self.pick, self.core_in, self.total, self.order = key, pick, core_in, total, order
            self.boxes, self.across = boxes[:-1], boxes[-1]
            start, size, self.plan = 0, total.shape[0], []
            for dim in order:
                if dim == "tensor":
                    self.plan.append((dim, start, size, start))
                else:
                    size //= 2
                    bit = lax.rem(spot // dim, 2)
                    self.plan.append((dim, start + bit * size, size, start + (1 - bit) * size))
                    start = start + bit * size
            self.back = [(i, *step) for i, step in enumerate(self.plan) if step[0] != "tensor"][::-1]
            self.like = {size: total.at[:size] for _, _, _, size, _ in self.back}
            self.along = order.index("tensor")

        def to_core(self, source):
            send(self.key, source, self.core_in, core, self.core_in)

        def add(self, parts, start, size, box):
            for n, part in enumerate(parts):
                kept = self.pick(part, at(start, size, 16))
                kept[...] = (kept[...].astype(F32) + box[n].astype(F32)).astype(BF)

        def stage(self, k):
            steps, rounds = len(self.plan), len(self.back)
            both = (0, 1)
            if k == 0:
                arrived(self.key, self.core_in)
                self.add(both, 0, self.total.shape[0], self.core_in)
            elif k <= steps:
                _, start, size, _ = self.plan[k - 1]
                arrived(self.key + k, self.boxes[k - 1])
                self.add((tensor,) if self.along < k else both, start, size, self.boxes[k - 1])
            else:
                _, _, _, size, start = self.back[k - steps - 1]
                arrived(self.key + k, self.total.at[at(start, size, 16)])
            if k < steps:
                dim, _, size, start = self.plan[k]
                if dim == "tensor":
                    device = beside
                    source = self.pick(pl.ds(1 - tensor, 1), at(start, size, 16))
                else:
                    device = mate(dim)[0]
                    parts = pl.ds(tensor, 1) if self.along < k else slice(None)
                    source = self.pick(parts, at(start, size, 16))
                send(self.key + k + 1, source, self.boxes[k], device, self.boxes[k])
            elif k == steps:
                _, start, size, _ = self.plan[-1]
                piece = self.total.at[at(start, size, 16)]
                piece[...] = self.pick(tensor, at(start, size, 16))[...]
                add_across(self.key + Cube.stages, piece, self.across)
            if steps <= k < steps + rounds:
                _, dim, start, size, _ = self.back[k - steps]
                region = self.total.at[at(start, size, 16)]
                send(self.key + k + 1, region, region, mate(dim)[0], self.like[size])

        stages = len(mlp_orders[0]) * 2
        keys = stages + teams

    class Straight:
        def __init__(self, key, pick, core_in, total, boxes):
            self.key, self.pick, self.core_in, self.total = key, pick, core_in, total
            self.beside_in, self.parts, self.across = boxes
            self.size = total.shape[0] // team
            self.like = total.at[: self.size]

        def part(self, place):
            return at(place * self.size, self.size, 16)

        def to_core(self, source):
            send(self.key, source, self.core_in, core, self.core_in)

        def stage(self, k):
            every = pl.ds(0, self.total.shape[0])
            near = self.pick(tensor, every)
            if k == 0:
                arrived(self.key, self.core_in)
                far = self.pick(1 - tensor, every)
                far[...] = (far[...].astype(F32) + self.core_in[1 - tensor].astype(F32)).astype(BF)
                send(self.key + 1, far, self.beside_in, beside, self.beside_in)
            if k == 1:
                arrived(self.key + 1, self.beside_in)
                both = near[...].astype(F32) + self.core_in[tensor].astype(F32)
                near[...] = (both + self.beside_in[...].astype(F32)).astype(BF)
                for n in range(1, team):
                    device, place = mate(n)
                    source = self.pick(tensor, self.part(place))
                    send(self.key + 1 + n, source, self.parts.at[n], device, self.like)
            if k == 2:
                whole = self.pick(tensor, self.part(spot))[...].astype(F32)
                for n in range(1, team):
                    arrived(self.key + 1 + n, self.parts.at[n])
                    whole = whole + self.parts[n].astype(F32)
                piece = self.total.at[self.part(spot)]
                piece[...] = whole.astype(BF)
                add_across(self.key + 1 + 2 * team, piece, self.across)
                for n in range(1, team):
                    send(self.key + 1 + team + n, piece, piece, mate(n)[0], self.like)
            if k == 3:
                for n in range(1, team):
                    arrived(self.key + 1 + team + n, self.total.at[self.part(mate(n)[1])])

        keys = 1 + 2 * team + teams

    chunks = len(mlp_orders)
    key, taken = 18, 0

    def boxes_of(count):
        nonlocal taken
        taken += count
        return boxes[taken - count : taken]

    def mlp_pick(q):
        return lambda parts, where: grad_mlp.at[section, parts, q, where]

    def attn_pick(n):
        return lambda parts, where: grad_attn.at[section, parts, n, where]

    dense, attn = [], []
    for q in range(chunks):
        total_of = mlp_sum.at[section, q]
        found = boxes_of(len(mlp_orders[q]) + 1)
        dense.append(Cube(key, mlp_pick(q), mlp_core.at[q], total_of, mlp_orders[q], found))
        key += Cube.keys
    for n in range(2):
        heard = wc.at[:, n * width : (n + 1) * width]
        attn.append(Straight(key, attn_pick(n), heard, attn_sum.at[n], boxes_of(3)))
        key += Straight.keys
    mlp_key, pack_key, small_key = key, key + 1, key + 1 + team + teams
    mlp_like = mlp_sum.at[0]

    def give_attn(b, n):
        @only(1 - b)
        def _():
            attn[n].to_core(grad_attn.at[b, :, n])

    def attn_stage(b, n, k):
        @only(b)
        def _():
            attn[n].stage(k)

    def give_dense(q):
        dense[q].to_core(grad_mlp.at[1 - section, :, q])

    def attention(b, x_of, out_ref, ahead_of_out):
        def norm(i):
            unit, _ = normalise(x_of(rows(i)))
            z[2 * b, rows(i)] = (unit * gains[b, 0:1, :]).astype(BF)

        loop(row_blocks, norm)
        zz = z[2 * b]
        for c, dest in enumerate((qt.at[b], kt.at[b], vt)):
            tall = dot_t(wqkv[b, c * width : (c + 1) * width], zz)
            tall = (tall.astype(BF) * jnp.asarray(HD**-0.5 if c == 0 else 1.0, BF)).reshape(pairs, LANES, window)
            dest[...] = tall
        for c, dest in ((1, kr), (2, vr)):
            flat = dot_t(zz, wqkv[b, c * width : (c + 1) * width]).astype(BF)
            for j in range(pairs):
                dest[b, j] = flat[:, j * LANES : (j + 1) * LANES]

        def pair(j):
            for q0, k0, count, kept in blocks:
                scores = dot(kr[b, j, k0 : k0 + count, :], pair_up(qt[b, j, :, q0 : q0 + LANES]))
                veil = bias[kept : kept + count, :]
                scores = scores + jnp.concatenate([veil, veil], axis=1)
                powers = jnp.exp(scores - jnp.max(scores, axis=0, keepdims=True))
                probs = (powers * (1.0 / jnp.sum(powers, axis=0, keepdims=True))).astype(BF)
                pt[b, j, kept : kept + count, :] = probs
                ot[b, j, :, q0 : q0 + LANES] = pair_down(dot(vt[j, :, k0 : k0 + count], probs)).astype(BF)

        loop(pairs, pair)
        for j in range(pairs):
            tok[:, j * LANES : (j + 1) * LANES] = ot[b, j].T

        ahead_of_out()

        def out(i):
            out_ref[rows(i, half)] = x_of(rows(i, half)) + dot(tok[rows(i, half)], wo[b])

        loop(2, out)

    def attention_back(b, x_of, beside_pairs, after_pairs):
        ga = low[...]
        got[...] = dot_t(wo[b], ga).astype(BF).reshape(pairs, LANES, window)
        for j in range(pairs):
            piece = dot(ot[b, j], ga).astype(BF)
            if j < 2:
                grad_attn[b, j, 1, 3 * HD : 5 * HD, :] = piece
            else:
                for t in range(2):
                    grad_attn[b, t, 1, 5 * HD : 6 * HD, :] = piece[t * HD : (t + 1) * HD]
        zz = z[2 * b]

        def pair(j):
            for at_pair, body in enumerate(beside_pairs):
                pl.when(j == at_pair)(body)
            gk_sum[...] = jnp.zeros_like(gk_sum)
            gv_sum[...] = jnp.zeros_like(gv_sum)
            for q0, k0, count, kept in blocks:
                go_pair = pair_up(got[j, :, q0 : q0 + LANES])
                q_pair = pair_up(qt[b, j, :, q0 : q0 + LANES])
                low_probs = pt[b, j, kept : kept + count, :]
                probs = low_probs.astype(F32)
                weighted = dot(vr[b, j, k0 : k0 + count, :], go_pair) * probs
                inner = jnp.sum(weighted, axis=0, keepdims=True)
                gs = (weighted - probs * inner).astype(BF)
                gq = pair_down(dot(kt[b, j, :, k0 : k0 + count], gs)) * HD**-0.5
                gt[:LANES, q0 : q0 + LANES] = gq.astype(BF)
                gk_sum[k0 : k0 + count] += dot_t(gs, q_pair)
                gv_sum[k0 : k0 + count] += dot_t(low_probs, go_pair)
            gtok[j] = gt[:LANES].T
            for c, total_of in ((1, gk_sum), (2, gv_sum)):
                low_sum = total_of[...].astype(BF)
                gtok[c * pairs + j] = low_sum
                gt[c * LANES : (c + 1) * LANES] = low_sum.T
            pieces = [dot(gt[c * LANES : (c + 1) * LANES], zz).astype(BF) for c in range(3)]

            @pl.when(j < 2)
            def _():
                for c in range(3):
                    grad_attn[b, j, 0, c * LANES : (c + 1) * LANES, :] = pieces[c]

            @pl.when(j == 2)
            def _():
                for c in range(3):
                    for t in range(2):
                        grad_attn[b, t, 1, c * HD : (c + 1) * HD, :] = pieces[c][t * HD : (t + 1) * HD]

        loop(pairs, pair)
        after_pairs()
        gain = gains[b, 0:1, :]

        def back(i, gain_grad):
            wide = jnp.concatenate([gtok[c, rows(i, half)] for c in range(3 * pairs)], axis=1)
            step, part = norm_back(x_of(rows(i, half)), gain, dot(wide, wqkv[b]))
            gx[rows(i, half)] += step
            return gain_grad + part

        small[2 * b : 2 * b + 1, :] = lax.fori_loop(0, 2, back, jnp.zeros((1, width), F32))

    attention(0, lambda r: xw[r].astype(F32), x1, first_out)

    def norm_middle(source, which):
        def body(i):
            unit, _ = normalise(source[rows(i)])
            z[which, rows(i)] = (unit * gains[which // 2, 1:2, :]).astype(BF)

        loop(row_blocks, body)

    norm_middle(x1, 1)

    for found in later_copies:
        found.wait()

    @only(0)
    def _():
        arrived(5, mi.at[1 - tensor])
        send(6, mi.at[1 - tensor], mi.at[1 - tensor], core, mi_own)
        arrived(6, mo.at[1 - tensor])

    @only(1)
    def _():
        arrived(5, mo.at[1 - tensor])
        send(6, mo.at[1 - tensor], mo.at[1 - tensor], core, mo_own)
        arrived(6, mi.at[1 - tensor])

    chunk = 256

    def hidden_chunk(i):
        part, first = i // chunks, pl.multiple_of(i % chunks * chunk, chunk)
        value, grad = gelu_parts(dot(z[1], mi[part, :, pl.ds(first, chunk)]))
        hidden[i] = value.astype(BF)
        slope[i] = grad.astype(BF)

    loop(2 * chunks, hidden_chunk)

    def dense_out(i):
        h = jnp.concatenate([hidden[c, rows(i, half)] for c in range(2 * chunks)], axis=1)
        sent[rows(i, half)] = (x1[rows(i, half)] + dot(h, mo[...].reshape(-1, width))).astype(BF)

    loop(2, dense_out)

    @only(0)
    def _():
        arrived(4, qkv_far)
        place(wc.at[1], 1, 1 - tensor, (0, 1, 2))

    @only(1)
    def _():
        arrived(3, qkv_here)
        send(4, qkv_here, qkv_far, core)
        place(wy, 1, 1 - tensor, (0, 1, 2))

    c_edge = c_own.at[at((1 - tensor) * (row_count - extra), extra)]
    send(7, c_edge, cw.at[at(tensor * row_count, extra)], beside)
    send(8, routert.at[tensor], routert.at[tensor], beside)

    attention(1, lambda r: sent[r].astype(F32), x3, second_out)
    norm_middle(x3, 3)
    z3 = z[3]
    arrived(8, routert.at[1 - tensor])
    powers = [jnp.exp(dot_t(routert[e], z3)[:1]) for e in range(2)]
    dispatch, combine = [], []
    for e in range(2):
        totals = jnp.sum(member * powers[e], axis=1, keepdims=True)
        dispatch.append(powers[e] / jnp.sum(member * totals, axis=0, keepdims=True))
        combine.append(powers[e] / (powers[0] + powers[1]))
        d_low = (member_own * dispatch[e].astype(BF).astype(F32)).astype(BF)
        c_low = (member * combine[e].astype(BF).astype(F32)).astype(BF)
        mixing[0, e * SLOTS : (e + 1) * SLOTS] = d_low
        mixing[1, e * SLOTS : (e + 1) * SLOTS] = c_low
        slots[e] = dot(d_low, z3).astype(BF)
    send(9, slots.at[1 - tensor], slot_in.at[0], beside)
    arrived(7, cw.at[at((1 - tensor) * row_count, extra)])

    def mask(i):
        wide = jnp.concatenate([own[rows(i)]] * pairs, axis=1)
        low[rows(i)] = jnp.where(wide > 0.0, cw[rows(i)].astype(F32), 0.0).astype(BF)

    loop(row_blocks, mask)
    gy = low[...]
    for e in range(2):
        geos[e] = dot(mixing[1, e * SLOTS : (e + 1) * SLOTS], gy).astype(BF)
    send(10, geos.at[1 - tensor], slot_in.at[1], beside)

    arrived(9, slot_in.at[0])
    pack[0] = slots[tensor] + slot_in[0]
    value, grad = gelu_parts(dot(pack[0], ei[...]))
    eslope[...] = grad
    eout[tensor] = dot(value.astype(BF), eo[...]).astype(BF)
    send(11, eout.at[tensor], eout.at[tensor], beside)
    arrived(10, slot_in.at[1])
    pack[1] = geos[tensor] + slot_in[1]
    g_hidden = dot_t(pack[1], eo[...])
    gslot[tensor] = dot_t((g_hidden * eslope[...]).astype(BF), ei[...]).astype(BF)
    send(12, gslot.at[tensor], gslot.at[tensor], beside)
    arrived(11, eout.at[1 - tensor])
    outputs = eout[...].reshape(2 * SLOTS, width)

    def finish(i):
        mixed = t_dot(mixing[1, :, rows(i)], outputs)
        act[rows(i)] = (x3[rows(i)] + mixed).astype(BF)

    loop(row_blocks, finish)
    send(13, act.at[at((1 - tensor) * row_count, extra)], edge_in.at[0], beside)

    def nothing():
        pass

    all_packs, team_like = packs.at[0], packs.at[0, 0]

    def share_slots():
        halves = [pack[n].astype(F32)[:IMAGES] for n in range(2)]
        small_pack[...] = jnp.concatenate(halves, axis=0).astype(BF)
        for k in range(1, team):
            send(pack_key + k, small_pack, packs.at[0, this_team, spot], mate(k)[0], small_pack)

    def gather_slots():
        for k in range(1, team):
            arrived(pack_key + k, packs.at[0, this_team, mate(k)[1]])
        packs[0, this_team, spot] = small_pack[...]
        for k in range(1, teams):
            team_packs = packs.at[0, this_team]
            send(pack_key + team + k, team_packs, team_packs, partner(k), team_like)
        for k in range(1, teams):
            arrived(pack_key + team + k, packs.at[0, lax.rem(this_team + k, teams)])
        send(pack_key, packs.at[0], packs.at[1], core, all_packs)

    per_token = [jnp.sum(dot_t(eout[e], gy) * member, axis=0, keepdims=True) for e in range(2)]
    inner = combine[0] * per_token[0] + combine[1] * per_token[1]
    arrived(12, gslot.at[1 - tensor])
    logit_grads = []
    for e in range(2):
        g_dispatch = jnp.sum(dot_t(gslot[e], z3) * member_own, axis=0, keepdims=True)
        weighted = dispatch[e] * g_dispatch
        sums = jnp.sum(member * weighted, axis=1, keepdims=True)
        from_dispatch = weighted - dispatch[e] * jnp.sum(member * sums, axis=0, keepdims=True)
        logit_grads.append(combine[e] * (per_token[e] - inner) + from_dispatch)
    which_row = lax.broadcasted_iota(jnp.int32, (SLOTS, width), 0)
    router_rows = jnp.where(
        which_row == 0,
        jnp.broadcast_to(routert[0].astype(F32)[:1], (SLOTS, width)),
        jnp.where(which_row == 1, jnp.broadcast_to(routert[1].astype(F32)[:1], (SLOTS, width)), 0.0),
    ).astype(BF)
    which = lax.broadcasted_iota(jnp.int32, (SLOTS, window), 0)
    logit_grad = jnp.where(which == 0, logit_grads[0], jnp.where(which == 1, logit_grads[1], 0.0)).astype(BF)
    small[4:6, :] = dot(logit_grad, z3)[:2]
    small[6:8, :] = jnp.zeros((2, width), F32)
    mixing[1, :SLOTS] = logit_grad
    slots_and_router = jnp.concatenate([gslot[0], gslot[1], router_rows], axis=0)

    def experts_back(i, gain_grad):
        at = pl.ds(pl.multiple_of(i * LANES, LANES), LANES)
        parts = jnp.concatenate([mixing[0, :, at], mixing[1, :SLOTS, at]], axis=0)
        step, part = norm_back(x3[rows(i)], gains[1, 1:2, :], t_dot(parts, slots_and_router))
        total_of = low[rows(i)].astype(F32) + step
        gx[rows(i)] = total_of
        low[rows(i)] = total_of.astype(BF)
        return gain_grad + part

    small[3:4, :] = lax.fori_loop(0, row_blocks, experts_back, jnp.zeros((1, width), F32))

    def shares_second():
        gather_slots()
        give_attn(1, 0)

    share_slots()
    attention_back(1, lambda r: sent[r].astype(F32), [nothing, nothing, shares_second], lambda: give_attn(1, 1))

    low[...] = gx[...].astype(BF)
    gsent = low[...]
    gsent_t = gsent.T
    z2 = z[1]
    z2_t = z2.T

    def hidden_back(n):
        for ahead, body in ((2, dense_first), (4, dense_second)):
            pl.when(n == ahead)(body)
        q, part = n // 2, lax.rem(n, 2)
        i, first = part * chunks + q, pl.multiple_of(q * chunk, chunk)
        grad_mlp[1, part, q] = dot(gsent_t, hidden[i]).astype(BF)
        g_hidden = dot_t(gsent, mo[part, pl.ds(first, chunk), :])
        g_pre = (g_hidden * slope[i].astype(F32)).astype(BF)
        hidden[i] = g_pre
        grad_mlp[0, part, q] = dot(z2_t, g_pre).astype(BF)

    def dense_first():
        give_dense(0)
        attn_stage(1, 0, 0)

    def dense_second():
        give_dense(1)
        attn_stage(1, 1, 0)

    loop(2 * chunks, hidden_back)
    give_dense(2)
    dense[0].stage(0)

    def dense_back(i, gain_grad):
        gz = jnp.zeros((half, width), F32)
        for part in range(2):
            g = jnp.concatenate([hidden[part * chunks + c, rows(i, half)] for c in range(chunks)], axis=1)
            gz = gz + dot_t(g, mi[part])
        step, part = norm_back(x1[rows(i, half)], gains[0, 1:2, :], gz)
        total_of = low[rows(i, half)].astype(F32) + step
        gx[rows(i, half)] = total_of
        low[rows(i, half)] = total_of.astype(BF)
        return gain_grad + part

    small[1:2, :] = lax.fori_loop(0, 2, dense_back, jnp.zeros((1, width), F32))

    def beside_first():
        dense[1].stage(0)
        attn_stage(1, 0, 1)

    def beside_second():
        dense[2].stage(0)
        dense[0].stage(1)
        attn_stage(1, 1, 1)

    def beside_third():
        give_attn(0, 0)
        dense[1].stage(1)
        attn_stage(1, 0, 2)

    def beside_rest():
        give_attn(0, 1)
        attn_stage(0, 0, 0)
        dense[2].stage(1)
        dense[0].stage(2)
        attn_stage(1, 1, 2)

    attention_back(0, lambda r: xw[r].astype(F32), [beside_first, beside_second, beside_third], beside_rest)
    low[...] = gx[...].astype(BF)
    send(14, low.at[at((1 - tensor) * row_count, extra)], edge_in.at[1], beside)
    send(small_key, small, small_in.at[0], core)
    attn_stage(0, 1, 0)
    dense[1].stage(2)
    dense[2].stage(2)
    arrived(small_key, small_in.at[0])
    small_in[1] = small[...] + small_in[0]
    send(small_key + 1, small_in.at[1], small_in.at[2], beside)
    attn_stage(0, 0, 1)
    dense[0].stage(3)

    arrived(pack_key, packs.at[1])
    split_packs = packs[...].astype(F32).reshape(-1, 2, IMAGES, width)
    every_slot, every_grad = (split_packs[:, n].reshape(-1, width).astype(BF) for n in range(2))
    every_slot_t = every_slot.T
    few = chunk if teams == 1 else LANES
    expert_steps = 2 * chunks * chunk // few

    def expert_grads(i):
        for part, body in ((1, beside_experts_first), (2, beside_experts_second)):
            pl.when(i == part * expert_steps // 3)(body)
        lanes = pl.ds(pl.multiple_of(i * few, few), few)
        value, grad = gelu_parts(dot(every_slot, ei[:, lanes]))
        g_pre = (dot_t(every_grad, eo[lanes, :]) * grad).astype(BF)
        expert_in_sum[:, lanes] = dot(every_slot_t, g_pre).astype(BF)
        expert_out_sum[lanes, :] = dot(value.astype(BF).T, every_grad).astype(BF)

    def beside_experts_first():
        attn_stage(0, 1, 1)
        dense[1].stage(3)
        dense[2].stage(3)

    def beside_experts_second():
        dense[0].stage(4)
        attn_stage(0, 0, 2)
        dense[1].stage(4)

    loop(expert_steps, expert_grads)

    last_copies = [local(0, expert_in_sum, expert_in_out), local(1, expert_out_sum, expert_out_out)]
    arrived(small_key + 1, small_in.at[2])
    small_parts[0] = small_in[1] + small_in[2]
    for k in range(1, team):
        send(small_key + 1 + k, small_parts.at[0], small_parts.at[k], mate(k)[0])
    dense[2].stage(4)
    dense[0].stage(5)
    attn_stage(0, 1, 2)
    dense[1].stage(5)
    dense[2].stage(5)

    for n, (source, dest) in enumerate(((act, act_out), (low, pg_out))):
        arrived(13 + n, edge_in.at[n])
        near = at(row_count - extra - tensor * (row_count - 2 * extra), extra)
        wide = jnp.concatenate([own[near]] * pairs, axis=1)
        source[near] = jnp.where(wide > 0.0, source[near].astype(F32), edge_in[n].astype(F32)).astype(BF)
        last_copies.append(local(2 + n, source.at[own_rows], dest))

    attn_stage(1, 0, 3)
    attn_stage(1, 1, 3)
    dense[0].stage(6)
    dense[1].stage(6)
    dense[2].stage(6)
    for k in range(1, team):
        arrived(small_key + 1 + k, small_parts.at[k])
    small_across[0] = sum([small_parts[k] for k in range(1, team)], start=small_parts[0])
    for k in range(1, teams):
        send(small_key + 1 + team + k, small_across.at[0], small_across.at[k], partner(k))
    for k in range(1, teams):
        arrived(small_key + 1 + team + k, small_across.at[k])
    small_out[...] = sum([small_across[k] for k in range(1, teams)], start=small_across[0])
    for q in range(chunks):
        dense[q].stage(7)
    send(mlp_key, mlp_sum.at[section], mlp_sum.at[section], core, mlp_like)
    arrived(mlp_key, mlp_sum.at[1 - section])
    for q in range(chunks):
        for n, dest in enumerate((mi_out, mot_out)):
            place_out = dest.at[:, q * chunk : (q + 1) * chunk]
            last_copies.append(local(4 + 2 * q + n, mlp_sum.at[n, q], place_out))
    attn_stage(0, 0, 3)
    attn_stage(0, 1, 3)
    used = 4 + 2 * chunks
    for c in range(3):
        first = c * 3 * HD
        main_rows, rest_rows = qkv_out.at[first : first + 2 * HD], qkv_out.at[first + 2 * HD : first + 3 * HD]
        last_copies.append(local(used + 2 * c, attn_sum.at[0, c * LANES : (c + 1) * LANES], main_rows))
        last_copies.append(local(used + 2 * c + 1, attn_sum.at[1, c * HD : (c + 1) * HD], rest_rows))
    last_copies.append(local(used + 6, attn_sum.at[1, 3 * HD :], attn_out))
    for found in last_copies:
        found.wait()

    for key, like in sent_off.items():
        copy(key, like, like, core).wait_send()


def compute(x_own, c_own, ids, gains, qkv, out, mi, mo, router, ei, eo):
    row_count, width = x_own.shape
    window = row_count + MOST // 2
    extra = window - row_count
    pairs = width // LANES
    ff = ei.shape[1]
    _, kept = bands(window)
    chunk_count = ff // 256
    chunks = chunk_count // 2
    vmem, hbm = pl.BlockSpec(memory_space=pltpu.VMEM), pl.BlockSpec(memory_space=pl.ANY)
    ranks = lax.axis_size("dp")
    team = min(8, ranks & -ranks)
    teams = ranks // team
    bits = [1 << n for n in range(team.bit_length() - 1)]
    spread = [bits[:1] + ["tensor"] + bits[1:], ["tensor"] + bits, bits[1::-1] + ["tensor"] + bits[2:]]
    mlp_orders = [spread[q % 3] for q in range(chunks)]
    boxes = []
    for order in mlp_orders:
        size = width
        for n, dim in enumerate(order):
            size = size if dim == "tensor" else size // 2
            boxes.append(pltpu.VMEM((2 if "tensor" in order[n + 1 :] else 1, size, 256), BF))
        boxes.append(pltpu.VMEM((teams, size, 256), BF))
    for _ in range(2):
        boxes.append(pltpu.VMEM((width, width), BF))
        boxes += [pltpu.VMEM((n, width // team, width), BF) for n in (team, teams)]
    copies = 18 + chunks * (2 * len(mlp_orders[0]) + teams) + 2 * (1 + 2 * team + teams) + 1 + 2 * (team + teams + 1)
    return pl.pallas_call(
        functools.partial(
            compute_kernel, team=team, teams=teams, mlp_orders=mlp_orders
        ),
        out_shape=(
            jax.ShapeDtypeStruct((row_count, width), BF),
            jax.ShapeDtypeStruct((row_count, width), BF),
            jax.ShapeDtypeStruct(qkv.shape, BF),
            jax.ShapeDtypeStruct(out.shape, BF),
            jax.ShapeDtypeStruct((width, ff // 2), BF),
            jax.ShapeDtypeStruct((width, ff // 2), BF),
            jax.ShapeDtypeStruct((width, ff), BF),
            jax.ShapeDtypeStruct((ff, width), BF),
            jax.ShapeDtypeStruct((8, width), F32),
        ),
        in_specs=[hbm, hbm, vmem, vmem, hbm, hbm, hbm, hbm, vmem, hbm, hbm],
        out_specs=[hbm] * 8 + [vmem],
        scratch_shapes=[
            pltpu.VMEM((window, width), BF),
            pltpu.VMEM((window, width), BF),
            pltpu.VMEM((2, 8, width), F32),
            pltpu.VMEM((2 * width, width), BF),
            pltpu.VMEM((2, 2 * width, width), BF),
            pltpu.VMEM((2 * width, width), BF),
            pltpu.VMEM((2, 3 * width, width), BF),
            pltpu.VMEM((2, width, width), BF),
            pltpu.VMEM((2, *mi.shape), BF),
            pltpu.VMEM((2, *mo.shape), BF),
            pltpu.VMEM(ei.shape, BF),
            pltpu.VMEM(eo.shape, BF),
            pltpu.VMEM(ei.shape, BF),
            pltpu.VMEM(eo.shape, BF),
            pltpu.VMEM((2, SLOTS, width), BF),
            pltpu.VMEM((window, width), BF),
            pltpu.VMEM((2, extra, width), BF),
            pltpu.VMEM((2, SLOTS, width), BF),
            pltpu.VMEM((2, SLOTS, width), BF),
            pltpu.VMEM((2, SLOTS, width), BF),
            pltpu.VMEM((2, SLOTS, width), BF),
            pltpu.VMEM((4, window, width), BF),
            pltpu.VMEM((window, width), F32),
            pltpu.VMEM((window, width), BF),
            pltpu.VMEM((window, width), F32),
            pltpu.VMEM((2, pairs, LANES, window), BF),
            pltpu.VMEM((2, pairs, LANES, window), BF),
            pltpu.VMEM((pairs, LANES, window), BF),
            pltpu.VMEM((2, pairs, window, LANES), BF),
            pltpu.VMEM((2, pairs, window, LANES), BF),
            pltpu.VMEM((2, pairs, LANES, window), BF),
            pltpu.VMEM((2, pairs, kept, 2 * LANES), BF),
            pltpu.VMEM((window, width), BF),
            pltpu.VMEM((chunk_count, window, 256), BF),
            pltpu.VMEM((chunk_count, window, 256), BF),
            pltpu.VMEM((window, width), F32),
            pltpu.VMEM((window, width), BF),
            pltpu.VMEM((pairs, LANES, window), BF),
            pltpu.VMEM((3 * LANES, window), BF),
            pltpu.VMEM((3 * pairs, window, LANES), BF),
            pltpu.VMEM((window, LANES), F32),
            pltpu.VMEM((window, LANES), F32),
            pltpu.VMEM((kept, LANES), F32),
            pltpu.VMEM((window, LANES), F32),
            pltpu.VMEM((2, 2 * SLOTS, window), BF),
            pltpu.VMEM((SLOTS, ff), F32),
            pltpu.VMEM((2, SLOTS, width), BF),
            pltpu.VMEM((2, SLOTS, width), BF),
            pltpu.VMEM((2, 2, 2, width, width), BF),
            pltpu.VMEM((2, width, width), BF),
            pltpu.VMEM((2, 2, chunks, width, 256), BF),
            pltpu.VMEM((chunks, 2, width, 256), BF),
            pltpu.VMEM((2, chunks, width, 256), BF),
            pltpu.VMEM((8, width), F32),
            pltpu.VMEM((3, 8, width), F32),
            pltpu.VMEM((team, 8, width), F32),
            pltpu.VMEM((teams, 8, width), F32),
            pltpu.VMEM((2, teams, team, 2 * IMAGES, width), BF),
            pltpu.VMEM((2 * IMAGES, width), BF),
            pltpu.SemaphoreType.DMA((copies,)),
            pltpu.SemaphoreType.DMA((copies,)),
            pltpu.SemaphoreType.DMA((11 + 2 * chunks,)),
            *boxes,
        ],
        compiler_params=pltpu.CompilerParams(
            vmem_limit_bytes=62 * 1024 * 1024, collective_id=0, has_side_effects=True
        ),
    )(x_own, c_own, ids, gains, qkv, out, mi, mo, router, ei, eo)


def finish_kernel(
    act, pg, qkv, attn, mi, mot, expert_in, expert_out, small,
    act_out, pg_out, gains_out, qkv_out, attn_out, mi_out, mo_out, router_out, expert_in_out, expert_out_out,
):
    section, tensor = lax.axis_index("section"), lax.axis_index("tensor")
    act_out[...] = act[...]
    pg_out[...] = pg[...]
    gains_out[...] = jnp.where(section == 0, small[0:2], small[2:4])
    router_out[...] = jnp.where(tensor == 0, small[4:5], small[5:6])
    pairs = ((qkv, qkv_out), (attn, attn_out), (mi, mi_out), (expert_in, expert_in_out), (expert_out, expert_out_out))
    for source, dest in pairs:
        dest[...] = source[...].astype(F32)
    mo_out[...] = mot[...].astype(F32).T


def finish(act, pg, qkv, attn, mi, mot, expert_in, expert_out, small):
    steps = 3

    def by_rows(a):
        return pl.BlockSpec((a.shape[0] // steps, a.shape[1]), lambda i: (i, 0))

    def whole(a):
        return pl.BlockSpec(a.shape, lambda i: (0, 0))

    def like(a):
        return jax.ShapeDtypeStruct(a.shape, F32)

    gains = jax.ShapeDtypeStruct((2, act.shape[1]), F32)
    router = jax.ShapeDtypeStruct((1, act.shape[1]), F32)
    mo = jax.ShapeDtypeStruct(mot.shape[::-1], F32)
    mot_spec = pl.BlockSpec((mot.shape[0], mot.shape[1] // steps), lambda i: (0, i))
    return pl.pallas_call(
        finish_kernel,
        grid=(steps,),
        out_shape=(
            act, pg, gains, like(qkv), like(attn), like(mi), mo, router, like(expert_in), like(expert_out)
        ),
        in_specs=[
            whole(act), whole(pg), by_rows(qkv), by_rows(attn), by_rows(mi), mot_spec, by_rows(expert_in),
            by_rows(expert_out), whole(small),
        ],
        out_specs=[
            whole(act), whole(pg), whole(gains), by_rows(qkv), by_rows(attn), by_rows(mi), by_rows(mo), whole(router),
            by_rows(expert_in), by_rows(expert_out),
        ],
        compiler_params=pltpu.CompilerParams(vmem_limit_bytes=60 * 1024 * 1024),
    )(act, pg, qkv, attn, mi, mot, expert_in, expert_out, small)


def per_device(
    patches, image_ids, cotangent, norm_gains, qkv_weight, out_weight, mlp_in, mlp_out, router, expert_in, expert_out
):
    width = patches.shape[2]
    part = qkv_weight.shape[3]
    qkv = jnp.transpose(qkv_weight[0], (1, 2, 0)).reshape(-1, width)
    results = compute(
        patches[0], cotangent[0], image_ids, norm_gains[0], qkv, out_weight[0], mlp_in, mlp_out, router.T,
        expert_in[0], expert_out[0],
    )
    act, pg, gains, qkv_grad, out_grad, mi_grad, mo_grad, router_grad, ei_grad, eo_grad = finish(*results)
    qkv_grad = jnp.transpose(qkv_grad.reshape(3, part, width), (2, 0, 1))
    return (
        act[None], pg[None], gains[None], qkv_grad[None], out_grad[None], mi_grad, mo_grad, router_grad.T,
        ei_grad[None], eo_grad[None],
    )


def solution(mesh):
    return jax.shard_map(
        per_device,
        mesh=mesh,
        in_specs=(
            P(("dp", "section"), "tensor", None),
            P("dp", None),
            P(("dp", "section"), "tensor", None),
            P("section", None, None),
            P("section", None, None, "tensor"),
            P("section", "tensor", None),
            P(None, "tensor"),
            P("tensor", None),
            P(None, "tensor"),
            P("tensor", None, None),
            P("tensor", None, None),
        ),
        out_specs=(
            P(("dp", "section"), "tensor", None),
            P(("dp", "section"), "tensor", None),
            P("section", None, None),
            P("section", None, None, "tensor"),
            P("section", "tensor", None),
            P(None, "tensor"),
            P("tensor", None),
            P(None, "tensor"),
            P("tensor", None, None),
            P("tensor", None, None),
        ),
        check_vma=False,
    )
```

```python
import functools

import jax
import jax.numpy as jnp
from jax import lax
from jax.experimental import pallas as pl
from jax.experimental.pallas import tpu as pltpu
from jax.sharding import PartitionSpec as P

HD = 64
IMAGES = 8
MOST = 256
LANES = 128
SLOTS = 16
EPSILON = 1e-06
BF = jnp.bfloat16
F32 = jnp.float32


def dot(a, b):
    return jnp.dot(a, b, preferred_element_type=F32)


def dot_t(a, b):
    return lax.dot_general(a, b, (((1,), (1,)), ((), ())), preferred_element_type=F32)


def t_dot(a, b):
    return lax.dot_general(a, b, (((0,), (0,)), ((), ())), preferred_element_type=F32)


def normalise(x):
    centred = x - jnp.mean(x, axis=-1, keepdims=True)
    scale = lax.rsqrt(jnp.mean(centred * centred, axis=-1, keepdims=True) + EPSILON)
    return centred * scale, scale


def norm_back(x, gain, gz):
    unit, scale = normalise(x)
    scaled = gz * gain
    mean_plain = jnp.mean(scaled, axis=-1, keepdims=True)
    mean_unit = jnp.mean(scaled * unit, axis=-1, keepdims=True)
    return scale * (scaled - mean_plain - unit * mean_unit), jnp.sum(gz * unit, axis=0, keepdims=True)


def gelu_parts(u):
    cdf = 0.5 * (1.0 + lax.erf(u * 0.7071067811865476))
    return u * cdf, cdf + u * (0.3989422804014327 * jnp.exp(-0.5 * u * u))


def pair_up(tile):
    row = lax.broadcasted_iota(jnp.int32, tile.shape, 0)
    zero = jnp.zeros_like(tile)
    return jnp.concatenate([jnp.where(row < HD, tile, zero), jnp.where(row >= HD, tile, zero)], axis=1)


def pair_down(both):
    n = both.shape[1] // 2
    row = lax.broadcasted_iota(jnp.int32, (both.shape[0], n), 0)
    return jnp.where(row < HD, both[:, :n], both[:, n:])


def bands(window):
    reach = MOST // LANES
    found, at = [], 0
    for i in range(window // LANES):
        first = max(0, i - reach) * LANES
        count = min(window, (i + reach + 1) * LANES) - first
        found.append((i * LANES, first, count, at))
        at += count
    return found, at


MESH = pl.DeviceIdType.MESH


def compute_kernel(
    x_own, c_own, ids, gains_own, qkv_own, out_own, mi_own, mo_own, router_own, ei_own, eo_own,
    act_out, pg_out, qkv_out, attn_out, mi_out, mot_out, expert_in_out, expert_out_out, small_out,
    xw, cw, gains, wy, wc, w_own, wqkv, wo, mi, mo, ei, eo, expert_in_sum, expert_out_sum, routert, act, edge_in, slots, geos, slot_in, pack,
    z, x1, sent, x3, qt, kt, vt, kr, vr, ot, pt, tok, hidden, slope, gx, low, got, gt, gtok, gk_sum, gv_sum,
    gz_all, veil, shares, own, mixing, eslope, eout, gslot, grad_attn, attn_sum, grad_mlp, mlp_core, mlp_sum,
    small, small_in, small_parts, small_across, packs, small_pack, send_sem, recv_sem, here_sem,
    *boxes, team, teams, mlp_orders,
):
    row_count, width = x_own.shape
    window = xw.shape[0]
    extra = window - row_count
    half = window // 2
    pairs = width // LANES
    total = ids.shape[1]
    dp = lax.axis_index("dp")
    section = lax.axis_index("section")
    tensor = lax.axis_index("tensor")
    core = (dp, 1 - section, tensor)
    beside = (dp, section, 1 - tensor)

    spot = lax.rem(dp, team)
    this_team = dp // team

    def mate(k):
        place, bit = spot, 1
        while bit < team:
            if k & bit:
                place = jnp.where(lax.rem(spot // bit, 2) == 0, place + bit, place - bit)
            bit *= 2
        return (dp - spot + place, section, tensor), place

    def partner(k):
        return (lax.rem(dp + k * team, team * teams), section, tensor)

    blocks, _ = bands(window)
    row_blocks = window // LANES

    def at(start, size, step=LANES):
        return pl.ds(pl.multiple_of(start, step), size)

    def rows(i, n=LANES):
        return pl.ds(pl.multiple_of(i * n, n), n)

    def loop(n, body):
        def step(i, carry):
            body(i)
            return carry

        lax.fori_loop(0, n, step, 0)

    sent_off = {}

    def copy(key, source, dest, device):
        return pltpu.make_async_remote_copy(
            src_ref=source,
            dst_ref=dest,
            send_sem=send_sem.at[key],
            recv_sem=recv_sem.at[key],
            device_id=device,
            device_id_type=MESH,
        )

    def send(key, source, dest, device, like=None):
        copy(key, source, dest, device).start()
        sent_off[key] = source if like is None else like

    def arrived(key, dest):
        copy(key, dest, dest, core).wait_recv()

    def only(which):
        return pl.when(section == which)

    barrier = pltpu.get_barrier_semaphore()
    neighbours = [core, beside] + [mate(k)[0] for k in range(1, team)] + [partner(k) for k in range(1, teams)]
    for device in neighbours:
        pl.semaphore_signal(barrier, inc=1, device_id=device, device_id_type=MESH)

    def local(key, source, dest):
        found = pltpu.make_async_copy(source, dest, here_sem.at[key])
        found.start()
        return found

    qkv_rows = qkv_own.shape[0]
    own_rows = at(tensor * extra, row_count)
    near_copies = [
        local(0, x_own, xw.at[own_rows]),
        local(1, qkv_own, w_own.at[:qkv_rows]),
        local(2, out_own, w_own.at[qkv_rows:]),
    ]
    later_copies = [
        local(3, mi_own, mi.at[tensor]),
        local(4, mo_own, mo.at[tensor]),
        local(5, c_own, cw.at[own_rows]),
        local(6, ei_own, ei),
        local(7, eo_own, eo),
    ]
    gains[section, :2] = gains_own[...]
    first_row = lax.broadcasted_iota(jnp.int32, (SLOTS, width), 0) == 0
    router_rows = jnp.broadcast_to(router_own[...].astype(F32), (SLOTS, width))
    routert[tensor] = jnp.where(first_row, router_rows, 0.0).astype(BF)
    pl.semaphore_wait(barrier, len(neighbours))

    qkv_here, out_here = wy.at[:qkv_rows], wy.at[qkv_rows:]
    qkv_near, out_near = wc.at[0, :qkv_rows], wc.at[0, qkv_rows:]
    qkv_far, out_far = wc.at[1, :qkv_rows], wc.at[1, qkv_rows:]

    edge = x_own.at[at((1 - tensor) * (row_count - extra), extra)]
    send(0, edge, xw.at[at(tensor * row_count, extra)], beside)

    @only(0)
    def _():
        send(3, qkv_own, qkv_here, beside)
        send(15, out_own, out_here, beside)
        send(5, mi_own, mi.at[tensor], beside)

    send(1, gains.at[section], gains.at[section], core)
    send(2, qkv_own, qkv_near, core)
    send(16, out_own, out_near, core)

    ids_row = ids[pl.ds(section, 1), :].astype(F32)
    image = lax.broadcasted_iota(jnp.int32, (SLOTS, total), 0).astype(F32)
    spread = jnp.broadcast_to(ids_row, (SLOTS, total))
    middle = jnp.sum((spread < image).astype(F32) + (spread <= image).astype(F32), axis=1, keepdims=True)
    first_half = (middle < total).astype(F32)
    mine = jnp.where(tensor == 0, first_half, 1.0 - first_half)
    window_ids = ids[pl.ds(section, 1), at(tensor * (total - window), window)].astype(F32)
    member = (jnp.broadcast_to(window_ids, (SLOTS, window)) == image[:, :window]).astype(F32)
    member_own = member * mine
    own_row = jnp.sum(member_own, axis=0, keepdims=True)
    own[...] = jnp.broadcast_to(own_row, (LANES, window)).T
    blank = jnp.zeros((LANES - SLOTS, window), F32)
    image_of = jnp.concatenate([member, blank], axis=0).T.astype(BF)
    for b in range(2):
        for j in range(pairs):
            kr[b, j, :, LANES:] = image_of
    veil[...] = jnp.concatenate([(1.0 - member) * -1e30, blank], axis=0).astype(BF)

    def place(source, b, t, kinds=(0, 1, 2, 3)):
        for c in kinds:
            first = c * 3 * HD
            if c < 3:
                own_pair, mixed_pair, dest = t * width + c * LANES, 2 * width + c * LANES + t * HD, wqkv
            else:
                own_pair, mixed_pair, dest = t * LANES, 2 * LANES + t * HD, wo
            dest[b, at(own_pair, 2 * HD)] = source[first : first + 2 * HD]
            dest[b, at(mixed_pair, HD, HD)] = source[first + 2 * HD : first + 3 * HD]

    for found in near_copies:
        found.wait()
    place(w_own, section, tensor)
    arrived(1, gains.at[1 - section])
    arrived(2, qkv_near)
    arrived(16, out_near)
    place(wc.at[0], 1 - section, tensor)
    arrived(0, xw.at[at((1 - tensor) * row_count, extra)])


    def first_far():
        @only(0)
        def _():
            arrived(3, qkv_here)
            send(4, qkv_here, qkv_far, core)
            place(wy, 0, 1 - tensor, (0, 1, 2))

        @only(1)
        def _():
            arrived(4, qkv_far)
            send(5, mo_own, mo.at[tensor], beside)
            place(wc.at[1], 0, 1 - tensor, (0, 1, 2))

    def second_far():
        @only(0)
        def _():
            arrived(4, qkv_far)
            place(wc.at[1], 1, 1 - tensor, (0, 1, 2))

        @only(1)
        def _():
            arrived(3, qkv_here)
            send(4, qkv_here, qkv_far, core)
            place(wy, 1, 1 - tensor, (0, 1, 2))

    def first_out():
        @only(0)
        def _():
            arrived(15, out_here)
            send(17, out_here, out_far, core)
            place(wy, 0, 1 - tensor, (3,))

        @only(1)
        def _():
            arrived(17, out_far)
            send(3, qkv_own, qkv_here, beside)
            send(15, out_own, out_here, beside)
            place(wc.at[1], 0, 1 - tensor, (3,))

    def second_out():
        @only(0)
        def _():
            arrived(17, out_far)
            place(wc.at[1], 1, 1 - tensor, (3,))

        @only(1)
        def _():
            arrived(15, out_here)
            send(17, out_here, out_far, core)
            place(wy, 1, 1 - tensor, (3,))

    def add_across(first, piece, heard):
        if teams == 1:
            return
        for k in range(1, teams):
            copy(first + k, piece, heard.at[k], partner(k)).start()
        whole = piece[...].astype(F32)
        for k in range(1, teams):
            arrived(first + k, heard.at[k])
            copy(first + k, piece, heard.at[k], partner(k)).wait_send()
            whole = whole + heard[k].astype(F32)
        piece[...] = whole.astype(BF)

    class Cube:
        def __init__(self, key, pick, core_in, total, order, boxes):
            self.key, self.pick, self.core_in, self.total, self.order = key, pick, core_in, total, order
            self.boxes, self.across = boxes[:-1], boxes[-1]
            start, size, self.plan = 0, total.shape[0], []
            for dim in order:
                if dim == "tensor":
                    self.plan.append((dim, start, size, start))
                else:
                    size //= 2
                    bit = lax.rem(spot // dim, 2)
                    self.plan.append((dim, start + bit * size, size, start + (1 - bit) * size))
                    start = start + bit * size
            self.back = [(i, *step) for i, step in enumerate(self.plan) if step[0] != "tensor"][::-1]
            self.like = {size: total.at[:size] for _, _, _, size, _ in self.back}
            self.along = order.index("tensor")

        def to_core(self, source):
            send(self.key, source, self.core_in, core, self.core_in)

        def add(self, parts, start, size, box):
            for n, part in enumerate(parts):
                kept = self.pick(part, at(start, size, 16))
                kept[...] = (kept[...].astype(F32) + box[n].astype(F32)).astype(BF)

        def stage(self, k):
            steps, rounds = len(self.plan), len(self.back)
            both = (0, 1)
            if k == 0:
                arrived(self.key, self.core_in)
                self.add(both, 0, self.total.shape[0], self.core_in)
            elif k <= steps:
                _, start, size, _ = self.plan[k - 1]
                arrived(self.key + k, self.boxes[k - 1])
                self.add((tensor,) if self.along < k else both, start, size, self.boxes[k - 1])
            else:
                _, _, _, size, start = self.back[k - steps - 1]
                arrived(self.key + k, self.total.at[at(start, size, 16)])
            if k < steps:
                dim, _, size, start = self.plan[k]
                if dim == "tensor":
                    device = beside
                    source = self.pick(pl.ds(1 - tensor, 1), at(start, size, 16))
                else:
                    device = mate(dim)[0]
                    parts = pl.ds(tensor, 1) if self.along < k else slice(None)
                    source = self.pick(parts, at(start, size, 16))
                send(self.key + k + 1, source, self.boxes[k], device, self.boxes[k])
            elif k == steps:
                _, start, size, _ = self.plan[-1]
                piece = self.total.at[at(start, size, 16)]
                piece[...] = self.pick(tensor, at(start, size, 16))[...]
                add_across(self.key + Cube.stages, piece, self.across)
            if steps <= k < steps + rounds:
                _, dim, start, size, _ = self.back[k - steps]
                region = self.total.at[at(start, size, 16)]
                send(self.key + k + 1, region, region, mate(dim)[0], self.like[size])

        stages = len(mlp_orders[0]) * 2
        keys = stages + teams

    class Straight:
        def __init__(self, key, pick, core_in, total, boxes):
            self.key, self.pick, self.core_in, self.total = key, pick, core_in, total
            self.beside_in, self.parts, self.across = boxes
            self.size = total.shape[0] // team
            self.like = total.at[: self.size]

        def part(self, place):
            return at(place * self.size, self.size, 16)

        def to_core(self, source):
            send(self.key, source, self.core_in, core, self.core_in)

        def stage(self, k):
            every = pl.ds(0, self.total.shape[0])
            near = self.pick(tensor, every)
            if k == 0:
                arrived(self.key, self.core_in)
                far = self.pick(1 - tensor, every)
                far[...] = (far[...].astype(F32) + self.core_in[1 - tensor].astype(F32)).astype(BF)
                send(self.key + 1, far, self.beside_in, beside, self.beside_in)
            if k == 1:
                arrived(self.key + 1, self.beside_in)
                both = near[...].astype(F32) + self.core_in[tensor].astype(F32)
                near[...] = (both + self.beside_in[...].astype(F32)).astype(BF)
                for n in range(1, team):
                    device, place = mate(n)
                    source = self.pick(tensor, self.part(place))
                    send(self.key + 1 + n, source, self.parts.at[n], device, self.like)
            if k == 2:
                whole = self.pick(tensor, self.part(spot))[...].astype(F32)
                for n in range(1, team):
                    arrived(self.key + 1 + n, self.parts.at[n])
                    whole = whole + self.parts[n].astype(F32)
                piece = self.total.at[self.part(spot)]
                piece[...] = whole.astype(BF)
                add_across(self.key + 1 + 2 * team, piece, self.across)
                for n in range(1, team):
                    send(self.key + 1 + team + n, piece, piece, mate(n)[0], self.like)
            if k == 3:
                for n in range(1, team):
                    arrived(self.key + 1 + team + n, self.total.at[self.part(mate(n)[1])])

        keys = 1 + 2 * team + teams

    chunks = len(mlp_orders)
    key, taken = 18, 0

    def boxes_of(count):
        nonlocal taken
        taken += count
        return boxes[taken - count : taken]

    def mlp_pick(q):
        return lambda parts, where: grad_mlp.at[section, parts, q, where]

    def attn_pick(n):
        return lambda parts, where: grad_attn.at[section, parts, n, where]

    dense, attn = [], []
    for q in range(chunks):
        total_of = mlp_sum.at[section, q]
        found = boxes_of(len(mlp_orders[q]) + 1)
        dense.append(Cube(key, mlp_pick(q), mlp_core.at[q], total_of, mlp_orders[q], found))
        key += Cube.keys
    for n in range(2):
        heard = wc.at[:, n * width : (n + 1) * width]
        attn.append(Straight(key, attn_pick(n), heard, attn_sum.at[n], boxes_of(3)))
        key += Straight.keys
    mlp_key, pack_key, small_key = key, key + chunks, key + chunks + team + teams
    mlp_like = mlp_sum.at[0, 0]

    def give_attn(b, n):
        @only(1 - b)
        def _():
            attn[n].to_core(grad_attn.at[b, :, n])

    def attn_stage(b, n, k):
        @only(b)
        def _():
            attn[n].stage(k)

    def give_dense(q):
        dense[q].to_core(grad_mlp.at[1 - section, :, q])

    def attention(b, x_of, out_ref, ahead_of_far, ahead_of_out):
        def norm(i):
            unit, _ = normalise(x_of(rows(i)))
            z[2 * b, rows(i)] = (unit * gains[b, 0:1, :]).astype(BF)

        loop(row_blocks, norm)

        def pair(n):
            pl.when(n == 1)(ahead_of_far)
            j = jnp.where(n == 0, tensor, jnp.where(n == 1, 1 - tensor, n))
            zz, weights = z[2 * b], wqkv.at[b, at(j * width, width)]
            flat = dot_t(zz, weights[...])
            qt[b, j] = (flat[:, :LANES] * HD**-0.5).astype(BF).T
            keys, values = flat[:, LANES : 2 * LANES].astype(BF), flat[:, 2 * LANES :].astype(BF)
            kr[b, j, :, :LANES] = keys
            vr[b, j] = values
            kt[b, j] = keys.T
            vt[...] = values.T
            for q0, k0, count, kept in blocks:
                queries = pair_up(qt[b, j, :, q0 : q0 + LANES])
                hidden_part = veil[:, q0 : q0 + LANES]
                queries = jnp.concatenate([queries, jnp.concatenate([hidden_part, hidden_part], axis=1)], axis=0)
                scores = dot(kr[b, j, k0 : k0 + count, :], queries)
                powers = jnp.exp(scores - jnp.max(scores, axis=0, keepdims=True))
                inverse = 1.0 / jnp.sum(powers, axis=0, keepdims=True)
                low_powers = powers.astype(BF)
                pt[b, j, kept : kept + count, :] = low_powers
                shares[b, j, q0 // LANES : q0 // LANES + 1, :] = inverse
                mixed = dot(vt[:, k0 : k0 + count], low_powers) * inverse
                ot[b, j, :, q0 : q0 + LANES] = pair_down(mixed).astype(BF)

        loop(pairs, pair)
        for j in range(pairs):
            tok[:, j * LANES : (j + 1) * LANES] = ot[b, j].T

        ahead_of_out()

        out_ref[...] = x_of(slice(None)) + dot(tok[...], wo[b])

    def attention_back(b, x_of, beside_pairs, after_pairs):
        ga = low[...]
        got[...] = dot_t(wo[b], ga).astype(BF).reshape(pairs, LANES, window)
        pieces = dot(ot[b].reshape(width, window), ga).astype(BF)
        for t in range(2):
            grad_attn[b, t, 1, 3 * HD : 5 * HD, :] = pieces[t * LANES : (t + 1) * LANES]
            grad_attn[b, t, 1, 5 * HD : 6 * HD, :] = pieces[2 * LANES + t * HD : 2 * LANES + (t + 1) * HD]
        def pair(j):
            gk_sum[...] = jnp.zeros_like(gk_sum)
            gv_sum[...] = jnp.zeros_like(gv_sum)
            for q0, k0, count, kept in blocks:
                for (at_pair, at_query), body in beside_pairs.items():
                    if at_query == q0 // LANES:
                        pl.when(j == at_pair)(body)
                inverse = shares[b, j, q0 // LANES : q0 // LANES + 1, :]
                go_pair = (pair_up(got[j, :, q0 : q0 + LANES]).astype(F32) * inverse).astype(BF)
                q_pair = pair_up(qt[b, j, :, q0 : q0 + LANES])
                low_powers = pt[b, j, kept : kept + count, :]
                powers = low_powers.astype(F32)
                weighted = dot(vr[b, j, k0 : k0 + count, :], go_pair) * powers
                inner = jnp.sum(weighted, axis=0, keepdims=True) * inverse
                gs = (weighted - powers * inner).astype(BF)
                gq = pair_down(dot(kt[b, j, :, k0 : k0 + count], gs)) * HD**-0.5
                gt[:LANES, q0 : q0 + LANES] = gq.astype(BF)
                gk_sum[k0 : k0 + count] += dot_t(gs, q_pair)
                gv_sum[k0 : k0 + count] += dot_t(low_powers, go_pair)
            gtok[3 * j] = gt[:LANES].T
            for c, total_of in ((1, gk_sum), (2, gv_sum)):
                low_sum = total_of[...].astype(BF)
                gtok[3 * j + c] = low_sum
                gt[c * LANES : (c + 1) * LANES] = low_sum.T
            pieces = dot(gt[...], z[2 * b]).astype(BF)

            @pl.when(j < 2)
            def _():
                grad_attn[b, j, 0] = pieces

            @pl.when(j == 2)
            def _():
                for c in range(3):
                    for t in range(2):
                        first = c * LANES + t * HD
                        grad_attn[b, t, 1, c * HD : (c + 1) * HD, :] = pieces[first : first + HD]

        loop(pairs, pair)
        after_pairs()
        gain = gains[b, 0:1, :]

        def back(i, gain_grad):
            wide = jnp.concatenate([gtok[c, rows(i, half)] for c in range(3 * pairs)], axis=1)
            step, part = norm_back(x_of(rows(i, half)), gain, dot(wide, wqkv[b]))
            gx[rows(i, half)] += step
            return gain_grad + part

        small[2 * b : 2 * b + 1, :] = lax.fori_loop(0, 2, back, jnp.zeros((1, width), F32))

    attention(0, lambda r: xw[r].astype(F32), x1, first_far, first_out)

    def norm_middle(source, which):
        def body(i):
            unit, _ = normalise(source[rows(i)])
            z[which, rows(i)] = (unit * gains[which // 2, 1:2, :]).astype(BF)

        loop(row_blocks, body)

    norm_middle(x1, 1)

    for found in later_copies:
        found.wait()

    def far_hidden():
        @only(0)
        def _():
            arrived(5, mi.at[1 - tensor])
            send(6, mi.at[1 - tensor], mi.at[1 - tensor], core, mi_own)

        @only(1)
        def _():
            arrived(5, mo.at[1 - tensor])
            send(6, mo.at[1 - tensor], mo.at[1 - tensor], core, mo_own)
            arrived(6, mi.at[1 - tensor])

    chunk = 256

    def hidden_chunk(n):
        pl.when(n == chunks)(far_hidden)
        q = lax.rem(n, chunks)
        part, first = jnp.where(n < chunks, tensor, 1 - tensor), pl.multiple_of(q * chunk, chunk)
        value, grad = gelu_parts(dot(z[1], mi[part, :, pl.ds(first, chunk)]))
        hidden[part * chunks + q] = value.astype(BF)
        slope[part * chunks + q] = grad.astype(BF)

    loop(2 * chunks, hidden_chunk)

    @only(0)
    def _():
        arrived(6, mo.at[1 - tensor])

    h = jnp.concatenate([hidden[c] for c in range(2 * chunks)], axis=1)
    sent[...] = (x1[...] + dot(h, mo[...].reshape(-1, width))).astype(BF)

    c_edge = c_own.at[at((1 - tensor) * (row_count - extra), extra)]
    send(7, c_edge, cw.at[at(tensor * row_count, extra)], beside)
    send(8, routert.at[tensor], routert.at[tensor], beside)

    attention(1, lambda r: sent[r].astype(F32), x3, second_far, second_out)
    norm_middle(x3, 3)
    z3 = z[3]
    arrived(8, routert.at[1 - tensor])
    powers = [jnp.exp(dot_t(routert[e], z3)[:1]) for e in range(2)]
    dispatch, combine = [], []
    for e in range(2):
        totals = jnp.sum(member * powers[e], axis=1, keepdims=True)
        dispatch.append(powers[e] / jnp.sum(member * totals, axis=0, keepdims=True))
        combine.append(powers[e] / (powers[0] + powers[1]))
        d_low = (member_own * dispatch[e].astype(BF).astype(F32)).astype(BF)
        c_low = (member * combine[e].astype(BF).astype(F32)).astype(BF)
        mixing[0, e * SLOTS : (e + 1) * SLOTS] = d_low
        mixing[1, e * SLOTS : (e + 1) * SLOTS] = c_low
        slots[e] = dot(d_low, z3).astype(BF)
    send(9, slots.at[1 - tensor], slot_in.at[0], beside)
    arrived(7, cw.at[at((1 - tensor) * row_count, extra)])

    def mask(i):
        wide = jnp.concatenate([own[rows(i)]] * pairs, axis=1)
        low[rows(i)] = jnp.where(wide > 0.0, cw[rows(i)].astype(F32), 0.0).astype(BF)

    loop(row_blocks, mask)
    gy = low[...]
    for e in range(2):
        geos[e] = dot(mixing[1, e * SLOTS : (e + 1) * SLOTS], gy).astype(BF)
    send(10, geos.at[1 - tensor], slot_in.at[1], beside)

    arrived(9, slot_in.at[0])
    pack[0] = slots[tensor] + slot_in[0]
    value, grad = gelu_parts(dot(pack[0], ei[...]))
    eslope[...] = grad
    eout[tensor] = dot(value.astype(BF), eo[...]).astype(BF)
    send(11, eout.at[tensor], eout.at[tensor], beside)
    arrived(10, slot_in.at[1])
    pack[1] = geos[tensor] + slot_in[1]
    g_hidden = dot_t(pack[1], eo[...])
    gslot[tensor] = dot_t((g_hidden * eslope[...]).astype(BF), ei[...]).astype(BF)
    send(12, gslot.at[tensor], gslot.at[tensor], beside)
    arrived(11, eout.at[1 - tensor])
    outputs = eout[...].reshape(2 * SLOTS, width)

    def finish(i):
        mixed = t_dot(mixing[1, :, rows(i)], outputs)
        act[rows(i)] = (x3[rows(i)] + mixed).astype(BF)

    loop(row_blocks, finish)
    send(13, act.at[at((1 - tensor) * row_count, extra)], edge_in.at[0], beside)

    all_packs, team_like = packs.at[0], packs.at[0, 0]

    def share_slots():
        halves = [pack[n].astype(F32)[:IMAGES] for n in range(2)]
        small_pack[...] = jnp.concatenate(halves, axis=0).astype(BF)
        for k in range(1, team):
            send(pack_key + k, small_pack, packs.at[0, this_team, spot], mate(k)[0], small_pack)

    def gather_slots():
        for k in range(1, team):
            arrived(pack_key + k, packs.at[0, this_team, mate(k)[1]])
        packs[0, this_team, spot] = small_pack[...]
        for k in range(1, teams):
            team_packs = packs.at[0, this_team]
            send(pack_key + team + k, team_packs, team_packs, partner(k), team_like)
        for k in range(1, teams):
            arrived(pack_key + team + k, packs.at[0, lax.rem(this_team + k, teams)])
        send(pack_key, packs.at[0], packs.at[1], core, all_packs)

    per_token = [jnp.sum(dot_t(eout[e], gy) * member, axis=0, keepdims=True) for e in range(2)]
    inner = combine[0] * per_token[0] + combine[1] * per_token[1]
    arrived(12, gslot.at[1 - tensor])
    logit_grads = []
    for e in range(2):
        g_dispatch = jnp.sum(dot_t(gslot[e], z3) * member_own, axis=0, keepdims=True)
        weighted = dispatch[e] * g_dispatch
        sums = jnp.sum(member * weighted, axis=1, keepdims=True)
        from_dispatch = weighted - dispatch[e] * jnp.sum(member * sums, axis=0, keepdims=True)
        logit_grads.append(combine[e] * (per_token[e] - inner) + from_dispatch)
    which_row = lax.broadcasted_iota(jnp.int32, (SLOTS, width), 0)
    router_rows = jnp.where(
        which_row == 0,
        jnp.broadcast_to(routert[0].astype(F32)[:1], (SLOTS, width)),
        jnp.where(which_row == 1, jnp.broadcast_to(routert[1].astype(F32)[:1], (SLOTS, width)), 0.0),
    ).astype(BF)
    which = lax.broadcasted_iota(jnp.int32, (SLOTS, window), 0)
    logit_grad = jnp.where(which == 0, logit_grads[0], jnp.where(which == 1, logit_grads[1], 0.0)).astype(BF)
    small[4:6, :] = dot(logit_grad, z3)[:2]
    small[6:8, :] = jnp.zeros((2, width), F32)
    mixing[1, :SLOTS] = logit_grad
    slots_and_router = jnp.concatenate([gslot[0], gslot[1], router_rows], axis=0)

    def experts_back(i, gain_grad):
        at = pl.ds(pl.multiple_of(i * LANES, LANES), LANES)
        parts = jnp.concatenate([mixing[0, :, at], mixing[1, :SLOTS, at]], axis=0)
        step, part = norm_back(x3[rows(i)], gains[1, 1:2, :], t_dot(parts, slots_and_router))
        total_of = low[rows(i)].astype(F32) + step
        gx[rows(i)] = total_of
        low[rows(i)] = total_of.astype(BF)
        return gain_grad + part

    small[3:4, :] = lax.fori_loop(0, row_blocks, experts_back, jnp.zeros((1, width), F32))

    def shares_second():
        gather_slots()
        give_attn(1, 0)

    share_slots()
    attention_back(1, lambda r: sent[r].astype(F32), {(2, 0): shares_second}, lambda: give_attn(1, 1))

    low[...] = gx[...].astype(BF)
    gsent = low[...]
    gsent_t = gsent.T
    z2 = z[1]
    z2_t = z2.T

    def hidden_back(n):
        for ahead, body in ((2, dense_first), (4, dense_second)):
            pl.when(n == ahead)(body)
        q, part = n // 2, lax.rem(n, 2)
        i, first = part * chunks + q, pl.multiple_of(q * chunk, chunk)
        grad_mlp[1, part, q] = dot(gsent_t, hidden[i]).astype(BF)
        g_hidden = dot_t(gsent, mo[part, pl.ds(first, chunk), :])
        g_pre = (g_hidden * slope[i].astype(F32)).astype(BF)
        hidden[i] = g_pre
        grad_mlp[0, part, q] = dot(z2_t, g_pre).astype(BF)

    def dense_first():
        give_dense(0)
        attn_stage(1, 0, 0)

    def dense_second():
        give_dense(1)
        attn_stage(1, 1, 0)
        dense[0].stage(0)

    loop(2 * chunks, hidden_back)
    give_dense(2)
    dense[1].stage(0)

    def dense_back(i, gain_grad):
        gz = jnp.zeros((half, width), F32)
        for part in range(2):
            g = jnp.concatenate([hidden[part * chunks + c, rows(i, half)] for c in range(chunks)], axis=1)
            gz = gz + dot_t(g, mi[part])
        step, part = norm_back(x1[rows(i, half)], gains[0, 1:2, :], gz)
        total_of = low[rows(i, half)].astype(F32) + step
        gx[rows(i, half)] = total_of
        low[rows(i, half)] = total_of.astype(BF)
        return gain_grad + part

    small[1:2, :] = lax.fori_loop(0, 2, dense_back, jnp.zeros((1, width), F32))

    dense[2].stage(0)
    attn_stage(1, 0, 1)

    def beside_first():
        dense[0].stage(1)
        attn_stage(1, 1, 1)

    def beside_third():
        give_attn(0, 0)
        attn_stage(1, 0, 2)
        dense[0].stage(2)

    def beside_last():
        dense[1].stage(2)
        attn_stage(0, 0, 0)

    def beside_rest():
        give_attn(0, 1)
        attn_stage(1, 1, 2)
        dense[2].stage(2)
        dense[0].stage(3)

    beside_pairs = {
        (0, 3): beside_first,
        (1, 0): lambda: dense[1].stage(1),
        (1, 3): lambda: dense[2].stage(1),
        (2, 0): beside_third,
        (2, 3): beside_last,
    }
    attention_back(0, lambda r: xw[r].astype(F32), beside_pairs, beside_rest)
    low[...] = gx[...].astype(BF)
    send(14, low.at[at((1 - tensor) * row_count, extra)], edge_in.at[1], beside)
    send(small_key, small, small_in.at[0], core)
    attn_stage(0, 1, 0)
    dense[1].stage(3)

    arrived(pack_key, packs.at[1])
    split_packs = packs[...].astype(F32).reshape(-1, 2, IMAGES, width)
    every_slot, every_grad = (split_packs[:, n].reshape(-1, width).astype(BF) for n in range(2))
    every_slot_t = every_slot.T
    few = chunk if teams == 1 else LANES
    expert_steps = 2 * chunks * chunk // few

    def expert_grads(i):
        for part, body in ((1, beside_experts_first), (2, beside_experts_second)):
            pl.when(i == part * expert_steps // 3)(body)
        lanes = pl.ds(pl.multiple_of(i * few, few), few)
        value, grad = gelu_parts(dot(every_slot, ei[:, lanes]))
        g_pre = (dot_t(every_grad, eo[lanes, :]) * grad).astype(BF)
        expert_in_sum[:, lanes] = dot(every_slot_t, g_pre).astype(BF)
        expert_out_sum[lanes, :] = dot(value.astype(BF).T, every_grad).astype(BF)

    def beside_experts_first():
        attn_stage(0, 0, 1)
        dense[0].stage(4)
        dense[2].stage(3)
        arrived(small_key, small_in.at[0])
        small_in[1] = small[...] + small_in[0]
        send(small_key + 1, small_in.at[1], small_in.at[2], beside, small)

    def beside_experts_second():
        dense[1].stage(4)

    loop(expert_steps, expert_grads)

    last_copies = [local(0, expert_in_sum, expert_in_out), local(1, expert_out_sum, expert_out_out)]
    attn_stage(0, 1, 1)
    arrived(small_key + 1, small_in.at[2])
    small_parts[0] = small_in[1] + small_in[2]
    for k in range(1, team):
        send(small_key + 1 + k, small_parts.at[0], small_parts.at[k], mate(k)[0])
    dense[0].stage(5)
    dense[2].stage(4)

    for n, (source, dest) in enumerate(((act, act_out), (low, pg_out))):
        arrived(13 + n, edge_in.at[n])
        near = at(row_count - extra - tensor * (row_count - 2 * extra), extra)
        wide = jnp.concatenate([own[near]] * pairs, axis=1)
        source[near] = jnp.where(wide > 0.0, source[near].astype(F32), edge_in[n].astype(F32)).astype(BF)
        last_copies.append(local(2 + n, source.at[own_rows], dest))

    attn_stage(1, 0, 3)
    attn_stage(1, 1, 3)
    dense[1].stage(5)
    dense[0].stage(6)
    attn_stage(0, 0, 2)
    dense[2].stage(5)
    for k in range(1, team):
        arrived(small_key + 1 + k, small_parts.at[k])
    small_across[0] = sum([small_parts[k] for k in range(1, team)], start=small_parts[0])
    for k in range(1, teams):
        send(small_key + 1 + team + k, small_across.at[0], small_across.at[k], partner(k))
    for k in range(1, teams):
        arrived(small_key + 1 + team + k, small_across.at[k])
    small_out[...] = sum([small_across[k] for k in range(1, teams)], start=small_across[0])
    dense[1].stage(6)

    def pass_dense(q):
        dense[q].stage(7)
        done = mlp_sum.at[section, q]
        send(mlp_key + q, done, done, core, mlp_like)

    dense[2].stage(6)
    attn_stage(0, 1, 2)
    pass_dense(0)
    pass_dense(1)
    pass_dense(2)
    for q in range(chunks):
        arrived(mlp_key + q, mlp_sum.at[1 - section, q])
        for n, dest in enumerate((mi_out, mot_out)):
            place_out = dest.at[:, q * chunk : (q + 1) * chunk]
            last_copies.append(local(4 + 2 * q + n, mlp_sum.at[n, q], place_out))
    attn_stage(0, 0, 3)
    used = 4 + 2 * chunks
    for c in range(3):
        place_out = qkv_out.at[c * 3 * HD : c * 3 * HD + 2 * HD]
        last_copies.append(local(used + c, attn_sum.at[0, c * LANES : (c + 1) * LANES], place_out))
    attn_stage(0, 1, 3)
    for c in range(3):
        place_out = qkv_out.at[c * 3 * HD + 2 * HD : (c + 1) * 3 * HD]
        last_copies.append(local(used + 3 + c, attn_sum.at[1, c * HD : (c + 1) * HD], place_out))
    last_copies.append(local(used + 6, attn_sum.at[1, 3 * HD :], attn_out))
    for found in last_copies:
        found.wait()

    for key, like in sent_off.items():
        copy(key, like, like, core).wait_send()


def compute(x_own, c_own, ids, gains, qkv, out, mi, mo, router, ei, eo):
    row_count, width = x_own.shape
    window = row_count + MOST // 2
    extra = window - row_count
    pairs = width // LANES
    ff = ei.shape[1]
    _, kept = bands(window)
    chunk_count = ff // 256
    chunks = chunk_count // 2
    vmem, hbm = pl.BlockSpec(memory_space=pltpu.VMEM), pl.BlockSpec(memory_space=pl.ANY)
    ranks = lax.axis_size("dp")
    team = min(8, ranks & -ranks)
    teams = ranks // team
    bits = [1 << n for n in range(team.bit_length() - 1)]
    spread = [bits[:1] + ["tensor"] + bits[1:], ["tensor"] + bits, bits[1::-1] + ["tensor"] + bits[2:]]
    mlp_orders = [spread[q % 3] for q in range(chunks)]
    boxes = []
    for order in mlp_orders:
        size = width
        for n, dim in enumerate(order):
            size = size if dim == "tensor" else size // 2
            boxes.append(pltpu.VMEM((2 if "tensor" in order[n + 1 :] else 1, size, 256), BF))
        boxes.append(pltpu.VMEM((teams, size, 256), BF))
    for _ in range(2):
        boxes.append(pltpu.VMEM((width, width), BF))
        boxes += [pltpu.VMEM((n, width // team, width), BF) for n in (team, teams)]
    copies = 18 + chunks * (2 * len(mlp_orders[0]) + teams) + 2 * (1 + 2 * team + teams) + chunks + 2 * (team + teams + 1)
    return pl.pallas_call(
        functools.partial(
            compute_kernel, team=team, teams=teams, mlp_orders=mlp_orders
        ),
        out_shape=(
            jax.ShapeDtypeStruct((row_count, width), BF),
            jax.ShapeDtypeStruct((row_count, width), BF),
            jax.ShapeDtypeStruct(qkv.shape, BF),
            jax.ShapeDtypeStruct(out.shape, BF),
            jax.ShapeDtypeStruct((width, ff // 2), BF),
            jax.ShapeDtypeStruct((width, ff // 2), BF),
            jax.ShapeDtypeStruct((width, ff), BF),
            jax.ShapeDtypeStruct((ff, width), BF),
            jax.ShapeDtypeStruct((8, width), F32),
        ),
        in_specs=[hbm, hbm, vmem, vmem, hbm, hbm, hbm, hbm, vmem, hbm, hbm],
        out_specs=[hbm] * 8 + [vmem],
        scratch_shapes=[
            pltpu.VMEM((window, width), BF),
            pltpu.VMEM((window, width), BF),
            pltpu.VMEM((2, 8, width), F32),
            pltpu.VMEM((2 * width, width), BF),
            pltpu.VMEM((2, 2 * width, width), BF),
            pltpu.VMEM((2 * width, width), BF),
            pltpu.VMEM((2, 3 * width, width), BF),
            pltpu.VMEM((2, width, width), BF),
            pltpu.VMEM((2, *mi.shape), BF),
            pltpu.VMEM((2, *mo.shape), BF),
            pltpu.VMEM(ei.shape, BF),
            pltpu.VMEM(eo.shape, BF),
            pltpu.VMEM(ei.shape, BF),
            pltpu.VMEM(eo.shape, BF),
            pltpu.VMEM((2, SLOTS, width), BF),
            pltpu.VMEM((window, width), BF),
            pltpu.VMEM((2, extra, width), BF),
            pltpu.VMEM((2, SLOTS, width), BF),
            pltpu.VMEM((2, SLOTS, width), BF),
            pltpu.VMEM((2, SLOTS, width), BF),
            pltpu.VMEM((2, SLOTS, width), BF),
            pltpu.VMEM((4, window, width), BF),
            pltpu.VMEM((window, width), F32),
            pltpu.VMEM((window, width), BF),
            pltpu.VMEM((window, width), F32),
            pltpu.VMEM((2, pairs, LANES, window), BF),
            pltpu.VMEM((2, pairs, LANES, window), BF),
            pltpu.VMEM((LANES, window), BF),
            pltpu.VMEM((2, pairs, window, 2 * LANES), BF),
            pltpu.VMEM((2, pairs, window, LANES), BF),
            pltpu.VMEM((2, pairs, LANES, window), BF),
            pltpu.VMEM((2, pairs, kept, 2 * LANES), BF),
            pltpu.VMEM((window, width), BF),
            pltpu.VMEM((chunk_count, window, 256), BF),
            pltpu.VMEM((chunk_count, window, 256), BF),
            pltpu.VMEM((window, width), F32),
            pltpu.VMEM((window, width), BF),
            pltpu.VMEM((pairs, LANES, window), BF),
            pltpu.VMEM((3 * LANES, window), BF),
            pltpu.VMEM((3 * pairs, window, LANES), BF),
            pltpu.VMEM((window, LANES), F32),
            pltpu.VMEM((window, LANES), F32),
            pltpu.VMEM((window, width), F32),
            pltpu.VMEM((LANES, window), BF),
            pltpu.VMEM((2, pairs, 8, 2 * LANES), F32),
            pltpu.VMEM((window, LANES), F32),
            pltpu.VMEM((2, 2 * SLOTS, window), BF),
            pltpu.VMEM((SLOTS, ff), F32),
            pltpu.VMEM((2, SLOTS, width), BF),
            pltpu.VMEM((2, SLOTS, width), BF),
            pltpu.VMEM((2, 2, 2, width, width), BF),
            pltpu.VMEM((2, width, width), BF),
            pltpu.VMEM((2, 2, chunks, width, 256), BF),
            pltpu.VMEM((chunks, 2, width, 256), BF),
            pltpu.VMEM((2, chunks, width, 256), BF),
            pltpu.VMEM((8, width), F32),
            pltpu.VMEM((3, 8, width), F32),
            pltpu.VMEM((team, 8, width), F32),
            pltpu.VMEM((teams, 8, width), F32),
            pltpu.VMEM((2, teams, team, 2 * IMAGES, width), BF),
            pltpu.VMEM((2 * IMAGES, width), BF),
            pltpu.SemaphoreType.DMA((copies,)),
            pltpu.SemaphoreType.DMA((copies,)),
            pltpu.SemaphoreType.DMA((11 + 2 * chunks,)),
            *boxes,
        ],
        compiler_params=pltpu.CompilerParams(
            vmem_limit_bytes=62 * 1024 * 1024, collective_id=0, has_side_effects=True
        ),
    )(x_own, c_own, ids, gains, qkv, out, mi, mo, router, ei, eo)


def finish_kernel(
    act, pg, qkv, attn, mi, mot, expert_in, expert_out, small,
    act_out, pg_out, gains_out, qkv_out, attn_out, mi_out, mo_out, router_out, expert_in_out, expert_out_out,
):
    section, tensor = lax.axis_index("section"), lax.axis_index("tensor")
    act_out[...] = act[...]
    pg_out[...] = pg[...]
    gains_out[...] = jnp.where(section == 0, small[0:2], small[2:4])
    router_out[...] = jnp.where(tensor == 0, small[4:5], small[5:6])
    pairs = ((qkv, qkv_out), (attn, attn_out), (mi, mi_out), (expert_in, expert_in_out), (expert_out, expert_out_out))
    for source, dest in pairs:
        dest[...] = source[...].astype(F32)
    mo_out[...] = mot[...].astype(F32).T


def finish(act, pg, qkv, attn, mi, mot, expert_in, expert_out, small):
    steps = 3

    def by_rows(a):
        return pl.BlockSpec((a.shape[0] // steps, a.shape[1]), lambda i: (i, 0))

    def whole(a):
        return pl.BlockSpec(a.shape, lambda i: (0, 0))

    def like(a):
        return jax.ShapeDtypeStruct(a.shape, F32)

    gains = jax.ShapeDtypeStruct((2, act.shape[1]), F32)
    router = jax.ShapeDtypeStruct((1, act.shape[1]), F32)
    mo = jax.ShapeDtypeStruct(mot.shape[::-1], F32)
    mot_spec = pl.BlockSpec((mot.shape[0], mot.shape[1] // steps), lambda i: (0, i))
    return pl.pallas_call(
        finish_kernel,
        grid=(steps,),
        out_shape=(
            act, pg, gains, like(qkv), like(attn), like(mi), mo, router, like(expert_in), like(expert_out)
        ),
        in_specs=[
            whole(act), whole(pg), by_rows(qkv), by_rows(attn), by_rows(mi), mot_spec, by_rows(expert_in),
            by_rows(expert_out), whole(small),
        ],
        out_specs=[
            whole(act), whole(pg), whole(gains), by_rows(qkv), by_rows(attn), by_rows(mi), by_rows(mo), whole(router),
            by_rows(expert_in), by_rows(expert_out),
        ],
        compiler_params=pltpu.CompilerParams(vmem_limit_bytes=60 * 1024 * 1024),
    )(act, pg, qkv, attn, mi, mot, expert_in, expert_out, small)


def per_device(
    patches, image_ids, cotangent, norm_gains, qkv_weight, out_weight, mlp_in, mlp_out, router, expert_in, expert_out
):
    width = patches.shape[2]
    part = qkv_weight.shape[3]
    qkv = jnp.transpose(qkv_weight[0], (1, 2, 0)).reshape(-1, width)
    results = compute(
        patches[0], cotangent[0], image_ids, norm_gains[0], qkv, out_weight[0], mlp_in, mlp_out, router.T,
        expert_in[0], expert_out[0],
    )
    act, pg, gains, qkv_grad, out_grad, mi_grad, mo_grad, router_grad, ei_grad, eo_grad = finish(*results)
    qkv_grad = jnp.transpose(qkv_grad.reshape(3, part, width), (2, 0, 1))
    return (
        act[None], pg[None], gains[None], qkv_grad[None], out_grad[None], mi_grad, mo_grad, router_grad.T,
        ei_grad[None], eo_grad[None],
    )


def solution(mesh):
    return jax.shard_map(
        per_device,
        mesh=mesh,
        in_specs=(
            P(("dp", "section"), "tensor", None),
            P("dp", None),
            P(("dp", "section"), "tensor", None),
            P("section", None, None),
            P("section", None, None, "tensor"),
            P("section", "tensor", None),
            P(None, "tensor"),
            P("tensor", None),
            P(None, "tensor"),
            P("tensor", None, None),
            P("tensor", None, None),
        ),
        out_specs=(
            P(("dp", "section"), "tensor", None),
            P(("dp", "section"), "tensor", None),
            P("section", None, None),
            P("section", None, None, "tensor"),
            P("section", "tensor", None),
            P(None, "tensor"),
            P("tensor", None),
            P(None, "tensor"),
            P("tensor", None, None),
            P("tensor", None, None),
        ),
        check_vma=False,
    )
```

```python
import functools

import jax
import jax.numpy as jnp
from jax import lax
from jax.experimental import pallas as pl
from jax.experimental.pallas import tpu as pltpu
from jax.sharding import PartitionSpec as P

HD = 64
IMAGES = 8
MOST = 256
LANES = 128
SLOTS = 16
EPSILON = 1e-06
BF = jnp.bfloat16
F32 = jnp.float32


def dot(a, b):
    return jnp.dot(a, b, preferred_element_type=F32)


def dot_t(a, b):
    return lax.dot_general(a, b, (((1,), (1,)), ((), ())), preferred_element_type=F32)


def t_dot(a, b):
    return lax.dot_general(a, b, (((0,), (0,)), ((), ())), preferred_element_type=F32)


def normalise(x):
    centred = x - jnp.mean(x, axis=-1, keepdims=True)
    scale = lax.rsqrt(jnp.mean(centred * centred, axis=-1, keepdims=True) + EPSILON)
    return centred * scale, scale


def norm_back(x, gain, gz):
    unit, scale = normalise(x)
    scaled = gz * gain
    mean_plain = jnp.mean(scaled, axis=-1, keepdims=True)
    mean_unit = jnp.mean(scaled * unit, axis=-1, keepdims=True)
    return scale * (scaled - mean_plain - unit * mean_unit), jnp.sum(gz * unit, axis=0, keepdims=True)


def gelu_parts(u):
    cdf = 0.5 * (1.0 + lax.erf(u * 0.7071067811865476))
    return u * cdf, cdf + u * (0.3989422804014327 * jnp.exp(-0.5 * u * u))


def pair_up(tile):
    row = lax.broadcasted_iota(jnp.int32, tile.shape, 0)
    zero = jnp.zeros_like(tile)
    return jnp.concatenate([jnp.where(row < HD, tile, zero), jnp.where(row >= HD, tile, zero)], axis=1)


def pair_down(both):
    n = both.shape[1] // 2
    row = lax.broadcasted_iota(jnp.int32, (both.shape[0], n), 0)
    return jnp.where(row < HD, both[:, :n], both[:, n:])


def bands(window):
    reach = MOST // LANES
    found, at = [], 0
    for i in range(window // LANES):
        first = max(0, i - reach) * LANES
        count = min(window, (i + reach + 1) * LANES) - first
        found.append((i * LANES, first, count, at))
        at += count
    return found, at


MESH = pl.DeviceIdType.MESH


def compute_kernel(
    x_own, c_own, ids, gains_own, qkv_own, out_own, mi_own, mo_own, router_own, ei_own, eo_own,
    act_out, pg_out, qkv_out, attn_out, mi_out, mot_out, expert_in_out, expert_out_out, small_out,
    xw, cw, gains, wy, wc, w_own, wqkv, wo, mi, mo, ei, eo, expert_in_sum, expert_out_sum, routert, act, edge_in, slots, geos, slot_in, pack,
    z, x1, sent, x3, qt, kt, vt, kr, vr, ot, pt, tok, hidden, slope, gx, low, got, gt, gtok, gk_sum, gv_sum,
    gz_all, veil, shares, own, mixing, eslope, eout, gslot, grad_attn, attn_sum, grad_mlp, mlp_core, mlp_sum,
    small, small_in, small_parts, small_across, packs, small_pack, send_sem, recv_sem, here_sem,
    *boxes, team, teams, mlp_orders, attn_orders,
):
    row_count, width = x_own.shape
    window = xw.shape[0]
    extra = window - row_count
    half = window // 2
    pairs = width // LANES
    total = ids.shape[1]
    dp = lax.axis_index("dp")
    section = lax.axis_index("section")
    tensor = lax.axis_index("tensor")
    core = (dp, 1 - section, tensor)
    beside = (dp, section, 1 - tensor)

    spot = lax.rem(dp, team)
    this_team = dp // team

    def mate(k):
        place, bit = spot, 1
        while bit < team:
            if k & bit:
                place = jnp.where(lax.rem(spot // bit, 2) == 0, place + bit, place - bit)
            bit *= 2
        return (dp - spot + place, section, tensor), place

    def partner(k):
        return (lax.rem(dp + k * team, team * teams), section, tensor)

    blocks, _ = bands(window)
    row_blocks = window // LANES

    def at(start, size, step=LANES):
        return pl.ds(pl.multiple_of(start, step), size)

    def rows(i, n=LANES):
        return pl.ds(pl.multiple_of(i * n, n), n)

    def loop(n, body):
        def step(i, carry):
            body(i)
            return carry

        lax.fori_loop(0, n, step, 0)

    sent_off, sent_by, within = {}, {}, (0, 1)

    def copy(key, source, dest, device):
        return pltpu.make_async_remote_copy(
            src_ref=source,
            dst_ref=dest,
            send_sem=send_sem.at[key],
            recv_sem=recv_sem.at[key],
            device_id=device,
            device_id_type=MESH,
        )

    def send(key, source, dest, device, like=None):
        copy(key, source, dest, device).start()
        sent_off[key] = source if like is None else like
        sent_by.setdefault(key, set()).update(within)

    def settle(last=False):
        for key in list(sent_off):
            like = sent_off[key]
            if len(sent_by[key]) == 2:
                copy(key, like, like, core).wait_send()
            elif last:
                only(*sent_by[key])(lambda key=key, like=like: copy(key, like, like, core).wait_send())
            else:
                continue
            sent_off.pop(key)

    def arrived(key, dest):
        copy(key, dest, dest, core).wait_recv()

    def only(which):
        def run(body):
            def marked():
                nonlocal within
                within = (which,)
                body()
                within = (0, 1)

            pl.when(section == which)(marked)

        return run

    barrier = pltpu.get_barrier_semaphore()
    neighbours = [core, beside] + [mate(k)[0] for k in range(1, team)] + [partner(k) for k in range(1, teams)]
    for device in neighbours:
        pl.semaphore_signal(barrier, inc=1, device_id=device, device_id_type=MESH)

    def local(key, source, dest):
        found = pltpu.make_async_copy(source, dest, here_sem.at[key])
        found.start()
        return found

    qkv_rows = qkv_own.shape[0]
    own_rows = at(tensor * extra, row_count)
    near_copies = [
        local(0, x_own, xw.at[own_rows]),
        local(1, qkv_own, w_own.at[:qkv_rows]),
        local(2, out_own, w_own.at[qkv_rows:]),
    ]
    later_copies = [
        local(3, mi_own, mi.at[tensor]),
        local(4, mo_own, mo.at[tensor]),
        local(5, c_own, cw.at[own_rows]),
        local(6, ei_own, ei),
        local(7, eo_own, eo),
    ]
    gains[section, :2] = gains_own[...]
    first_row = lax.broadcasted_iota(jnp.int32, (SLOTS, width), 0) == 0
    router_rows = jnp.broadcast_to(router_own[...].astype(F32), (SLOTS, width))
    routert[tensor] = jnp.where(first_row, router_rows, 0.0).astype(BF)
    pl.semaphore_wait(barrier, len(neighbours))

    qkv_here, out_here = wy.at[:qkv_rows], wy.at[qkv_rows:]
    qkv_near, out_near = wc.at[0, :qkv_rows], wc.at[0, qkv_rows:]
    qkv_far, out_far = wc.at[1, :qkv_rows], wc.at[1, qkv_rows:]

    edge = x_own.at[at((1 - tensor) * (row_count - extra), extra)]
    send(0, edge, xw.at[at(tensor * row_count, extra)], beside)

    @only(0)
    def _():
        send(3, qkv_own, qkv_here, beside)
        send(15, out_own, out_here, beside)
        send(5, mi_own, mi.at[tensor], beside)

    send(1, gains.at[section], gains.at[section], core)
    send(2, qkv_own, qkv_near, core)
    send(16, out_own, out_near, core)

    ids_row = ids[pl.ds(section, 1), :].astype(F32)
    image = lax.broadcasted_iota(jnp.int32, (SLOTS, total), 0).astype(F32)
    spread = jnp.broadcast_to(ids_row, (SLOTS, total))
    middle = jnp.sum((spread < image).astype(F32) + (spread <= image).astype(F32), axis=1, keepdims=True)
    first_half = (middle < total).astype(F32)
    mine = jnp.where(tensor == 0, first_half, 1.0 - first_half)
    window_ids = ids[pl.ds(section, 1), at(tensor * (total - window), window)].astype(F32)
    member = (jnp.broadcast_to(window_ids, (SLOTS, window)) == image[:, :window]).astype(F32)
    member_own = member * mine
    own_row = jnp.sum(member_own, axis=0, keepdims=True)
    own[...] = jnp.broadcast_to(own_row, (LANES, window)).T
    blank = jnp.zeros((LANES - SLOTS, window), F32)
    image_of = jnp.concatenate([member, blank], axis=0).T.astype(BF)
    for b in range(2):
        for j in range(pairs):
            kr[b, j, :, LANES:] = image_of
    veil[...] = jnp.concatenate([(1.0 - member) * -1e30, blank], axis=0).astype(BF)

    def place(source, b, t, kinds=(0, 1, 2, 3)):
        for c in kinds:
            first = c * 3 * HD
            if c < 3:
                own_pair, mixed_pair, dest = t * width + c * LANES, 2 * width + c * LANES + t * HD, wqkv
            else:
                own_pair, mixed_pair, dest = t * LANES, 2 * LANES + t * HD, wo
            dest[b, at(own_pair, 2 * HD)] = source[first : first + 2 * HD]
            dest[b, at(mixed_pair, HD, HD)] = source[first + 2 * HD : first + 3 * HD]

    for found in near_copies:
        found.wait()
    place(w_own, section, tensor)
    arrived(1, gains.at[1 - section])
    arrived(2, qkv_near)
    arrived(16, out_near)
    place(wc.at[0], 1 - section, tensor)
    arrived(0, xw.at[at((1 - tensor) * row_count, extra)])


    def first_far():
        @only(0)
        def _():
            arrived(3, qkv_here)
            send(4, qkv_here, qkv_far, core)
            place(wy, 0, 1 - tensor, (0, 1, 2))

        @only(1)
        def _():
            arrived(4, qkv_far)
            place(wc.at[1], 0, 1 - tensor, (0, 1, 2))

    def send_dense():
        @only(1)
        def _():
            send(5, mo_own, mo.at[tensor], beside)

    def second_far():
        @only(0)
        def _():
            arrived(4, qkv_far)
            place(wc.at[1], 1, 1 - tensor, (0, 1, 2))

        @only(1)
        def _():
            arrived(3, qkv_here)
            send(4, qkv_here, qkv_far, core)
            place(wy, 1, 1 - tensor, (0, 1, 2))

    def first_out():
        @only(0)
        def _():
            arrived(15, out_here)
            send(17, out_here, out_far, core)
            place(wy, 0, 1 - tensor, (3,))

        @only(1)
        def _():
            arrived(17, out_far)
            place(wc.at[1], 0, 1 - tensor, (3,))

    def second_out():
        @only(0)
        def _():
            arrived(17, out_far)
            place(wc.at[1], 1, 1 - tensor, (3,))

        @only(1)
        def _():
            arrived(15, out_here)
            send(17, out_here, out_far, core)
            place(wy, 1, 1 - tensor, (3,))

    def add_across(first, piece, heard):
        if teams == 1:
            return
        for k in range(1, teams):
            copy(first + k, piece, heard.at[k], partner(k)).start()
        whole = piece[...].astype(F32)
        for k in range(1, teams):
            arrived(first + k, heard.at[k])
            copy(first + k, piece, heard.at[k], partner(k)).wait_send()
            whole = whole + heard[k].astype(F32)
        piece[...] = whole.astype(BF)

    class Cube:
        def __init__(self, key, pick, core_in, total, order, boxes):
            self.key, self.pick, self.core_in, self.total, self.order = key, pick, core_in, total, order
            self.boxes, self.across = boxes[:-1], boxes[-1]
            start, size, self.plan = 0, total.shape[0], []
            for dim in order:
                if dim == "tensor":
                    self.plan.append((dim, start, size, start))
                else:
                    size //= 2
                    bit = lax.rem(spot // dim, 2)
                    self.plan.append((dim, start + bit * size, size, start + (1 - bit) * size))
                    start = start + bit * size
            self.back = [(i, *step) for i, step in enumerate(self.plan) if step[0] != "tensor"][::-1]
            self.like = {size: total.at[:size] for _, _, _, size, _ in self.back}
            self.along = order.index("tensor")

        def to_core(self, source):
            send(self.key, source, self.core_in, core, self.core_in)

        def add(self, parts, start, size, box):
            for n, part in enumerate(parts):
                kept = self.pick(part, at(start, size, 16))
                kept[...] = (kept[...].astype(F32) + box[n].astype(F32)).astype(BF)

        def stage(self, k):
            steps, rounds = len(self.plan), len(self.back)
            both = (0, 1)
            if k == 0:
                arrived(self.key, self.core_in)
                self.add(both, 0, self.total.shape[0], self.core_in)
            elif k <= steps:
                _, start, size, _ = self.plan[k - 1]
                arrived(self.key + k, self.boxes[k - 1])
                self.add((tensor,) if self.along < k else both, start, size, self.boxes[k - 1])
            else:
                _, _, _, size, start = self.back[k - steps - 1]
                arrived(self.key + k, self.total.at[at(start, size, 16)])
            if k < steps:
                dim, _, size, start = self.plan[k]
                if dim == "tensor":
                    device = beside
                    source = self.pick(pl.ds(1 - tensor, 1), at(start, size, 16))
                else:
                    device = mate(dim)[0]
                    parts = pl.ds(tensor, 1) if self.along < k else slice(None)
                    source = self.pick(parts, at(start, size, 16))
                send(self.key + k + 1, source, self.boxes[k], device, self.boxes[k])
            elif k == steps:
                _, start, size, _ = self.plan[-1]
                piece = self.total.at[at(start, size, 16)]
                piece[...] = self.pick(tensor, at(start, size, 16))[...]
                add_across(self.key + Cube.stages, piece, self.across)
            if steps <= k < steps + rounds:
                _, dim, start, size, _ = self.back[k - steps]
                region = self.total.at[at(start, size, 16)]
                send(self.key + k + 1, region, region, mate(dim)[0], self.like[size])

        stages = len(mlp_orders[0]) * 2
        keys = stages + teams

    class Straight:
        def __init__(self, key, pick, core_in, total, boxes):
            self.key, self.pick, self.core_in, self.total = key, pick, core_in, total
            self.beside_in, self.parts, self.across = boxes
            self.size = total.shape[0] // team
            self.like = total.at[: self.size]

        def part(self, place):
            return at(place * self.size, self.size, 16)

        def to_core(self, source):
            send(self.key, source, self.core_in, core, self.core_in)

        def stage(self, k):
            every = pl.ds(0, self.total.shape[0])
            near = self.pick(tensor, every)
            if k == 0:
                arrived(self.key, self.core_in)
                far = self.pick(1 - tensor, every)
                far[...] = (far[...].astype(F32) + self.core_in[1 - tensor].astype(F32)).astype(BF)
                send(self.key + 1, far, self.beside_in, beside, self.beside_in)
            if k == 1:
                arrived(self.key + 1, self.beside_in)
                both = near[...].astype(F32) + self.core_in[tensor].astype(F32)
                near[...] = (both + self.beside_in[...].astype(F32)).astype(BF)
                for n in range(1, team):
                    device, place = mate(n)
                    source = self.pick(tensor, self.part(place))
                    send(self.key + 1 + n, source, self.parts.at[n], device, self.like)
            if k == 2:
                whole = self.pick(tensor, self.part(spot))[...].astype(F32)
                for n in range(1, team):
                    arrived(self.key + 1 + n, self.parts.at[n])
                    whole = whole + self.parts[n].astype(F32)
                piece = self.total.at[self.part(spot)]
                piece[...] = whole.astype(BF)
                add_across(self.key + 1 + 2 * team, piece, self.across)
                for n in range(1, team):
                    send(self.key + 1 + team + n, piece, piece, mate(n)[0], self.like)
            if k == 3:
                for n in range(1, team):
                    arrived(self.key + 1 + team + n, self.total.at[self.part(mate(n)[1])])

        keys = 1 + 2 * team + teams

    chunks = len(mlp_orders)
    key, taken = 18, 0

    def boxes_of(count):
        nonlocal taken
        taken += count
        return boxes[taken - count : taken]

    def mlp_pick(q):
        return lambda parts, where: grad_mlp.at[section, parts, q, where]

    def attn_pick(n):
        return lambda parts, where: grad_attn.at[section, parts, n, where]

    dense, attn = [], []
    for q in range(chunks):
        total_of = mlp_sum.at[section, q]
        found = boxes_of(len(mlp_orders[q]) + 1)
        dense.append(Cube(key, mlp_pick(q), mlp_core.at[q], total_of, mlp_orders[q], found))
        key += Cube.keys
    attn = {}
    for n in range(2):
        heard, found = wc.at[:, n * width : (n + 1) * width], boxes_of(len(attn_orders[n]) + 1)
        attn[1, n] = Cube(key, attn_pick(n), heard, attn_sum.at[n], attn_orders[n], found)
        key += Cube.keys
    for n in range(2):
        heard = wc.at[:, n * width : (n + 1) * width]
        attn[0, n] = Straight(key, attn_pick(n), heard, attn_sum.at[n], boxes_of(3))
        key += Straight.keys
    mlp_key, pack_key, small_key = key, key + chunks, key + chunks + team + teams
    mlp_like = mlp_sum.at[0, 0]

    def give_attn(b, n):
        @only(1 - b)
        def _():
            attn[b, n].to_core(grad_attn.at[b, :, n])

    def attn_stage(b, n, k):
        @only(b)
        def _():
            attn[b, n].stage(k)

    def give_dense(q):
        dense[q].to_core(grad_mlp.at[1 - section, :, q])

    def attention(b, x_of, out_ref, ahead_of_far, ahead_of_out):
        def norm(i):
            unit, _ = normalise(x_of(rows(i)))
            z[2 * b, rows(i)] = (unit * gains[b, 0:1, :]).astype(BF)

        loop(row_blocks, norm)

        def pair(n):
            pl.when(n == 1)(ahead_of_far)
            if b == 0:
                pl.when(n == 2)(send_dense)
            j = jnp.where(n == 0, tensor, jnp.where(n == 1, 1 - tensor, n))
            zz, weights = z[2 * b], wqkv.at[b, at(j * width, width)]
            flat = dot_t(zz, weights[...])
            qt[b, j] = (flat[:, :LANES] * HD**-0.5).astype(BF).T
            keys, values = flat[:, LANES : 2 * LANES].astype(BF), flat[:, 2 * LANES :].astype(BF)
            kr[b, j, :, :LANES] = keys
            vr[b, j] = values
            kt[b, j] = keys.T
            vt[...] = values.T
            for q0, k0, count, kept in blocks:
                queries = pair_up(qt[b, j, :, q0 : q0 + LANES])
                hidden_part = veil[:, q0 : q0 + LANES]
                queries = jnp.concatenate([queries, jnp.concatenate([hidden_part, hidden_part], axis=1)], axis=0)
                scores = dot(kr[b, j, k0 : k0 + count, :], queries)
                powers = jnp.exp(scores - jnp.max(scores, axis=0, keepdims=True))
                inverse = 1.0 / jnp.sum(powers, axis=0, keepdims=True)
                low_powers = powers.astype(BF)
                pt[b, j, kept : kept + count, :] = low_powers
                shares[b, j, q0 // LANES : q0 // LANES + 1, :] = inverse
                mixed = dot(vt[:, k0 : k0 + count], low_powers) * inverse
                ot[b, j, :, q0 : q0 + LANES] = pair_down(mixed).astype(BF)

        loop(pairs, pair)
        for j in range(pairs):
            tok[:, j * LANES : (j + 1) * LANES] = ot[b, j].T

        ahead_of_out()

        out_ref[...] = x_of(slice(None)) + dot(tok[...], wo[b])

    def attention_back(b, x_of, beside_pairs, after_pairs):
        ga = low[...]
        got[...] = dot_t(wo[b], ga).astype(BF).reshape(pairs, LANES, window)
        pieces = dot(ot[b].reshape(width, window), ga).astype(BF)
        for t in range(2):
            grad_attn[b, t, 1, 3 * HD : 5 * HD, :] = pieces[t * LANES : (t + 1) * LANES]
            grad_attn[b, t, 1, 5 * HD : 6 * HD, :] = pieces[2 * LANES + t * HD : 2 * LANES + (t + 1) * HD]
        def pair(j):
            gk_sum[...] = jnp.zeros_like(gk_sum)
            gv_sum[...] = jnp.zeros_like(gv_sum)
            for q0, k0, count, kept in blocks:
                for (at_pair, at_query), body in beside_pairs.items():
                    if at_query == q0 // LANES:
                        pl.when(j == at_pair)(body)
                inverse = shares[b, j, q0 // LANES : q0 // LANES + 1, :]
                go_pair = (pair_up(got[j, :, q0 : q0 + LANES]).astype(F32) * inverse).astype(BF)
                q_pair = pair_up(qt[b, j, :, q0 : q0 + LANES])
                low_powers = pt[b, j, kept : kept + count, :]
                powers = low_powers.astype(F32)
                weighted = dot(vr[b, j, k0 : k0 + count, :], go_pair) * powers
                inner = jnp.sum(weighted, axis=0, keepdims=True) * inverse
                gs = (weighted - powers * inner).astype(BF)
                gq = pair_down(dot(kt[b, j, :, k0 : k0 + count], gs)) * HD**-0.5
                gt[:LANES, q0 : q0 + LANES] = gq.astype(BF)
                gk_sum[k0 : k0 + count] += dot_t(gs, q_pair)
                gv_sum[k0 : k0 + count] += dot_t(low_powers, go_pair)
            gtok[3 * j] = gt[:LANES].T
            for c, total_of in ((1, gk_sum), (2, gv_sum)):
                low_sum = total_of[...].astype(BF)
                gtok[3 * j + c] = low_sum
                gt[c * LANES : (c + 1) * LANES] = low_sum.T
            pieces = dot(gt[...], z[2 * b]).astype(BF)

            @pl.when(j < 2)
            def _():
                grad_attn[b, j, 0] = pieces

            @pl.when(j == 2)
            def _():
                for c in range(3):
                    for t in range(2):
                        first = c * LANES + t * HD
                        grad_attn[b, t, 1, c * HD : (c + 1) * HD, :] = pieces[first : first + HD]

        loop(pairs, pair)
        after_pairs()
        gain = gains[b, 0:1, :]

        def back(i, gain_grad):
            wide = jnp.concatenate([gtok[c, rows(i, half)] for c in range(3 * pairs)], axis=1)
            step, part = norm_back(x_of(rows(i, half)), gain, dot(wide, wqkv[b]))
            gx[rows(i, half)] += step
            return gain_grad + part

        small[2 * b : 2 * b + 1, :] = lax.fori_loop(0, 2, back, jnp.zeros((1, width), F32))

    attention(0, lambda r: xw[r].astype(F32), x1, first_far, first_out)

    def norm_middle(source, which):
        def body(i):
            unit, _ = normalise(source[rows(i)])
            z[which, rows(i)] = (unit * gains[which // 2, 1:2, :]).astype(BF)

        loop(row_blocks, body)

    norm_middle(x1, 1)

    for found in later_copies:
        found.wait()

    def far_hidden():
        @only(0)
        def _():
            arrived(5, mi.at[1 - tensor])
            send(6, mi.at[1 - tensor], mi.at[1 - tensor], core, mi_own)

        @only(1)
        def _():
            send(3, qkv_own, qkv_here, beside)
            send(15, out_own, out_here, beside)
            arrived(5, mo.at[1 - tensor])
            send(6, mo.at[1 - tensor], mo.at[1 - tensor], core, mo_own)
            arrived(6, mi.at[1 - tensor])

    chunk = 256

    def hidden_chunk(n):
        pl.when(n == chunks)(far_hidden)
        q = lax.rem(n, chunks)
        part, first = jnp.where(n < chunks, tensor, 1 - tensor), pl.multiple_of(q * chunk, chunk)
        value, grad = gelu_parts(dot(z[1], mi[part, :, pl.ds(first, chunk)]))
        hidden[part * chunks + q] = value.astype(BF)
        slope[part * chunks + q] = grad.astype(BF)

    loop(2 * chunks, hidden_chunk)

    @only(0)
    def _():
        arrived(6, mo.at[1 - tensor])

    h = jnp.concatenate([hidden[c] for c in range(2 * chunks)], axis=1)
    sent[...] = (x1[...] + dot(h, mo[...].reshape(-1, width))).astype(BF)

    c_edge = c_own.at[at((1 - tensor) * (row_count - extra), extra)]
    send(7, c_edge, cw.at[at(tensor * row_count, extra)], beside)
    send(8, routert.at[tensor], routert.at[tensor], beside)

    attention(1, lambda r: sent[r].astype(F32), x3, second_far, second_out)
    norm_middle(x3, 3)
    z3 = z[3]
    arrived(8, routert.at[1 - tensor])
    powers = [jnp.exp(dot_t(routert[e], z3)[:1]) for e in range(2)]
    dispatch, combine = [], []
    for e in range(2):
        totals = jnp.sum(member * powers[e], axis=1, keepdims=True)
        dispatch.append(powers[e] / jnp.sum(member * totals, axis=0, keepdims=True))
        combine.append(powers[e] / (powers[0] + powers[1]))
        d_low = (member_own * dispatch[e].astype(BF).astype(F32)).astype(BF)
        c_low = (member * combine[e].astype(BF).astype(F32)).astype(BF)
        mixing[0, e * SLOTS : (e + 1) * SLOTS] = d_low
        mixing[1, e * SLOTS : (e + 1) * SLOTS] = c_low
        slots[e] = dot(d_low, z3).astype(BF)
    send(9, slots.at[1 - tensor], slot_in.at[0], beside)
    arrived(7, cw.at[at((1 - tensor) * row_count, extra)])

    def mask(i):
        wide = jnp.concatenate([own[rows(i)]] * pairs, axis=1)
        low[rows(i)] = jnp.where(wide > 0.0, cw[rows(i)].astype(F32), 0.0).astype(BF)

    loop(row_blocks, mask)
    gy = low[...]
    for e in range(2):
        geos[e] = dot(mixing[1, e * SLOTS : (e + 1) * SLOTS], gy).astype(BF)
    send(10, geos.at[1 - tensor], slot_in.at[1], beside)

    arrived(9, slot_in.at[0])
    pack[0] = slots[tensor] + slot_in[0]
    value, grad = gelu_parts(dot(pack[0], ei[...]))
    eslope[...] = grad
    eout[tensor] = dot(value.astype(BF), eo[...]).astype(BF)
    send(11, eout.at[tensor], eout.at[tensor], beside)
    arrived(10, slot_in.at[1])
    pack[1] = geos[tensor] + slot_in[1]
    g_hidden = dot_t(pack[1], eo[...])
    gslot[tensor] = dot_t((g_hidden * eslope[...]).astype(BF), ei[...]).astype(BF)
    send(12, gslot.at[tensor], gslot.at[tensor], beside)
    arrived(11, eout.at[1 - tensor])
    outputs = eout[...].reshape(2 * SLOTS, width)

    def finish(i):
        mixed = t_dot(mixing[1, :, rows(i)], outputs)
        act[rows(i)] = (x3[rows(i)] + mixed).astype(BF)

    loop(row_blocks, finish)
    send(13, act.at[at((1 - tensor) * row_count, extra)], edge_in.at[0], beside)

    all_packs, team_like = packs.at[0], packs.at[0, 0]

    def share_slots():
        halves = [pack[n].astype(F32)[:IMAGES] for n in range(2)]
        small_pack[...] = jnp.concatenate(halves, axis=0).astype(BF)
        for k in range(1, team):
            send(pack_key + k, small_pack, packs.at[0, this_team, spot], mate(k)[0], small_pack)

    def gather_slots():
        for k in range(1, team):
            arrived(pack_key + k, packs.at[0, this_team, mate(k)[1]])
        packs[0, this_team, spot] = small_pack[...]
        for k in range(1, teams):
            team_packs = packs.at[0, this_team]
            send(pack_key + team + k, team_packs, team_packs, partner(k), team_like)
        for k in range(1, teams):
            arrived(pack_key + team + k, packs.at[0, lax.rem(this_team + k, teams)])
        send(pack_key, packs.at[0], packs.at[1], core, all_packs)

    per_token = [jnp.sum(dot_t(eout[e], gy) * member, axis=0, keepdims=True) for e in range(2)]
    inner = combine[0] * per_token[0] + combine[1] * per_token[1]
    arrived(12, gslot.at[1 - tensor])
    logit_grads = []
    for e in range(2):
        g_dispatch = jnp.sum(dot_t(gslot[e], z3) * member_own, axis=0, keepdims=True)
        weighted = dispatch[e] * g_dispatch
        sums = jnp.sum(member * weighted, axis=1, keepdims=True)
        from_dispatch = weighted - dispatch[e] * jnp.sum(member * sums, axis=0, keepdims=True)
        logit_grads.append(combine[e] * (per_token[e] - inner) + from_dispatch)
    which_row = lax.broadcasted_iota(jnp.int32, (SLOTS, width), 0)
    router_rows = jnp.where(
        which_row == 0,
        jnp.broadcast_to(routert[0].astype(F32)[:1], (SLOTS, width)),
        jnp.where(which_row == 1, jnp.broadcast_to(routert[1].astype(F32)[:1], (SLOTS, width)), 0.0),
    ).astype(BF)
    which = lax.broadcasted_iota(jnp.int32, (SLOTS, window), 0)
    logit_grad = jnp.where(which == 0, logit_grads[0], jnp.where(which == 1, logit_grads[1], 0.0)).astype(BF)
    small[4:6, :] = dot(logit_grad, z3)[:2]
    small[6:8, :] = jnp.zeros((2, width), F32)
    mixing[1, :SLOTS] = logit_grad
    slots_and_router = jnp.concatenate([gslot[0], gslot[1], router_rows], axis=0)

    def experts_back(i, gain_grad):
        at = pl.ds(pl.multiple_of(i * LANES, LANES), LANES)
        parts = jnp.concatenate([mixing[0, :, at], mixing[1, :SLOTS, at]], axis=0)
        step, part = norm_back(x3[rows(i)], gains[1, 1:2, :], t_dot(parts, slots_and_router))
        total_of = low[rows(i)].astype(F32) + step
        gx[rows(i)] = total_of
        low[rows(i)] = total_of.astype(BF)
        return gain_grad + part

    small[3:4, :] = lax.fori_loop(0, row_blocks, experts_back, jnp.zeros((1, width), F32))

    def shares_second():
        gather_slots()
        give_attn(1, 0)

    share_slots()
    attention_back(1, lambda r: sent[r].astype(F32), {(2, 0): shares_second}, lambda: give_attn(1, 1))

    low[...] = gx[...].astype(BF)
    gsent = low[...]
    gsent_t = gsent.T
    z2 = z[1]
    z2_t = z2.T

    def hidden_back(n):
        for ahead, body in ((2, dense_first), (4, dense_second)):
            pl.when(n == ahead)(body)
        q, part = n // 2, lax.rem(n, 2)
        i, first = part * chunks + q, pl.multiple_of(q * chunk, chunk)
        grad_mlp[1, part, q] = dot(gsent_t, hidden[i]).astype(BF)
        g_hidden = dot_t(gsent, mo[part, pl.ds(first, chunk), :])
        g_pre = (g_hidden * slope[i].astype(F32)).astype(BF)
        hidden[i] = g_pre
        grad_mlp[0, part, q] = dot(z2_t, g_pre).astype(BF)

    def dense_first():
        give_dense(0)
        attn_stage(1, 0, 0)

    def dense_second():
        give_dense(1)
        attn_stage(1, 1, 0)
        dense[0].stage(0)

    loop(2 * chunks, hidden_back)
    give_dense(2)
    dense[1].stage(0)

    def dense_back(i, gain_grad):
        gz = jnp.zeros((half, width), F32)
        for part in range(2):
            g = jnp.concatenate([hidden[part * chunks + c, rows(i, half)] for c in range(chunks)], axis=1)
            gz = gz + dot_t(g, mi[part])
        step, part = norm_back(x1[rows(i, half)], gains[0, 1:2, :], gz)
        total_of = low[rows(i, half)].astype(F32) + step
        gx[rows(i, half)] = total_of
        low[rows(i, half)] = total_of.astype(BF)
        return gain_grad + part

    small[1:2, :] = lax.fori_loop(0, 2, dense_back, jnp.zeros((1, width), F32))

    dense[2].stage(0)
    attn_stage(1, 0, 1)

    def beside_first():
        dense[0].stage(1)
        attn_stage(1, 1, 1)

    def beside_second():
        dense[1].stage(1)
        attn_stage(1, 0, 2)

    def beside_middle():
        dense[2].stage(1)
        attn_stage(1, 1, 2)

    def beside_third():
        give_attn(0, 0)
        attn_stage(1, 0, 3)
        dense[0].stage(2)

    def beside_last():
        dense[1].stage(2)
        attn_stage(1, 1, 3)
        attn_stage(0, 0, 0)

    def beside_rest():
        give_attn(0, 1)
        attn_stage(1, 0, 4)
        dense[2].stage(2)
        dense[0].stage(3)

    beside_pairs = {
        (0, 3): beside_first,
        (1, 0): beside_second,
        (1, 3): beside_middle,
        (2, 0): beside_third,
        (2, 3): beside_last,
    }
    attention_back(0, lambda r: xw[r].astype(F32), beside_pairs, beside_rest)
    low[...] = gx[...].astype(BF)
    send(14, low.at[at((1 - tensor) * row_count, extra)], edge_in.at[1], beside)
    send(small_key, small, small_in.at[0], core)
    attn_stage(0, 1, 0)
    attn_stage(1, 1, 4)
    dense[1].stage(3)

    arrived(pack_key, packs.at[1])
    split_packs = packs[...].astype(F32).reshape(-1, 2, IMAGES, width)
    every_slot, every_grad = (split_packs[:, n].reshape(-1, width).astype(BF) for n in range(2))
    every_slot_t = every_slot.T
    few = chunk if teams == 1 else LANES
    expert_steps = 2 * chunks * chunk // few

    def expert_grads(i):
        for part, body in ((1, beside_experts_first), (2, beside_experts_second)):
            pl.when(i == part * expert_steps // 3)(body)
        lanes = pl.ds(pl.multiple_of(i * few, few), few)
        value, grad = gelu_parts(dot(every_slot, ei[:, lanes]))
        g_pre = (dot_t(every_grad, eo[lanes, :]) * grad).astype(BF)
        expert_in_sum[:, lanes] = dot(every_slot_t, g_pre).astype(BF)
        expert_out_sum[lanes, :] = dot(value.astype(BF).T, every_grad).astype(BF)

    def beside_experts_first():
        attn_stage(0, 0, 1)
        attn_stage(1, 0, 5)
        dense[0].stage(4)
        dense[2].stage(3)
        arrived(small_key, small_in.at[0])
        small_in[1] = small[...] + small_in[0]
        send(small_key + 1, small_in.at[1], small_in.at[2], beside, small)

    def beside_experts_second():
        attn_stage(1, 1, 5)
        dense[1].stage(4)

    loop(expert_steps, expert_grads)

    last_copies = [local(0, expert_in_sum, expert_in_out), local(1, expert_out_sum, expert_out_out)]
    attn_stage(0, 1, 1)
    attn_stage(1, 0, 6)
    arrived(small_key + 1, small_in.at[2])
    small_parts[0] = small_in[1] + small_in[2]
    for k in range(1, team):
        send(small_key + 1 + k, small_parts.at[0], small_parts.at[k], mate(k)[0])
    dense[0].stage(5)
    dense[2].stage(4)

    for n, (source, dest) in enumerate(((act, act_out), (low, pg_out))):
        arrived(13 + n, edge_in.at[n])
        near = at(row_count - extra - tensor * (row_count - 2 * extra), extra)
        wide = jnp.concatenate([own[near]] * pairs, axis=1)
        source[near] = jnp.where(wide > 0.0, source[near].astype(F32), edge_in[n].astype(F32)).astype(BF)
        last_copies.append(local(2 + n, source.at[own_rows], dest))

    attn_stage(1, 1, 6)
    dense[1].stage(5)
    dense[0].stage(6)
    attn_stage(1, 0, 7)
    attn_stage(0, 0, 2)
    dense[2].stage(5)
    for k in range(1, team):
        arrived(small_key + 1 + k, small_parts.at[k])
    small_across[0] = sum([small_parts[k] for k in range(1, team)], start=small_parts[0])
    for k in range(1, teams):
        send(small_key + 1 + team + k, small_across.at[0], small_across.at[k], partner(k))
    for k in range(1, teams):
        arrived(small_key + 1 + team + k, small_across.at[k])
    small_out[...] = sum([small_across[k] for k in range(1, teams)], start=small_across[0])
    dense[1].stage(6)

    def pass_dense(q):
        dense[q].stage(7)
        done = mlp_sum.at[section, q]
        send(mlp_key + q, done, done, core, mlp_like)

    dense[2].stage(6)
    attn_stage(0, 1, 2)
    attn_stage(1, 1, 7)
    pass_dense(0)
    pass_dense(1)
    pass_dense(2)
    for q in range(chunks):
        arrived(mlp_key + q, mlp_sum.at[1 - section, q])
        for n, dest in enumerate((mi_out, mot_out)):
            place_out = dest.at[:, q * chunk : (q + 1) * chunk]
            last_copies.append(local(4 + 2 * q + n, mlp_sum.at[n, q], place_out))
    attn_stage(0, 0, 3)
    used = 4 + 2 * chunks
    for c in range(3):
        place_out = qkv_out.at[c * 3 * HD : c * 3 * HD + 2 * HD]
        last_copies.append(local(used + c, attn_sum.at[0, c * LANES : (c + 1) * LANES], place_out))
    settle()
    attn_stage(0, 1, 3)
    for c in range(3):
        place_out = qkv_out.at[c * 3 * HD + 2 * HD : (c + 1) * 3 * HD]
        last_copies.append(local(used + 3 + c, attn_sum.at[1, c * HD : (c + 1) * HD], place_out))
    last_copies.append(local(used + 6, attn_sum.at[1, 3 * HD :], attn_out))
    for found in last_copies:
        found.wait()

    settle(True)


def compute(x_own, c_own, ids, gains, qkv, out, mi, mo, router, ei, eo):
    row_count, width = x_own.shape
    window = row_count + MOST // 2
    extra = window - row_count
    pairs = width // LANES
    ff = ei.shape[1]
    _, kept = bands(window)
    chunk_count = ff // 256
    chunks = chunk_count // 2
    vmem, hbm = pl.BlockSpec(memory_space=pltpu.VMEM), pl.BlockSpec(memory_space=pl.ANY)
    ranks = lax.axis_size("dp")
    team = min(8, ranks & -ranks)
    teams = ranks // team
    bits = [1 << n for n in range(team.bit_length() - 1)]
    spread = [bits[:1] + ["tensor"] + bits[1:], ["tensor"] + bits, bits[1::-1] + ["tensor"] + bits[2:]]
    mlp_orders = [spread[q % 3] for q in range(chunks)]
    attn_orders = [spread[2], spread[1]]
    boxes = []
    for order, lanes in [(order, 256) for order in mlp_orders] + [(order, width) for order in attn_orders]:
        size = width
        for n, dim in enumerate(order):
            size = size if dim == "tensor" else size // 2
            boxes.append(pltpu.VMEM((2 if "tensor" in order[n + 1 :] else 1, size, lanes), BF))
        boxes.append(pltpu.VMEM((teams, size, lanes), BF))
    for _ in range(2):
        boxes.append(pltpu.VMEM((width, width), BF))
        boxes += [pltpu.VMEM((n, width // team, width), BF) for n in (team, teams)]
    copies = 18 + (chunks + 2) * (2 * len(mlp_orders[0]) + teams) + 2 * (1 + 2 * team + teams) + chunks + 2 * (team + teams + 1)
    return pl.pallas_call(
        functools.partial(
            compute_kernel, team=team, teams=teams, mlp_orders=mlp_orders, attn_orders=attn_orders
        ),
        out_shape=(
            jax.ShapeDtypeStruct((row_count, width), BF),
            jax.ShapeDtypeStruct((row_count, width), BF),
            jax.ShapeDtypeStruct(qkv.shape, BF),
            jax.ShapeDtypeStruct(out.shape, BF),
            jax.ShapeDtypeStruct((width, ff // 2), BF),
            jax.ShapeDtypeStruct((width, ff // 2), BF),
            jax.ShapeDtypeStruct((width, ff), BF),
            jax.ShapeDtypeStruct((ff, width), BF),
            jax.ShapeDtypeStruct((8, width), F32),
        ),
        in_specs=[hbm, hbm, vmem, vmem, hbm, hbm, hbm, hbm, vmem, hbm, hbm],
        out_specs=[hbm] * 8 + [vmem],
        scratch_shapes=[
            pltpu.VMEM((window, width), BF),
            pltpu.VMEM((window, width), BF),
            pltpu.VMEM((2, 8, width), F32),
            pltpu.VMEM((2 * width, width), BF),
            pltpu.VMEM((2, 2 * width, width), BF),
            pltpu.VMEM((2 * width, width), BF),
            pltpu.VMEM((2, 3 * width, width), BF),
            pltpu.VMEM((2, width, width), BF),
            pltpu.VMEM((2, *mi.shape), BF),
            pltpu.VMEM((2, *mo.shape), BF),
            pltpu.VMEM(ei.shape, BF),
            pltpu.VMEM(eo.shape, BF),
            pltpu.VMEM(ei.shape, BF),
            pltpu.VMEM(eo.shape, BF),
            pltpu.VMEM((2, SLOTS, width), BF),
            pltpu.VMEM((window, width), BF),
            pltpu.VMEM((2, extra, width), BF),
            pltpu.VMEM((2, SLOTS, width), BF),
            pltpu.VMEM((2, SLOTS, width), BF),
            pltpu.VMEM((2, SLOTS, width), BF),
            pltpu.VMEM((2, SLOTS, width), BF),
            pltpu.VMEM((4, window, width), BF),
            pltpu.VMEM((window, width), F32),
            pltpu.VMEM((window, width), BF),
            pltpu.VMEM((window, width), F32),
            pltpu.VMEM((2, pairs, LANES, window), BF),
            pltpu.VMEM((2, pairs, LANES, window), BF),
            pltpu.VMEM((LANES, window), BF),
            pltpu.VMEM((2, pairs, window, 2 * LANES), BF),
            pltpu.VMEM((2, pairs, window, LANES), BF),
            pltpu.VMEM((2, pairs, LANES, window), BF),
            pltpu.VMEM((2, pairs, kept, 2 * LANES), BF),
            pltpu.VMEM((window, width), BF),
            pltpu.VMEM((chunk_count, window, 256), BF),
            pltpu.VMEM((chunk_count, window, 256), BF),
            pltpu.VMEM((window, width), F32),
            pltpu.VMEM((window, width), BF),
            pltpu.VMEM((pairs, LANES, window), BF),
            pltpu.VMEM((3 * LANES, window), BF),
            pltpu.VMEM((3 * pairs, window, LANES), BF),
            pltpu.VMEM((window, LANES), F32),
            pltpu.VMEM((window, LANES), F32),
            pltpu.VMEM((window, width), F32),
            pltpu.VMEM((LANES, window), BF),
            pltpu.VMEM((2, pairs, 8, 2 * LANES), F32),
            pltpu.VMEM((window, LANES), F32),
            pltpu.VMEM((2, 2 * SLOTS, window), BF),
            pltpu.VMEM((SLOTS, ff), F32),
            pltpu.VMEM((2, SLOTS, width), BF),
            pltpu.VMEM((2, SLOTS, width), BF),
            pltpu.VMEM((2, 2, 2, width, width), BF),
            pltpu.VMEM((2, width, width), BF),
            pltpu.VMEM((2, 2, chunks, width, 256), BF),
            pltpu.VMEM((chunks, 2, width, 256), BF),
            pltpu.VMEM((2, chunks, width, 256), BF),
            pltpu.VMEM((8, width), F32),
            pltpu.VMEM((3, 8, width), F32),
            pltpu.VMEM((team, 8, width), F32),
            pltpu.VMEM((teams, 8, width), F32),
            pltpu.VMEM((2, teams, team, 2 * IMAGES, width), BF),
            pltpu.VMEM((2 * IMAGES, width), BF),
            pltpu.SemaphoreType.DMA((copies,)),
            pltpu.SemaphoreType.DMA((copies,)),
            pltpu.SemaphoreType.DMA((11 + 2 * chunks,)),
            *boxes,
        ],
        compiler_params=pltpu.CompilerParams(
            vmem_limit_bytes=62 * 1024 * 1024, collective_id=0, has_side_effects=True
        ),
    )(x_own, c_own, ids, gains, qkv, out, mi, mo, router, ei, eo)


def finish_kernel(
    act, pg, qkv, attn, mi, mot, expert_in, expert_out, small,
    act_out, pg_out, gains_out, qkv_out, attn_out, mi_out, mo_out, router_out, expert_in_out, expert_out_out,
):
    section, tensor = lax.axis_index("section"), lax.axis_index("tensor")
    act_out[...] = act[...]
    pg_out[...] = pg[...]
    gains_out[...] = jnp.where(section == 0, small[0:2], small[2:4])
    router_out[...] = jnp.where(tensor == 0, small[4:5], small[5:6])
    pairs = ((qkv, qkv_out), (attn, attn_out), (mi, mi_out), (expert_in, expert_in_out), (expert_out, expert_out_out))
    for source, dest in pairs:
        dest[...] = source[...].astype(F32)
    mo_out[...] = mot[...].astype(F32).T


def finish(act, pg, qkv, attn, mi, mot, expert_in, expert_out, small):
    steps = 2

    def by_rows(a):
        return pl.BlockSpec((a.shape[0] // steps, a.shape[1]), lambda i: (i, 0))

    def whole(a):
        return pl.BlockSpec(a.shape, lambda i: (0, 0))

    def like(a):
        return jax.ShapeDtypeStruct(a.shape, F32)

    gains = jax.ShapeDtypeStruct((2, act.shape[1]), F32)
    router = jax.ShapeDtypeStruct((1, act.shape[1]), F32)
    mo = jax.ShapeDtypeStruct(mot.shape[::-1], F32)
    mot_spec = pl.BlockSpec((mot.shape[0], mot.shape[1] // steps), lambda i: (0, i))
    return pl.pallas_call(
        finish_kernel,
        grid=(steps,),
        out_shape=(
            act, pg, gains, like(qkv), like(attn), like(mi), mo, router, like(expert_in), like(expert_out)
        ),
        in_specs=[
            whole(act), whole(pg), by_rows(qkv), by_rows(attn), by_rows(mi), mot_spec, by_rows(expert_in),
            by_rows(expert_out), whole(small),
        ],
        out_specs=[
            whole(act), whole(pg), whole(gains), by_rows(qkv), by_rows(attn), by_rows(mi), by_rows(mo), whole(router),
            by_rows(expert_in), by_rows(expert_out),
        ],
        compiler_params=pltpu.CompilerParams(vmem_limit_bytes=60 * 1024 * 1024),
    )(act, pg, qkv, attn, mi, mot, expert_in, expert_out, small)


def per_device(
    patches, image_ids, cotangent, norm_gains, qkv_weight, out_weight, mlp_in, mlp_out, router, expert_in, expert_out
):
    width = patches.shape[2]
    part = qkv_weight.shape[3]
    qkv = jnp.transpose(qkv_weight[0], (1, 2, 0)).reshape(-1, width)
    results = compute(
        patches[0], cotangent[0], image_ids, norm_gains[0], qkv, out_weight[0], mlp_in, mlp_out, router.T,
        expert_in[0], expert_out[0],
    )
    act, pg, gains, qkv_grad, out_grad, mi_grad, mo_grad, router_grad, ei_grad, eo_grad = finish(*results)
    qkv_grad = jnp.transpose(qkv_grad.reshape(3, part, width), (2, 0, 1))
    return (
        act[None], pg[None], gains[None], qkv_grad[None], out_grad[None], mi_grad, mo_grad, router_grad.T,
        ei_grad[None], eo_grad[None],
    )


def solution(mesh):
    return jax.shard_map(
        per_device,
        mesh=mesh,
        in_specs=(
            P(("dp", "section"), "tensor", None),
            P("dp", None),
            P(("dp", "section"), "tensor", None),
            P("section", None, None),
            P("section", None, None, "tensor"),
            P("section", "tensor", None),
            P(None, "tensor"),
            P("tensor", None),
            P(None, "tensor"),
            P("tensor", None, None),
            P("tensor", None, None),
        ),
        out_specs=(
            P(("dp", "section"), "tensor", None),
            P(("dp", "section"), "tensor", None),
            P("section", None, None),
            P("section", None, None, "tensor"),
            P("section", "tensor", None),
            P(None, "tensor"),
            P("tensor", None),
            P(None, "tensor"),
            P("tensor", None, None),
            P("tensor", None, None),
        ),
        check_vma=False,
    )
```

```python
import functools

import jax
import jax.numpy as jnp
from jax import lax
from jax.experimental import pallas as pl
from jax.experimental.pallas import tpu as pltpu
from jax.sharding import PartitionSpec as P

HD = 64
IMAGES = 8
MOST = 256
LANES = 128
SLOTS = 16
EPSILON = 1e-06
BF = jnp.bfloat16
F32 = jnp.float32


def dot(a, b):
    return jnp.dot(a, b, preferred_element_type=F32)


def dot_t(a, b):
    return lax.dot_general(a, b, (((1,), (1,)), ((), ())), preferred_element_type=F32)


def t_dot(a, b):
    return lax.dot_general(a, b, (((0,), (0,)), ((), ())), preferred_element_type=F32)


def normalise(x):
    centred = x - jnp.mean(x, axis=-1, keepdims=True)
    scale = lax.rsqrt(jnp.mean(centred * centred, axis=-1, keepdims=True) + EPSILON)
    return centred * scale, scale


def norm_back(x, gain, gz):
    unit, scale = normalise(x)
    scaled = gz * gain
    mean_plain = jnp.mean(scaled, axis=-1, keepdims=True)
    mean_unit = jnp.mean(scaled * unit, axis=-1, keepdims=True)
    return scale * (scaled - mean_plain - unit * mean_unit), jnp.sum(gz * unit, axis=0, keepdims=True)


def gelu_parts(u):
    cdf = 0.5 * (1.0 + lax.erf(u * 0.7071067811865476))
    return u * cdf, cdf + u * (0.3989422804014327 * jnp.exp(-0.5 * u * u))


def pair_up(tile):
    row = lax.broadcasted_iota(jnp.int32, tile.shape, 0)
    zero = jnp.zeros_like(tile)
    return jnp.concatenate([jnp.where(row < HD, tile, zero), jnp.where(row >= HD, tile, zero)], axis=1)


def pair_down(both):
    n = both.shape[1] // 2
    row = lax.broadcasted_iota(jnp.int32, (both.shape[0], n), 0)
    return jnp.where(row < HD, both[:, :n], both[:, n:])


def bands(window):
    reach = MOST // LANES
    found, at = [], 0
    for i in range(window // LANES):
        first = max(0, i - reach) * LANES
        count = min(window, (i + reach + 1) * LANES) - first
        found.append((i * LANES, first, count, at))
        at += count
    return found, at


MESH = pl.DeviceIdType.MESH


def compute_kernel(
    x_own, c_own, ids, gains_own, qkv_own, out_own, mi_own, mo_own, router_own, ei_own, eo_own,
    act_out, pg_out, qkv_out, attn_out, mi_out, mot_out, expert_in_out, expert_out_out, small_out,
    xw, cw, gains, wy, wc, w_own, wqkv, wo, mi, mo, ei, eo, expert_in_sum, expert_out_sum, routert, act, edge_in, slots, geos, slot_in, pack,
    z, x1, sent, x3, qt, kt, vt, kr, vr, ot, pt, tok, hidden, slope, gx, low, got, gt, gtok, gk_sum, gv_sum,
    gz_all, veil, shares, own, mixing, eslope, eout, gslot, grad_attn, attn_sum, grad_mlp, mlp_core, mlp_sum,
    small, small_in, small_parts, small_across, packs, small_pack, send_sem, recv_sem, here_sem,
    *boxes, team, teams, mlp_orders, attn_orders,
):
    row_count, width = x_own.shape
    window = xw.shape[0]
    extra = window - row_count
    half = window // 2
    pairs = width // LANES
    total = ids.shape[1]
    dp = lax.axis_index("dp")
    section = lax.axis_index("section")
    tensor = lax.axis_index("tensor")
    core = (dp, 1 - section, tensor)
    beside = (dp, section, 1 - tensor)

    spot = lax.rem(dp, team)
    this_team = dp // team

    def mate(k):
        place, bit = spot, 1
        while bit < team:
            if k & bit:
                place = jnp.where(lax.rem(spot // bit, 2) == 0, place + bit, place - bit)
            bit *= 2
        return (dp - spot + place, section, tensor), place

    def partner(k):
        return (lax.rem(dp + k * team, team * teams), section, tensor)

    blocks, _ = bands(window)
    row_blocks = window // LANES

    def at(start, size, step=LANES):
        return pl.ds(pl.multiple_of(start, step), size)

    def rows(i, n=LANES):
        return pl.ds(pl.multiple_of(i * n, n), n)

    def loop(n, body):
        def step(i, carry):
            body(i)
            return carry

        lax.fori_loop(0, n, step, 0)

    sent_off, sent_by, within = {}, {}, (0, 1)

    def copy(key, source, dest, device):
        return pltpu.make_async_remote_copy(
            src_ref=source,
            dst_ref=dest,
            send_sem=send_sem.at[key],
            recv_sem=recv_sem.at[key],
            device_id=device,
            device_id_type=MESH,
        )

    def send(key, source, dest, device, like=None):
        copy(key, source, dest, device).start()
        sent_off[key] = source if like is None else like
        sent_by.setdefault(key, set()).update(within)

    def settle(last=False):
        for key in list(sent_off):
            like = sent_off[key]
            if len(sent_by[key]) == 2:
                copy(key, like, like, core).wait_send()
            elif last:
                only(*sent_by[key])(lambda key=key, like=like: copy(key, like, like, core).wait_send())
            else:
                continue
            sent_off.pop(key)

    def arrived(key, dest):
        copy(key, dest, dest, core).wait_recv()

    def only(which):
        def run(body):
            def marked():
                nonlocal within
                within = (which,)
                body()
                within = (0, 1)

            pl.when(section == which)(marked)

        return run

    barrier = pltpu.get_barrier_semaphore()
    neighbours = [core, beside] + [mate(k)[0] for k in range(1, team)] + [partner(k) for k in range(1, teams)]
    for device in neighbours:
        pl.semaphore_signal(barrier, inc=1, device_id=device, device_id_type=MESH)

    def local(key, source, dest):
        found = pltpu.make_async_copy(source, dest, here_sem.at[key])
        found.start()
        return found

    qkv_rows = qkv_own.shape[0]
    own_rows = at(tensor * extra, row_count)
    near_copies = [
        local(0, x_own, xw.at[own_rows]),
        local(1, qkv_own, w_own.at[:qkv_rows]),
        local(2, out_own, w_own.at[qkv_rows:]),
    ]
    later_copies = [
        local(3, mi_own, mi.at[tensor]),
        local(4, mo_own, mo.at[tensor]),
        local(5, c_own, cw.at[own_rows]),
        local(6, ei_own, ei),
        local(7, eo_own, eo),
    ]
    gains[section, :2] = gains_own[...]
    first_row = lax.broadcasted_iota(jnp.int32, (SLOTS, width), 0) == 0
    router_rows = jnp.broadcast_to(router_own[...].astype(F32), (SLOTS, width))
    routert[tensor] = jnp.where(first_row, router_rows, 0.0).astype(BF)
    pl.semaphore_wait(barrier, len(neighbours))

    qkv_here, out_here = wy.at[:qkv_rows], wy.at[qkv_rows:]
    qkv_near, out_near = wc.at[0, :qkv_rows], wc.at[0, qkv_rows:]
    qkv_far, out_far = wc.at[1, :qkv_rows], wc.at[1, qkv_rows:]

    edge = x_own.at[at((1 - tensor) * (row_count - extra), extra)]
    send(0, edge, xw.at[at(tensor * row_count, extra)], beside)

    @only(0)
    def _():
        send(3, qkv_own, qkv_here, beside)
        send(15, out_own, out_here, beside)
        send(5, mi_own, mi.at[tensor], beside)

    send(1, gains.at[section], gains.at[section], core)
    send(2, qkv_own, qkv_near, core)
    send(16, out_own, out_near, core)

    ids_row = ids[pl.ds(section, 1), :].astype(F32)
    image = lax.broadcasted_iota(jnp.int32, (SLOTS, total), 0).astype(F32)
    spread = jnp.broadcast_to(ids_row, (SLOTS, total))
    middle = jnp.sum((spread < image).astype(F32) + (spread <= image).astype(F32), axis=1, keepdims=True)
    first_half = (middle < total).astype(F32)
    mine = jnp.where(tensor == 0, first_half, 1.0 - first_half)
    window_ids = ids[pl.ds(section, 1), at(tensor * (total - window), window)].astype(F32)
    member = (jnp.broadcast_to(window_ids, (SLOTS, window)) == image[:, :window]).astype(F32)
    member_own = member * mine
    own_row = jnp.sum(member_own, axis=0, keepdims=True)
    own[...] = jnp.broadcast_to(own_row, (LANES, window)).T
    blank = jnp.zeros((LANES - SLOTS, window), F32)
    image_of = jnp.concatenate([member, blank], axis=0).T.astype(BF)
    for b in range(2):
        for j in range(pairs):
            kr[b, j, :, LANES:] = image_of
    veil[...] = jnp.concatenate([(1.0 - member) * -1e30, blank], axis=0).astype(BF)

    def place(source, b, t, kinds=(0, 1, 2, 3)):
        for c in kinds:
            first = c * 3 * HD
            if c < 3:
                own_pair, mixed_pair, dest = t * width + c * LANES, 2 * width + c * LANES + t * HD, wqkv
            else:
                own_pair, mixed_pair, dest = t * LANES, 2 * LANES + t * HD, wo
            dest[b, at(own_pair, 2 * HD)] = source[first : first + 2 * HD]
            dest[b, at(mixed_pair, HD, HD)] = source[first + 2 * HD : first + 3 * HD]

    for found in near_copies:
        found.wait()
    place(w_own, section, tensor)
    arrived(1, gains.at[1 - section])
    arrived(2, qkv_near)
    arrived(16, out_near)
    place(wc.at[0], 1 - section, tensor)
    arrived(0, xw.at[at((1 - tensor) * row_count, extra)])


    def first_far():
        @only(0)
        def _():
            arrived(3, qkv_here)
            send(4, qkv_here, qkv_far, core)
            place(wy, 0, 1 - tensor, (0, 1, 2))

        @only(1)
        def _():
            arrived(4, qkv_far)
            place(wc.at[1], 0, 1 - tensor, (0, 1, 2))

    def send_dense():
        @only(1)
        def _():
            send(5, mo_own, mo.at[tensor], beside)

    def second_far():
        @only(0)
        def _():
            arrived(4, qkv_far)
            place(wc.at[1], 1, 1 - tensor, (0, 1, 2))

        @only(1)
        def _():
            arrived(3, qkv_here)
            send(4, qkv_here, qkv_far, core)
            place(wy, 1, 1 - tensor, (0, 1, 2))

    def first_out():
        @only(0)
        def _():
            arrived(15, out_here)
            send(17, out_here, out_far, core)
            place(wy, 0, 1 - tensor, (3,))

        @only(1)
        def _():
            arrived(17, out_far)
            place(wc.at[1], 0, 1 - tensor, (3,))

    def second_out():
        @only(0)
        def _():
            arrived(17, out_far)
            place(wc.at[1], 1, 1 - tensor, (3,))

        @only(1)
        def _():
            arrived(15, out_here)
            send(17, out_here, out_far, core)
            place(wy, 1, 1 - tensor, (3,))

    def add_across(first, piece, heard):
        if teams == 1:
            return
        for k in range(1, teams):
            copy(first + k, piece, heard.at[k], partner(k)).start()
        whole = piece[...].astype(F32)
        for k in range(1, teams):
            arrived(first + k, heard.at[k])
            copy(first + k, piece, heard.at[k], partner(k)).wait_send()
            whole = whole + heard[k].astype(F32)
        piece[...] = whole.astype(BF)

    class Cube:
        def __init__(self, key, pick, core_in, total, order, boxes):
            self.key, self.pick, self.core_in, self.total, self.order = key, pick, core_in, total, order
            self.boxes, self.across = boxes[:-1], boxes[-1]
            start, size, self.plan = 0, total.shape[0], []
            for dim in order:
                if dim == "tensor":
                    self.plan.append((dim, start, size, start))
                else:
                    size //= 2
                    bit = lax.rem(spot // dim, 2)
                    self.plan.append((dim, start + bit * size, size, start + (1 - bit) * size))
                    start = start + bit * size
            self.back = [(i, *step) for i, step in enumerate(self.plan) if step[0] != "tensor"][::-1]
            self.like = {size: total.at[:size] for _, _, _, size, _ in self.back}
            self.along = order.index("tensor")

        def to_core(self, source):
            send(self.key, source, self.core_in, core, self.core_in)

        def add(self, parts, start, size, box):
            for n, part in enumerate(parts):
                kept = self.pick(part, at(start, size, 16))
                kept[...] = (kept[...].astype(F32) + box[n].astype(F32)).astype(BF)

        def stage(self, k):
            steps, rounds = len(self.plan), len(self.back)
            both = (0, 1)
            if k == 0:
                arrived(self.key, self.core_in)
                self.add(both, 0, self.total.shape[0], self.core_in)
            elif k <= steps:
                _, start, size, _ = self.plan[k - 1]
                arrived(self.key + k, self.boxes[k - 1])
                self.add((tensor,) if self.along < k else both, start, size, self.boxes[k - 1])
            else:
                _, _, _, size, start = self.back[k - steps - 1]
                arrived(self.key + k, self.total.at[at(start, size, 16)])
            if k < steps:
                dim, _, size, start = self.plan[k]
                if dim == "tensor":
                    device = beside
                    source = self.pick(pl.ds(1 - tensor, 1), at(start, size, 16))
                else:
                    device = mate(dim)[0]
                    parts = pl.ds(tensor, 1) if self.along < k else slice(None)
                    source = self.pick(parts, at(start, size, 16))
                send(self.key + k + 1, source, self.boxes[k], device, self.boxes[k])
            elif k == steps:
                _, start, size, _ = self.plan[-1]
                piece = self.total.at[at(start, size, 16)]
                piece[...] = self.pick(tensor, at(start, size, 16))[...]
                add_across(self.key + Cube.stages, piece, self.across)
            if steps <= k < steps + rounds:
                _, dim, start, size, _ = self.back[k - steps]
                region = self.total.at[at(start, size, 16)]
                send(self.key + k + 1, region, region, mate(dim)[0], self.like[size])

        stages = len(mlp_orders[0]) * 2
        keys = stages + teams

    class Straight:
        def __init__(self, key, pick, core_in, total, boxes):
            self.key, self.pick, self.core_in, self.total = key, pick, core_in, total
            self.beside_in, self.parts, self.across = boxes
            self.size = total.shape[0] // team
            self.like = total.at[: self.size]

        def part(self, place):
            return at(place * self.size, self.size, 16)

        def to_core(self, source):
            send(self.key, source, self.core_in, core, self.core_in)

        def stage(self, k):
            every = pl.ds(0, self.total.shape[0])
            near = self.pick(tensor, every)
            if k == 0:
                arrived(self.key, self.core_in)
                far = self.pick(1 - tensor, every)
                far[...] = (far[...].astype(F32) + self.core_in[1 - tensor].astype(F32)).astype(BF)
                send(self.key + 1, far, self.beside_in, beside, self.beside_in)
            if k == 1:
                arrived(self.key + 1, self.beside_in)
                both = near[...].astype(F32) + self.core_in[tensor].astype(F32)
                near[...] = (both + self.beside_in[...].astype(F32)).astype(BF)
                for n in range(1, team):
                    device, place = mate(n)
                    source = self.pick(tensor, self.part(place))
                    send(self.key + 1 + n, source, self.parts.at[n], device, self.like)
            if k == 2:
                whole = self.pick(tensor, self.part(spot))[...].astype(F32)
                for n in range(1, team):
                    arrived(self.key + 1 + n, self.parts.at[n])
                    whole = whole + self.parts[n].astype(F32)
                piece = self.total.at[self.part(spot)]
                piece[...] = whole.astype(BF)
                add_across(self.key + 1 + 2 * team, piece, self.across)
                for n in range(1, team):
                    send(self.key + 1 + team + n, piece, piece, mate(n)[0], self.like)
            if k == 3:
                for n in range(1, team):
                    arrived(self.key + 1 + team + n, self.total.at[self.part(mate(n)[1])])

        keys = 1 + 2 * team + teams

    chunks = len(mlp_orders)
    key, taken = 18, 0

    def boxes_of(count):
        nonlocal taken
        taken += count
        return boxes[taken - count : taken]

    def mlp_pick(q):
        return lambda parts, where: grad_mlp.at[section, parts, q, where]

    def attn_pick(n):
        return lambda parts, where: grad_attn.at[section, parts, n, where]

    dense, attn = [], []
    for q in range(chunks):
        total_of = mlp_sum.at[section, q]
        found = boxes_of(len(mlp_orders[q]) + 1)
        dense.append(Cube(key, mlp_pick(q), mlp_core.at[q], total_of, mlp_orders[q], found))
        key += Cube.keys
    attn = {}
    for n in range(2):
        heard, found = wc.at[:, n * width : (n + 1) * width], boxes_of(len(attn_orders[n]) + 1)
        attn[1, n] = Cube(key, attn_pick(n), heard, attn_sum.at[n], attn_orders[n], found)
        key += Cube.keys
    for n in range(2):
        heard = wc.at[:, n * width : (n + 1) * width]
        attn[0, n] = Straight(key, attn_pick(n), heard, attn_sum.at[n], boxes_of(3))
        key += Straight.keys
    mlp_key, pack_key, small_key = key, key + chunks, key + chunks + team + teams
    mlp_like = mlp_sum.at[0, 0]

    def give_attn(b, n):
        @only(1 - b)
        def _():
            attn[b, n].to_core(grad_attn.at[b, :, n])

    def attn_stage(b, n, k):
        @only(b)
        def _():
            attn[b, n].stage(k)

    def give_dense(q):
        dense[q].to_core(grad_mlp.at[1 - section, :, q])

    def attention(b, x_of, out_ref, ahead_of_far, ahead_of_out):
        def norm(i):
            unit, _ = normalise(x_of(rows(i)))
            z[2 * b, rows(i)] = (unit * gains[b, 0:1, :]).astype(BF)

        loop(row_blocks, norm)

        def pair(n):
            pl.when(n == 1)(ahead_of_far)
            if b == 0:
                pl.when(n == 2)(send_dense)
            j = jnp.where(n == 0, tensor, jnp.where(n == 1, 1 - tensor, n))
            zz, weights = z[2 * b], wqkv.at[b, at(j * width, width)]
            flat = dot_t(zz, weights[...])
            qt[b, j] = (flat[:, :LANES] * HD**-0.5).astype(BF).T
            keys, values = flat[:, LANES : 2 * LANES].astype(BF), flat[:, 2 * LANES :].astype(BF)
            kr[b, j, :, :LANES] = keys
            vr[b, j] = values
            kt[b, j] = keys.T
            vt[...] = values.T
            for q0, k0, count, kept in blocks:
                queries = pair_up(qt[b, j, :, q0 : q0 + LANES])
                hidden_part = veil[:, q0 : q0 + LANES]
                queries = jnp.concatenate([queries, jnp.concatenate([hidden_part, hidden_part], axis=1)], axis=0)
                scores = dot(kr[b, j, k0 : k0 + count, :], queries)
                powers = jnp.exp(scores - jnp.max(scores, axis=0, keepdims=True))
                inverse = 1.0 / jnp.sum(powers, axis=0, keepdims=True)
                low_powers = powers.astype(BF)
                pt[b, j, kept : kept + count, :] = low_powers
                shares[b, j, q0 // LANES : q0 // LANES + 1, :] = inverse
                mixed = dot(vt[:, k0 : k0 + count], low_powers) * inverse
                ot[b, j, :, q0 : q0 + LANES] = pair_down(mixed).astype(BF)

        loop(pairs, pair)
        for j in range(pairs):
            tok[:, j * LANES : (j + 1) * LANES] = ot[b, j].T

        ahead_of_out()

        out_ref[...] = x_of(slice(None)) + dot(tok[...], wo[b])

    def attention_back(b, x_of, beside_pairs, after_pairs):
        ga = low[...]
        got[...] = dot_t(wo[b], ga).astype(BF).reshape(pairs, LANES, window)
        pieces = dot(ot[b].reshape(width, window), ga).astype(BF)
        for t in range(2):
            grad_attn[b, t, 1, 3 * HD : 5 * HD, :] = pieces[t * LANES : (t + 1) * LANES]
            grad_attn[b, t, 1, 5 * HD : 6 * HD, :] = pieces[2 * LANES + t * HD : 2 * LANES + (t + 1) * HD]
        def pair(j):
            gk_sum[...] = jnp.zeros_like(gk_sum)
            gv_sum[...] = jnp.zeros_like(gv_sum)
            for q0, k0, count, kept in blocks:
                for (at_pair, at_query), body in beside_pairs.items():
                    if at_query == q0 // LANES:
                        pl.when(j == at_pair)(body)
                inverse = shares[b, j, q0 // LANES : q0 // LANES + 1, :]
                go_pair = (pair_up(got[j, :, q0 : q0 + LANES]).astype(F32) * inverse).astype(BF)
                q_pair = pair_up(qt[b, j, :, q0 : q0 + LANES])
                low_powers = pt[b, j, kept : kept + count, :]
                powers = low_powers.astype(F32)
                weighted = dot(vr[b, j, k0 : k0 + count, :], go_pair) * powers
                inner = jnp.sum(weighted, axis=0, keepdims=True) * inverse
                gs = (weighted - powers * inner).astype(BF)
                gq = pair_down(dot(kt[b, j, :, k0 : k0 + count], gs)) * HD**-0.5
                gt[:LANES, q0 : q0 + LANES] = gq.astype(BF)
                gk_sum[k0 : k0 + count] += dot_t(gs, q_pair)
                gv_sum[k0 : k0 + count] += dot_t(low_powers, go_pair)
            gtok[3 * j] = gt[:LANES].T
            for c, total_of in ((1, gk_sum), (2, gv_sum)):
                low_sum = total_of[...].astype(BF)
                gtok[3 * j + c] = low_sum
                gt[c * LANES : (c + 1) * LANES] = low_sum.T
            pieces = dot(gt[...], z[2 * b]).astype(BF)

            @pl.when(j < 2)
            def _():
                grad_attn[b, j, 0] = pieces

            @pl.when(j == 2)
            def _():
                for c in range(3):
                    for t in range(2):
                        first = c * LANES + t * HD
                        grad_attn[b, t, 1, c * HD : (c + 1) * HD, :] = pieces[first : first + HD]

        loop(pairs, pair)
        after_pairs()
        gain = gains[b, 0:1, :]

        def back(i, gain_grad):
            wide = jnp.concatenate([gtok[c, rows(i, half)] for c in range(3 * pairs)], axis=1)
            step, part = norm_back(x_of(rows(i, half)), gain, dot(wide, wqkv[b]))
            gx[rows(i, half)] += step
            return gain_grad + part

        small[2 * b : 2 * b + 1, :] = lax.fori_loop(0, 2, back, jnp.zeros((1, width), F32))

    attention(0, lambda r: xw[r].astype(F32), x1, first_far, first_out)

    def norm_middle(source, which):
        def body(i):
            unit, _ = normalise(source[rows(i)])
            z[which, rows(i)] = (unit * gains[which // 2, 1:2, :]).astype(BF)

        loop(row_blocks, body)

    norm_middle(x1, 1)

    for found in later_copies:
        found.wait()

    def far_hidden():
        @only(0)
        def _():
            arrived(5, mi.at[1 - tensor])
            send(6, mi.at[1 - tensor], mi.at[1 - tensor], core, mi_own)

        @only(1)
        def _():
            send(3, qkv_own, qkv_here, beside)
            send(15, out_own, out_here, beside)
            arrived(5, mo.at[1 - tensor])
            send(6, mo.at[1 - tensor], mo.at[1 - tensor], core, mo_own)
            arrived(6, mi.at[1 - tensor])

    chunk = 256

    def hidden_chunk(n):
        pl.when(n == chunks)(far_hidden)
        q = lax.rem(n, chunks)
        part, first = jnp.where(n < chunks, tensor, 1 - tensor), pl.multiple_of(q * chunk, chunk)
        value, grad = gelu_parts(dot(z[1], mi[part, :, pl.ds(first, chunk)]))
        hidden[part * chunks + q] = value.astype(BF)
        slope[part * chunks + q] = grad.astype(BF)

    loop(2 * chunks, hidden_chunk)

    @only(0)
    def _():
        arrived(6, mo.at[1 - tensor])

    h = jnp.concatenate([hidden[c] for c in range(2 * chunks)], axis=1)
    sent[...] = (x1[...] + dot(h, mo[...].reshape(-1, width))).astype(BF)

    c_edge = c_own.at[at((1 - tensor) * (row_count - extra), extra)]
    send(7, c_edge, cw.at[at(tensor * row_count, extra)], beside)
    send(8, routert.at[tensor], routert.at[tensor], beside)

    attention(1, lambda r: sent[r].astype(F32), x3, second_far, second_out)
    norm_middle(x3, 3)
    z3 = z[3]
    arrived(8, routert.at[1 - tensor])
    powers = [jnp.exp(dot_t(routert[e], z3)[:1]) for e in range(2)]
    dispatch, combine = [], []
    for e in range(2):
        totals = jnp.sum(member * powers[e], axis=1, keepdims=True)
        dispatch.append(powers[e] / jnp.sum(member * totals, axis=0, keepdims=True))
        combine.append(powers[e] / (powers[0] + powers[1]))
        d_low = (member_own * dispatch[e].astype(BF).astype(F32)).astype(BF)
        c_low = (member * combine[e].astype(BF).astype(F32)).astype(BF)
        mixing[0, e * SLOTS : (e + 1) * SLOTS] = d_low
        mixing[1, e * SLOTS : (e + 1) * SLOTS] = c_low
        slots[e] = dot(d_low, z3).astype(BF)
    send(9, slots.at[1 - tensor], slot_in.at[0], beside)
    arrived(7, cw.at[at((1 - tensor) * row_count, extra)])

    def mask(i):
        wide = jnp.concatenate([own[rows(i)]] * pairs, axis=1)
        low[rows(i)] = jnp.where(wide > 0.0, cw[rows(i)].astype(F32), 0.0).astype(BF)

    loop(row_blocks, mask)
    gy = low[...]
    for e in range(2):
        geos[e] = dot(mixing[1, e * SLOTS : (e + 1) * SLOTS], gy).astype(BF)
    send(10, geos.at[1 - tensor], slot_in.at[1], beside)

    arrived(9, slot_in.at[0])
    pack[0] = slots[tensor] + slot_in[0]
    value, grad = gelu_parts(dot(pack[0], ei[...]))
    eslope[...] = grad
    eout[tensor] = dot(value.astype(BF), eo[...]).astype(BF)
    send(11, eout.at[tensor], eout.at[tensor], beside)
    arrived(10, slot_in.at[1])
    pack[1] = geos[tensor] + slot_in[1]
    g_hidden = dot_t(pack[1], eo[...])
    gslot[tensor] = dot_t((g_hidden * eslope[...]).astype(BF), ei[...]).astype(BF)
    send(12, gslot.at[tensor], gslot.at[tensor], beside)
    per_own = jnp.sum(dot_t(eout[tensor], gy) * member, axis=0, keepdims=True)
    to_own = jnp.sum(dot_t(gslot[tensor], z3) * member_own, axis=0, keepdims=True)
    arrived(11, eout.at[1 - tensor])
    outputs = eout[...].reshape(2 * SLOTS, width)

    def finish(i):
        mixed = t_dot(mixing[1, :, rows(i)], outputs)
        act[rows(i)] = (x3[rows(i)] + mixed).astype(BF)

    loop(row_blocks, finish)
    send(13, act.at[at((1 - tensor) * row_count, extra)], edge_in.at[0], beside)

    all_packs, team_like = packs.at[0], packs.at[0, 0]

    def share_slots():
        halves = [pack[n].astype(F32)[:IMAGES] for n in range(2)]
        small_pack[...] = jnp.concatenate(halves, axis=0).astype(BF)
        for k in range(1, team):
            send(pack_key + k, small_pack, packs.at[0, this_team, spot], mate(k)[0], small_pack)

    def gather_slots():
        for k in range(1, team):
            arrived(pack_key + k, packs.at[0, this_team, mate(k)[1]])
        packs[0, this_team, spot] = small_pack[...]
        for k in range(1, teams):
            team_packs = packs.at[0, this_team]
            send(pack_key + team + k, team_packs, team_packs, partner(k), team_like)
        for k in range(1, teams):
            arrived(pack_key + team + k, packs.at[0, lax.rem(this_team + teams - k, teams)])
        send(pack_key, packs.at[0], packs.at[1], core, all_packs)

    per_other = jnp.sum(dot_t(eout[1 - tensor], gy) * member, axis=0, keepdims=True)
    first = tensor == 0
    per_token = [jnp.where(first, per_own, per_other), jnp.where(first, per_other, per_own)]
    inner = combine[0] * per_token[0] + combine[1] * per_token[1]
    arrived(12, gslot.at[1 - tensor])
    to_other = jnp.sum(dot_t(gslot[1 - tensor], z3) * member_own, axis=0, keepdims=True)
    to_dispatch = [jnp.where(first, to_own, to_other), jnp.where(first, to_other, to_own)]
    logit_grads = []
    for e in range(2):
        weighted = dispatch[e] * to_dispatch[e]
        sums = jnp.sum(member * weighted, axis=1, keepdims=True)
        from_dispatch = weighted - dispatch[e] * jnp.sum(member * sums, axis=0, keepdims=True)
        logit_grads.append(combine[e] * (per_token[e] - inner) + from_dispatch)
    which_row = lax.broadcasted_iota(jnp.int32, (SLOTS, width), 0)
    router_rows = jnp.where(
        which_row == 0,
        jnp.broadcast_to(routert[0].astype(F32)[:1], (SLOTS, width)),
        jnp.where(which_row == 1, jnp.broadcast_to(routert[1].astype(F32)[:1], (SLOTS, width)), 0.0),
    ).astype(BF)
    which = lax.broadcasted_iota(jnp.int32, (SLOTS, window), 0)
    logit_grad = jnp.where(which == 0, logit_grads[0], jnp.where(which == 1, logit_grads[1], 0.0)).astype(BF)
    small[4:6, :] = dot(logit_grad, z3)[:2]
    small[6:8, :] = jnp.zeros((2, width), F32)
    mixing[1, :SLOTS] = logit_grad
    slots_and_router = jnp.concatenate([gslot[0], gslot[1], router_rows], axis=0)

    def experts_back(i, gain_grad):
        at = pl.ds(pl.multiple_of(i * LANES, LANES), LANES)
        parts = jnp.concatenate([mixing[0, :, at], mixing[1, :SLOTS, at]], axis=0)
        step, part = norm_back(x3[rows(i)], gains[1, 1:2, :], t_dot(parts, slots_and_router))
        total_of = low[rows(i)].astype(F32) + step
        gx[rows(i)] = total_of
        low[rows(i)] = total_of.astype(BF)
        return gain_grad + part

    small[3:4, :] = lax.fori_loop(0, row_blocks, experts_back, jnp.zeros((1, width), F32))

    def shares_second():
        gather_slots()
        give_attn(1, 0)

    share_slots()
    attention_back(1, lambda r: sent[r].astype(F32), {(2, 0): shares_second}, lambda: give_attn(1, 1))

    low[...] = gx[...].astype(BF)
    gsent = low[...]
    gsent_t = gsent.T
    z2 = z[1]
    z2_t = z2.T

    def hidden_back(n):
        for ahead, body in ((2, dense_first), (4, dense_second)):
            pl.when(n == ahead)(body)
        q, part = n // 2, lax.rem(n, 2)
        i, first = part * chunks + q, pl.multiple_of(q * chunk, chunk)
        grad_mlp[1, part, q] = dot(gsent_t, hidden[i]).astype(BF)
        g_hidden = dot_t(gsent, mo[part, pl.ds(first, chunk), :])
        g_pre = (g_hidden * slope[i].astype(F32)).astype(BF)
        hidden[i] = g_pre
        grad_mlp[0, part, q] = dot(z2_t, g_pre).astype(BF)

    def dense_first():
        give_dense(0)
        attn_stage(1, 0, 0)

    def dense_second():
        give_dense(1)
        attn_stage(1, 1, 0)
        dense[0].stage(0)

    loop(2 * chunks, hidden_back)
    give_dense(2)
    dense[1].stage(0)

    def dense_back(i, gain_grad):
        gz = jnp.zeros((half, width), F32)
        for part in range(2):
            g = jnp.concatenate([hidden[part * chunks + c, rows(i, half)] for c in range(chunks)], axis=1)
            gz = gz + dot_t(g, mi[part])
        step, part = norm_back(x1[rows(i, half)], gains[0, 1:2, :], gz)
        total_of = low[rows(i, half)].astype(F32) + step
        gx[rows(i, half)] = total_of
        low[rows(i, half)] = total_of.astype(BF)
        return gain_grad + part

    small[1:2, :] = lax.fori_loop(0, 2, dense_back, jnp.zeros((1, width), F32))

    dense[2].stage(0)
    attn_stage(1, 0, 1)

    def beside_first():
        dense[0].stage(1)
        attn_stage(1, 1, 1)

    def beside_second():
        dense[1].stage(1)
        attn_stage(1, 0, 2)

    def beside_middle():
        dense[2].stage(1)
        attn_stage(1, 1, 2)

    def beside_third():
        give_attn(0, 0)
        attn_stage(1, 0, 3)
        dense[0].stage(2)

    def beside_last():
        dense[1].stage(2)
        attn_stage(1, 1, 3)
        attn_stage(0, 0, 0)

    def beside_rest():
        give_attn(0, 1)
        attn_stage(1, 0, 4)
        dense[2].stage(2)
        dense[0].stage(3)

    beside_pairs = {
        (0, 3): beside_first,
        (1, 0): beside_second,
        (1, 3): beside_middle,
        (2, 0): beside_third,
        (2, 3): beside_last,
    }
    attention_back(0, lambda r: xw[r].astype(F32), beside_pairs, beside_rest)
    low[...] = gx[...].astype(BF)
    send(14, low.at[at((1 - tensor) * row_count, extra)], edge_in.at[1], beside)
    send(small_key, small, small_in.at[0], core)
    attn_stage(0, 1, 0)
    attn_stage(1, 1, 4)
    dense[1].stage(3)

    arrived(pack_key, packs.at[1])
    split_packs = packs[...].astype(F32).reshape(-1, 2, IMAGES, width)
    every_slot, every_grad = (split_packs[:, n].reshape(-1, width).astype(BF) for n in range(2))
    every_slot_t = every_slot.T
    few = chunk if teams == 1 else LANES
    expert_steps = 2 * chunks * chunk // few

    def expert_grads(i):
        for part, body in ((1, beside_experts_first), (2, beside_experts_second)):
            pl.when(i == part * expert_steps // 3)(body)
        lanes = pl.ds(pl.multiple_of(i * few, few), few)
        value, grad = gelu_parts(dot(every_slot, ei[:, lanes]))
        g_pre = (dot_t(every_grad, eo[lanes, :]) * grad).astype(BF)
        expert_in_sum[:, lanes] = dot(every_slot_t, g_pre).astype(BF)
        expert_out_sum[lanes, :] = dot(value.astype(BF).T, every_grad).astype(BF)

    def beside_experts_first():
        attn_stage(0, 0, 1)
        attn_stage(1, 0, 5)
        dense[0].stage(4)
        dense[2].stage(3)
        arrived(small_key, small_in.at[0])
        small_in[1] = small[...] + small_in[0]
        send(small_key + 1, small_in.at[1], small_in.at[2], beside, small)

    def beside_experts_second():
        attn_stage(1, 1, 5)
        dense[1].stage(4)

    loop(expert_steps, expert_grads)

    last_copies = [local(0, expert_in_sum, expert_in_out), local(1, expert_out_sum, expert_out_out)]
    attn_stage(0, 1, 1)
    attn_stage(1, 0, 6)
    arrived(small_key + 1, small_in.at[2])
    small_parts[0] = small_in[1] + small_in[2]
    for k in range(1, team):
        send(small_key + 1 + k, small_parts.at[0], small_parts.at[k], mate(k)[0])
    dense[0].stage(5)
    dense[2].stage(4)

    for n, (source, dest) in enumerate(((act, act_out), (low, pg_out))):
        arrived(13 + n, edge_in.at[n])
        near = at(row_count - extra - tensor * (row_count - 2 * extra), extra)
        wide = jnp.concatenate([own[near]] * pairs, axis=1)
        source[near] = jnp.where(wide > 0.0, source[near].astype(F32), edge_in[n].astype(F32)).astype(BF)
        last_copies.append(local(2 + n, source.at[own_rows], dest))

    attn_stage(1, 1, 6)
    attn_stage(0, 0, 2)
    dense[1].stage(5)
    dense[0].stage(6)
    attn_stage(1, 0, 7)
    dense[2].stage(5)
    attn_stage(0, 1, 2)
    for k in range(1, team):
        arrived(small_key + 1 + k, small_parts.at[k])
    small_across[0] = sum([small_parts[k] for k in range(1, team)], start=small_parts[0])
    for k in range(1, teams):
        send(small_key + 1 + team + k, small_across.at[0], small_across.at[k], partner(k))
    for k in range(1, teams):
        arrived(small_key + 1 + team + k, small_across.at[k])
    small_out[...] = sum([small_across[k] for k in range(1, teams)], start=small_across[0])
    def pass_dense(q):
        dense[q].stage(7)
        done = mlp_sum.at[section, q]
        send(mlp_key + q, done, done, core, mlp_like)

    dense[1].stage(6)
    dense[2].stage(6)
    attn_stage(1, 1, 7)
    pass_dense(0)
    pass_dense(1)
    pass_dense(2)
    for q in range(chunks):
        arrived(mlp_key + q, mlp_sum.at[1 - section, q])
        for n, dest in enumerate((mi_out, mot_out)):
            place_out = dest.at[:, q * chunk : (q + 1) * chunk]
            last_copies.append(local(4 + 2 * q + n, mlp_sum.at[n, q], place_out))
    attn_stage(0, 0, 3)
    used = 4 + 2 * chunks
    for c in range(3):
        place_out = qkv_out.at[c * 3 * HD : c * 3 * HD + 2 * HD]
        last_copies.append(local(used + c, attn_sum.at[0, c * LANES : (c + 1) * LANES], place_out))
    settle()
    attn_stage(0, 1, 3)
    for c in range(3):
        place_out = qkv_out.at[c * 3 * HD + 2 * HD : (c + 1) * 3 * HD]
        last_copies.append(local(used + 3 + c, attn_sum.at[1, c * HD : (c + 1) * HD], place_out))
    last_copies.append(local(used + 6, attn_sum.at[1, 3 * HD :], attn_out))
    for found in last_copies:
        found.wait()

    settle(True)


def compute(x_own, c_own, ids, gains, qkv, out, mi, mo, router, ei, eo):
    row_count, width = x_own.shape
    window = row_count + MOST // 2
    extra = window - row_count
    pairs = width // LANES
    ff = ei.shape[1]
    _, kept = bands(window)
    chunk_count = ff // 256
    chunks = chunk_count // 2
    vmem, hbm = pl.BlockSpec(memory_space=pltpu.VMEM), pl.BlockSpec(memory_space=pl.ANY)
    ranks = lax.axis_size("dp")
    team = min(8, ranks & -ranks)
    teams = ranks // team
    bits = [1 << n for n in range(team.bit_length() - 1)]
    spread = [bits[:1] + ["tensor"] + bits[1:], ["tensor"] + bits, bits[1::-1] + ["tensor"] + bits[2:]]
    mlp_orders = [spread[q % 3] for q in range(chunks)]
    attn_orders = [spread[2], spread[1]]
    boxes = []
    for order, lanes in [(order, 256) for order in mlp_orders] + [(order, width) for order in attn_orders]:
        size = width
        for n, dim in enumerate(order):
            size = size if dim == "tensor" else size // 2
            boxes.append(pltpu.VMEM((2 if "tensor" in order[n + 1 :] else 1, size, lanes), BF))
        boxes.append(pltpu.VMEM((teams, size, lanes), BF))
    for _ in range(2):
        boxes.append(pltpu.VMEM((width, width), BF))
        boxes += [pltpu.VMEM((n, width // team, width), BF) for n in (team, teams)]
    copies = 18 + (chunks + 2) * (2 * len(mlp_orders[0]) + teams) + 2 * (1 + 2 * team + teams) + chunks + 2 * (team + teams + 1)
    return pl.pallas_call(
        functools.partial(
            compute_kernel, team=team, teams=teams, mlp_orders=mlp_orders, attn_orders=attn_orders
        ),
        out_shape=(
            jax.ShapeDtypeStruct((row_count, width), BF),
            jax.ShapeDtypeStruct((row_count, width), BF),
            jax.ShapeDtypeStruct(qkv.shape, BF),
            jax.ShapeDtypeStruct(out.shape, BF),
            jax.ShapeDtypeStruct((width, ff // 2), BF),
            jax.ShapeDtypeStruct((width, ff // 2), BF),
            jax.ShapeDtypeStruct((width, ff), BF),
            jax.ShapeDtypeStruct((ff, width), BF),
            jax.ShapeDtypeStruct((8, width), F32),
        ),
        in_specs=[hbm, hbm, vmem, vmem, hbm, hbm, hbm, hbm, vmem, hbm, hbm],
        out_specs=[hbm] * 8 + [vmem],
        scratch_shapes=[
            pltpu.VMEM((window, width), BF),
            pltpu.VMEM((window, width), BF),
            pltpu.VMEM((2, 8, width), F32),
            pltpu.VMEM((2 * width, width), BF),
            pltpu.VMEM((2, 2 * width, width), BF),
            pltpu.VMEM((2 * width, width), BF),
            pltpu.VMEM((2, 3 * width, width), BF),
            pltpu.VMEM((2, width, width), BF),
            pltpu.VMEM((2, *mi.shape), BF),
            pltpu.VMEM((2, *mo.shape), BF),
            pltpu.VMEM(ei.shape, BF),
            pltpu.VMEM(eo.shape, BF),
            pltpu.VMEM(ei.shape, BF),
            pltpu.VMEM(eo.shape, BF),
            pltpu.VMEM((2, SLOTS, width), BF),
            pltpu.VMEM((window, width), BF),
            pltpu.VMEM((2, extra, width), BF),
            pltpu.VMEM((2, SLOTS, width), BF),
            pltpu.VMEM((2, SLOTS, width), BF),
            pltpu.VMEM((2, SLOTS, width), BF),
            pltpu.VMEM((2, SLOTS, width), BF),
            pltpu.VMEM((4, window, width), BF),
            pltpu.VMEM((window, width), F32),
            pltpu.VMEM((window, width), BF),
            pltpu.VMEM((window, width), F32),
            pltpu.VMEM((2, pairs, LANES, window), BF),
            pltpu.VMEM((2, pairs, LANES, window), BF),
            pltpu.VMEM((LANES, window), BF),
            pltpu.VMEM((2, pairs, window, 2 * LANES), BF),
            pltpu.VMEM((2, pairs, window, LANES), BF),
            pltpu.VMEM((2, pairs, LANES, window), BF),
            pltpu.VMEM((2, pairs, kept, 2 * LANES), BF),
            pltpu.VMEM((window, width), BF),
            pltpu.VMEM((chunk_count, window, 256), BF),
            pltpu.VMEM((chunk_count, window, 256), BF),
            pltpu.VMEM((window, width), F32),
            pltpu.VMEM((window, width), BF),
            pltpu.VMEM((pairs, LANES, window), BF),
            pltpu.VMEM((3 * LANES, window), BF),
            pltpu.VMEM((3 * pairs, window, LANES), BF),
            pltpu.VMEM((window, LANES), F32),
            pltpu.VMEM((window, LANES), F32),
            pltpu.VMEM((window, width), F32),
            pltpu.VMEM((LANES, window), BF),
            pltpu.VMEM((2, pairs, 8, 2 * LANES), F32),
            pltpu.VMEM((window, LANES), F32),
            pltpu.VMEM((2, 2 * SLOTS, window), BF),
            pltpu.VMEM((SLOTS, ff), F32),
            pltpu.VMEM((2, SLOTS, width), BF),
            pltpu.VMEM((2, SLOTS, width), BF),
            pltpu.VMEM((2, 2, 2, width, width), BF),
            pltpu.VMEM((2, width, width), BF),
            pltpu.VMEM((2, 2, chunks, width, 256), BF),
            pltpu.VMEM((chunks, 2, width, 256), BF),
            pltpu.VMEM((2, chunks, width, 256), BF),
            pltpu.VMEM((8, width), F32),
            pltpu.VMEM((3, 8, width), F32),
            pltpu.VMEM((team, 8, width), F32),
            pltpu.VMEM((teams, 8, width), F32),
            pltpu.VMEM((2, teams, team, 2 * IMAGES, width), BF),
            pltpu.VMEM((2 * IMAGES, width), BF),
            pltpu.SemaphoreType.DMA((copies,)),
            pltpu.SemaphoreType.DMA((copies,)),
            pltpu.SemaphoreType.DMA((11 + 2 * chunks,)),
            *boxes,
        ],
        compiler_params=pltpu.CompilerParams(
            vmem_limit_bytes=62 * 1024 * 1024, collective_id=0, has_side_effects=True
        ),
    )(x_own, c_own, ids, gains, qkv, out, mi, mo, router, ei, eo)


def finish_kernel(
    act, pg, qkv, attn, mi, mot, expert_in, expert_out, small,
    act_out, pg_out, gains_out, qkv_out, attn_out, mi_out, mo_out, router_out, expert_in_out, expert_out_out,
):
    section, tensor = lax.axis_index("section"), lax.axis_index("tensor")
    act_out[...] = act[...]
    pg_out[...] = pg[...]
    gains_out[...] = jnp.where(section == 0, small[0:2], small[2:4])
    router_out[...] = jnp.where(tensor == 0, small[4:5], small[5:6])
    pairs = ((qkv, qkv_out), (attn, attn_out), (mi, mi_out), (expert_in, expert_in_out), (expert_out, expert_out_out))
    for source, dest in pairs:
        dest[...] = source[...].astype(F32)
    mo_out[...] = mot[...].astype(F32).T


def finish(act, pg, qkv, attn, mi, mot, expert_in, expert_out, small):
    steps = 2

    def by_rows(a):
        return pl.BlockSpec((a.shape[0] // steps, a.shape[1]), lambda i: (i, 0))

    def whole(a):
        return pl.BlockSpec(a.shape, lambda i: (0, 0))

    def like(a):
        return jax.ShapeDtypeStruct(a.shape, F32)

    gains = jax.ShapeDtypeStruct((2, act.shape[1]), F32)
    router = jax.ShapeDtypeStruct((1, act.shape[1]), F32)
    mo = jax.ShapeDtypeStruct(mot.shape[::-1], F32)
    mot_spec = pl.BlockSpec((mot.shape[0], mot.shape[1] // steps), lambda i: (0, i))
    return pl.pallas_call(
        finish_kernel,
        grid=(steps,),
        out_shape=(
            act, pg, gains, like(qkv), like(attn), like(mi), mo, router, like(expert_in), like(expert_out)
        ),
        in_specs=[
            by_rows(act), by_rows(pg), by_rows(qkv), by_rows(attn), by_rows(mi), mot_spec, by_rows(expert_in),
            by_rows(expert_out), whole(small),
        ],
        out_specs=[
            by_rows(act), by_rows(pg), whole(gains), by_rows(qkv), by_rows(attn), by_rows(mi), by_rows(mo), whole(router),
            by_rows(expert_in), by_rows(expert_out),
        ],
        compiler_params=pltpu.CompilerParams(vmem_limit_bytes=60 * 1024 * 1024),
    )(act, pg, qkv, attn, mi, mot, expert_in, expert_out, small)


def per_device(
    patches, image_ids, cotangent, norm_gains, qkv_weight, out_weight, mlp_in, mlp_out, router, expert_in, expert_out
):
    width = patches.shape[2]
    part = qkv_weight.shape[3]
    qkv = jnp.transpose(qkv_weight[0], (1, 2, 0)).reshape(-1, width)
    results = compute(
        patches[0], cotangent[0], image_ids, norm_gains[0], qkv, out_weight[0], mlp_in, mlp_out, router.T,
        expert_in[0], expert_out[0],
    )
    act, pg, gains, qkv_grad, out_grad, mi_grad, mo_grad, router_grad, ei_grad, eo_grad = finish(*results)
    qkv_grad = jnp.transpose(qkv_grad.reshape(3, part, width), (2, 0, 1))
    return (
        act[None], pg[None], gains[None], qkv_grad[None], out_grad[None], mi_grad, mo_grad, router_grad.T,
        ei_grad[None], eo_grad[None],
    )


def solution(mesh):
    return jax.shard_map(
        per_device,
        mesh=mesh,
        in_specs=(
            P(("dp", "section"), "tensor", None),
            P("dp", None),
            P(("dp", "section"), "tensor", None),
            P("section", None, None),
            P("section", None, None, "tensor"),
            P("section", "tensor", None),
            P(None, "tensor"),
            P("tensor", None),
            P(None, "tensor"),
            P("tensor", None, None),
            P("tensor", None, None),
        ),
        out_specs=(
            P(("dp", "section"), "tensor", None),
            P(("dp", "section"), "tensor", None),
            P("section", None, None),
            P("section", None, None, "tensor"),
            P("section", "tensor", None),
            P(None, "tensor"),
            P("tensor", None),
            P(None, "tensor"),
            P("tensor", None, None),
            P("tensor", None, None),
        ),
        check_vma=False,
    )
```
